32 devices in a mesh: ep: 8 (over y, x, core), gd: 4 (over z).
Axes of the slice: x: 2, y: 2, z: 4, core: 2. Of those that a mesh axis runs over, the one named last changes fastest.
Arguments:
- tokens: bfloat16 [256, 4096], P(('ep', 'gd')), may hold values from -6 to 6
- expert_ids: int32 [256, 4], P(('ep', 'gd')), may hold values from 0 to 7, all different within a row; in each aligned block of 8 rows (0 to 7, 8 to 15, ...) at most 6 rows name the same one
- combine: float32 [256, 4], P(('ep', 'gd')), may hold values from 0.02 to 0.3
- w_gate: bfloat16 [8, 4096, 1536], P('ep', None, 'gd'), may hold values from -0.09375 to 0.09375
- w_up: bfloat16 [8, 4096, 1536], P('ep', None, 'gd'), may hold values from -0.09375 to 0.09375
- w_down: bfloat16 [8, 1536, 4096], P('ep', 'gd'), may hold values from -0.15625 to 0.15625
- w_query: bfloat16 [4096, 2048], P(None, 'gd'), may hold values from -0.09375 to 0.09375
- w_key: bfloat16 [4096, 512], P(None, 'gd'), may hold values from -0.09375 to 0.09375
- w_value: bfloat16 [4096, 512], P(None, 'gd'), may hold values from -0.09375 to 0.09375
- cache_keys: bfloat16 [256, 4, 64, 128], P('ep', 'gd'), may hold values from -68 to 68
- cache_values: bfloat16 [256, 4, 64, 128], P('ep', 'gd'), may hold values from -6 to 6
- lengths: int32 [256], P('ep'), may hold values from 1 to 64, as said below
Outputs:
- stream: bfloat16 [256, 4096], P(('ep', 'gd'))
- guard: bfloat16 [256, 2048], P('ep', 'gd')
The draws below stay inside these ranges and needn't reach their ends.
Inputs may be any that keep to these rules, and one draw needn't show every extreme that they name: `expert_ids`: each row names 4 different experts; in the rows of one device no expert is named by more than 6 rows. `lengths`: some row has the full window of 64 positions.
All inputs are finite; a program needn't handle non-finite values.
Results may differ from the reference program's by a relative error of at most 0.03.
Values may be sent and summed in bfloat16 or wider, within the bound.
A program may use at most 128 MiB of HBM per device.

```python
import math
import jax
import jax.numpy as jnp
import numpy as np
from jax import lax

D = 4096
FF = 1536
HD = 128
GROUP = 4
WIN = 64
ROWS_DEV = 8
EXPERTS = 8
TOP = 4
CAP = 6
TOKENS = 256
KVH = 4
HQ = 16
N_GD = 4


def draw_lengths(key, part):
    window_len = jax.random.randint(key, (TOKENS,), 1, WIN + 1).astype(jnp.int32)
    longest = jax.random.randint(jax.random.fold_in(key, 11), (), 0, TOKENS)
    shortest = (longest + 1 + jax.random.randint(jax.random.fold_in(key, 12), (), 0, TOKENS - 1)) % TOKENS
    window_len = window_len.at[shortest].set(1)
    window_len = window_len.at[longest].set(WIN)
    return window_len.astype(jnp.int32)


def draw_cache_keys(key, part):
    shape_all = (TOKENS, KVH, WIN, HD)
    values = jnp.clip(jax.random.normal(key, shape_all, jnp.float32), -6.0, 6.0)
    return values.astype(jnp.bfloat16)


def block_scale(stream_key, dims, split, low, high):
    level = 1.0
    for position, shards_of in split:
        heights = jax.random.uniform(jax.random.fold_in(jax.random.fold_in(stream_key, 6), position), (shards_of,), jnp.float32, low / len(split), high / len(split))
        level = level * jnp.repeat(jnp.exp(heights), dims[position] // shards_of).reshape((-1,) + (1,) * (len(dims) - 1 - position))
    return level


def shared_out(key, own, number, rows, number_of, top, limit, slope):
    order = jax.random.permutation(key, number_of)
    heavy_load, usual = portions_of(number_of, rows * top, limit, slope, True), portions_of(number_of, rows * top, limit, slope, False)
    places = jnp.arange(number_of)

    def named(sizes, rotation):
        used = int((sizes > 0).sum())
        fixed = max(1, used // 4)
        moved = fixed + (places - fixed + rotation * (used - fixed)) % max(1, number_of - fixed)
        return jnp.zeros((number_of,), jnp.int32).at[order[jnp.where(places < fixed, places, moved)]].set(jnp.asarray(sizes, jnp.int32))

    sizes = jnp.where(number % 4 == 0, named(heavy_load, number // 4), named(usual, number - number // 4 - 1))
    mixed = jax.random.permutation(jax.random.fold_in(own, 3), number_of)
    donor, sink = mixed[0:number_of // 2 * 2:2], mixed[1:number_of // 2 * 2:2]
    margin = jnp.minimum(sizes[donor] - 1, limit - sizes[sink]) // 2
    margin = jnp.where((donor == order[0]) | (sink == order[0]) | (sizes[sink] == 0), 0, jnp.maximum(margin, 0))
    moved = jax.random.randint(jax.random.fold_in(own, 4), (number_of // 2,), 0, 1 << 20) % (margin + 1)
    sizes = sizes.at[donor].add(-moved).at[sink].add(moved)
    items = jnp.searchsorted(jnp.cumsum(sizes), jnp.arange(rows * top), side="right").astype(jnp.int32)
    table = items.reshape(top, rows).T
    table = table[jax.random.permutation(jax.random.fold_in(own, 1), rows)]
    rotation = jax.random.randint(jax.random.fold_in(own, 2), (rows, 1), 0, top)
    return jnp.take_along_axis(table, (jnp.arange(top)[None, :] + rotation) % top, axis=1)


def portions_of(number_of, total, most, slope, full):
    portions = [(1 << 20) // math.isqrt(rank ** slope) + 1 for rank in range(1, number_of + 1)]
    largest = most if full else min(most, max(-(-total // number_of), total * portions[0] // sum(portions)))
    least = 1 if total - largest >= number_of - 1 else 0
    given, surplus = [largest] + [least] * (number_of - 1), total - largest - least * (number_of - 1)
    while surplus > 0:
        movable = [i for i in range(1, number_of) if given[i] < largest] or [i for i in range(1, number_of) if given[i] < most]
        whole, left = sum([portions[i] for i in movable]), surplus
        for i in movable:
            extra = min(most - given[i], max(1, left * portions[i] // whole), surplus)
            given[i] = given[i] + extra
            surplus = surplus - extra
    return np.array(given)


def gaussian(own_key, extent, scale, reach, pieces=(), kind=jnp.bfloat16):
    entries = scale * jax.random.normal(own_key, extent, jnp.float32)
    if pieces:
        entries = entries * block_scale(own_key, extent, pieces, -0.22, 0.18)
    return jnp.clip(entries, -reach, reach).astype(kind)


def setup_inputs(seed: int = 0) -> dict:
    streams_of = jax.random.split(jax.random.key(seed), 13)
    tokens = gaussian(streams_of[0], (TOKENS, D), 1.0, 6.0, ((0, 32),))
    expert_ids_keys = jax.random.split(jax.random.fold_in(streams_of[1], 1), TOKENS // ROWS_DEV)
    expert_ids_turns = jax.random.permutation(jax.random.fold_in(streams_of[1], 3), TOKENS // ROWS_DEV)
    expert_ids = jax.vmap(lambda own, number: shared_out(jax.random.fold_in(streams_of[1], 2), own, number, ROWS_DEV, EXPERTS, TOP, CAP, 2))(expert_ids_keys, expert_ids_turns).reshape((TOKENS, TOP))
    combine = jnp.clip(0.02 + 0.28 * jax.random.uniform(streams_of[2], (TOKENS, TOP), jnp.float32) ** block_scale(streams_of[2], (TOKENS, TOP), ((0, 32),), -0.2, 0.2), 0.02, 0.3)
    w_gate = gaussian(streams_of[3], (EXPERTS, D, FF), D ** -0.5, 0.09375, ((0, 8), (2, 4)))
    w_up = gaussian(streams_of[4], (EXPERTS, D, FF), D ** -0.5, 0.09375, ((0, 8), (2, 4)))
    w_down = gaussian(streams_of[5], (EXPERTS, FF, D), FF ** -0.5, 0.15625, ((0, 8), (1, 4)))
    w_query = gaussian(streams_of[6], (D, HQ * HD), D ** -0.5, 0.09375, ((1, 4),))
    w_key = gaussian(streams_of[7], (D, KVH * HD), D ** -0.5, 0.09375, ((1, 4),))
    w_value = gaussian(streams_of[8], (D, KVH * HD), D ** -0.5, 0.09375, ((1, 4),))
    cache_keys = draw_cache_keys(jax.random.fold_in(streams_of[12], 71), 0)
    cache_values = gaussian(streams_of[10], (TOKENS, KVH, WIN, HD), 1.0, 6.0, ((0, 8), (1, 4)))
    lengths = draw_lengths(jax.random.fold_in(streams_of[12], 71), 0)
    return dict(tokens=tokens, expert_ids=expert_ids, combine=combine, w_gate=w_gate, w_up=w_up, w_down=w_down, w_query=w_query, w_key=w_key, w_value=w_value, cache_keys=cache_keys, cache_values=cache_values, lengths=lengths)


EPSILON = 1e-06

def norm_rows(values):
    widened = values.astype(jnp.float32)
    return (widened * lax.rsqrt(lax.optimization_barrier(jnp.mean(widened * widened, axis=-1, keepdims=True)) + EPSILON)).astype(jnp.bfloat16)

def slot_numbers(chosen, experts):
    blocks_n, rows_n, picks_n = chosen.shape
    flat_ids = chosen.reshape(blocks_n, rows_n * picks_n)
    onehot = (flat_ids[:, :, None] == jnp.arange(experts, dtype=jnp.int32)[None, None, :]).astype(jnp.int32)
    before = jnp.cumsum(onehot, axis=1) - onehot
    return lax.optimization_barrier(jnp.sum(before * onehot, axis=-1)).reshape(blocks_n, rows_n, picks_n).astype(jnp.int32)

def attend(inputs):
    queries, keys_blk, values_blk, key_new, value_new, window = inputs
    scale_factor = 1.0 / math.sqrt(queries.shape[-1])
    scores = jnp.einsum('rhgd,rhjd->rhgj', queries.astype(jnp.float32), keys_blk.astype(jnp.float32), precision=lax.Precision.HIGHEST) * scale_factor
    own_score = jnp.einsum('rhgd,rhd->rhg', queries.astype(jnp.float32), key_new.astype(jnp.float32), precision=lax.Precision.HIGHEST) * scale_factor
    positions = jnp.arange(keys_blk.shape[2], dtype=jnp.int32)
    allowed = positions[None, None, None, :] >= (keys_blk.shape[2] - window)[:, None, None, None]
    masked = jnp.where(allowed, scores, -jnp.inf)
    highest = jnp.maximum(lax.optimization_barrier(jnp.max(masked, axis=-1)), own_score)
    weights = jnp.exp(masked - highest[..., None])
    own_weight = jnp.exp(own_score - highest)
    denominator = lax.optimization_barrier(jnp.sum(weights, axis=-1)) + own_weight
    probabilities = weights / denominator[..., None]
    own_prob = own_weight / denominator
    attended = jnp.einsum('rhgj,rhjd->rhgd', probabilities, values_blk.astype(jnp.float32), precision=lax.Precision.HIGHEST)
    attended = attended + own_prob[..., None] * value_new.astype(jnp.float32)[:, :, None, :]
    return attended.astype(jnp.bfloat16).reshape(queries.shape[0], -1)

def reference(tokens, expert_ids, combine, w_gate, w_up, w_down, w_query, w_key, w_value, cache_keys, cache_values, lengths):
    normed = norm_rows(tokens)
    blocks_n = TOKENS // ROWS_DEV
    chosen = expert_ids.reshape(blocks_n, ROWS_DEV, TOP)
    slot_ids = slot_numbers(chosen, EXPERTS)
    block_ids = jnp.arange(blocks_n, dtype=jnp.int32)[:, None, None]
    places = (chosen * (blocks_n * CAP) + block_ids * CAP + slot_ids).reshape(-1)
    row_ids = jnp.broadcast_to(jnp.arange(TOKENS, dtype=jnp.int32).reshape(blocks_n, ROWS_DEV, 1), chosen.shape).reshape(-1)
    slot_table = jnp.full((EXPERTS * blocks_n * CAP,), TOKENS, jnp.int32).at[places].set(row_ids)
    slot_table = slot_table.reshape(EXPERTS, blocks_n * CAP)
    weight_table = jnp.zeros((EXPERTS * blocks_n * CAP,), jnp.float32).at[places].set(combine.reshape(-1))
    weight_table = weight_table.reshape(EXPERTS, blocks_n * CAP)
    padded = jnp.concatenate([normed, jnp.zeros((1, D), jnp.bfloat16)], axis=0)
    hidden_group = FF // N_GD

    def expert_step(mixture, inputs):
        gate_w, up_w, down_w, indices, slot_weights = inputs
        picked = padded[indices]
        gate_val = jnp.dot(picked, gate_w, preferred_element_type=jnp.float32)
        up_val = jnp.dot(picked, up_w, preferred_element_type=jnp.float32)
        active = (jax.nn.silu(gate_val) * up_val).astype(jnp.bfloat16)
        result = jnp.zeros((indices.shape[0], D), jnp.float32)
        for member in range(N_GD):
            lower_edge = member * hidden_group
            partial_out = jnp.dot(active[:, lower_edge:lower_edge + hidden_group], down_w[lower_edge:lower_edge + hidden_group], preferred_element_type=jnp.float32).astype(jnp.bfloat16)
            result = result + partial_out.astype(jnp.float32)
        mixture = mixture.at[indices].add(slot_weights[:, None] * result)
        return (mixture, None)
    mixture, unused = lax.scan(expert_step, jnp.zeros((TOKENS + 1, D), jnp.float32), (w_gate, w_up, w_down, slot_table, weight_table))
    stream = (tokens.astype(jnp.float32) + mixture[:TOKENS]).astype(jnp.bfloat16)
    guard_norm = norm_rows(stream)
    queries = jnp.dot(guard_norm, w_query, preferred_element_type=jnp.float32)
    key_new = jnp.dot(guard_norm, w_key, preferred_element_type=jnp.float32).astype(jnp.bfloat16)
    value_new = jnp.dot(guard_norm, w_value, preferred_element_type=jnp.float32).astype(jnp.bfloat16)
    group_rows = ROWS_DEV * N_GD
    count_blocks = TOKENS // group_rows
    guard = lax.map(attend, (queries.reshape(count_blocks, group_rows, KVH, GROUP, HD), cache_keys.reshape(count_blocks, group_rows, KVH, WIN, HD), cache_values.reshape(count_blocks, group_rows, KVH, WIN, HD), key_new.reshape(count_blocks, group_rows, KVH, HD), value_new.reshape(count_blocks, group_rows, KVH, HD), lengths.reshape(count_blocks, group_rows)))
    return (stream, guard.reshape(TOKENS, HQ * HD))
```

```python
import functools
import math

import jax
import jax.numpy as jnp
from jax import lax
from jax.experimental import pallas as pl
from jax.experimental.pallas import tpu as pltpu
from jax.sharding import PartitionSpec as P

EPSILON = 1e-06


def norm_rows(values):
    widened = values.astype(jnp.float32)
    return (
        widened * lax.rsqrt(jnp.mean(widened * widened, axis=-1, keepdims=True) + EPSILON)
    ).astype(jnp.bfloat16)


def slot_numbers(chosen, experts):
    blocks_n, rows_n, picks_n = chosen.shape
    flat_ids = chosen.reshape(blocks_n, rows_n * picks_n)
    onehot = (flat_ids[:, :, None] == jnp.arange(experts, dtype=jnp.int32)[None, None, :]).astype(
        jnp.int32
    )
    before = jnp.cumsum(onehot, axis=1) - onehot
    return jnp.sum(before * onehot, axis=-1).reshape(blocks_n, rows_n, picks_n)


def build_slots(row_blocks, targets, slots_n):
    wanted = jnp.any(
        targets[:, None, :, :] == jnp.arange(slots_n, dtype=jnp.int32)[None, :, None, None], axis=-1
    )
    selector = wanted.astype(jnp.bfloat16)
    return jnp.einsum(
        "bsr,brd->bsd", selector, row_blocks, preferred_element_type=jnp.float32
    ).astype(jnp.bfloat16)


def per_device(
    tokens,
    expert_ids,
    combine,
    w_gate,
    w_up,
    w_down,
    w_query,
    w_key,
    w_value,
    cache_keys,
    cache_values,
    lengths,
):
    rows_n, width = tokens.shape
    picks_n = expert_ids.shape[1]
    experts = lax.axis_size("ep")
    members = lax.axis_size("gd")
    capacity = max(2, 3 * rows_n * picks_n // (2 * experts))
    slots_n = experts * capacity
    normed = norm_rows(tokens)
    own_slot = slot_numbers(expert_ids[None], experts)[0]
    own_dest = expert_ids * capacity + own_slot
    group_normed, group_ids = (
        lax.all_gather(normed, "gd", axis=0, tiled=True),
        lax.all_gather(expert_ids, "gd", axis=0, tiled=True),
    )
    group_ids = group_ids.reshape(members, rows_n, picks_n)
    group_dest = group_ids * capacity + slot_numbers(group_ids, experts)
    outgoing = build_slots(group_normed.reshape(members, rows_n, width), group_dest, slots_n)
    outgoing = outgoing.reshape(members, experts, capacity, width)
    arrived = lax.all_to_all(outgoing, "ep", split_axis=1, concat_axis=1, tiled=True)
    slot_rows = arrived.reshape(-1, width)
    gate_val = jnp.dot(slot_rows, w_gate[0], preferred_element_type=jnp.float32)
    up_val = jnp.dot(slot_rows, w_up[0], preferred_element_type=jnp.float32)
    active = (jax.nn.silu(gate_val) * up_val).astype(jnp.bfloat16)
    partial_out = jnp.dot(active, w_down[0], preferred_element_type=jnp.float32).astype(
        jnp.bfloat16
    )
    summed = lax.psum_scatter(
        lax.optimization_barrier(partial_out).astype(jnp.float32).astype(jnp.bfloat16),
        "gd",
        scatter_dimension=0,
        tiled=True,
    ).astype(jnp.float32)
    returned = lax.all_to_all(
        summed.reshape(experts, capacity, width), "ep", split_axis=0, concat_axis=0, tiled=True
    )
    matches = own_dest[:, :, None] == jnp.arange(slots_n, dtype=jnp.int32)[None, None, :]
    weight_rows = jnp.sum(jnp.where(matches, combine[:, :, None], 0.0), axis=1)
    mixture = jnp.dot(
        weight_rows,
        returned.reshape(slots_n, width),
        precision=lax.Precision.HIGHEST,
        preferred_element_type=jnp.float32,
    )
    stream = (tokens.astype(jnp.float32) + mixture).astype(jnp.bfloat16)
    group_stream = lax.all_gather(stream, "gd", axis=0, tiled=True)
    guard_norm = norm_rows(group_stream)
    queries = jnp.dot(guard_norm, w_query, preferred_element_type=jnp.float32)
    key_new = jnp.dot(guard_norm, w_key, preferred_element_type=jnp.float32).astype(jnp.bfloat16)
    value_new = jnp.dot(guard_norm, w_value, preferred_element_type=jnp.float32).astype(
        jnp.bfloat16
    )
    group_total, heads_kv, window_len, head_size = cache_keys.shape
    heads_per = w_query.shape[1] // (heads_kv * head_size)
    queries = queries.reshape(group_total, heads_kv, heads_per, head_size)
    key_new = key_new.reshape(group_total, heads_kv, head_size)
    value_new = value_new.reshape(group_total, heads_kv, head_size)
    scale_factor = 1.0 / math.sqrt(head_size)
    scores = (
        jnp.einsum(
            "rhgd,rhjd->rhgj",
            queries,
            cache_keys.astype(jnp.float32),
            precision=lax.Precision.HIGHEST,
        )
        * scale_factor
    )
    own_score = (
        jnp.einsum(
            "rhgd,rhd->rhg", queries, key_new.astype(jnp.float32), precision=lax.Precision.HIGHEST
        )
        * scale_factor
    )
    positions = jnp.arange(window_len, dtype=jnp.int32)
    allowed = positions[None, None, None, :] >= (window_len - lengths)[:, None, None, None]
    masked = jnp.where(allowed, scores, -jnp.inf)
    highest = jnp.maximum(jnp.max(masked, axis=-1), own_score)
    weights = jnp.exp(masked - highest[..., None])
    own_weight = jnp.exp(own_score - highest)
    denominator = jnp.sum(weights, axis=-1) + own_weight
    probabilities = weights / denominator[..., None]
    own_prob = own_weight / denominator
    attended = jnp.einsum(
        "rhgj,rhjd->rhgd",
        probabilities,
        cache_values.astype(jnp.float32),
        precision=lax.Precision.HIGHEST,
    )
    attended = attended + own_prob[..., None] * value_new.astype(jnp.float32)[:, :, None, :]
    guard = attended.astype(jnp.bfloat16).reshape(group_total, heads_kv * heads_per * head_size)
    return (stream, guard)


CORES = 2
CHIPS = 4
CHUNKS = 4
MESH = pl.DeviceIdType.MESH


def fused_kernel(
    groups,
    tokens_ref,
    ids_ref,
    combine_ref,
    lengths_ref,
    gate_hbm,
    up_hbm,
    down_hbm,
    query_hbm,
    key_hbm,
    value_hbm,
    cache_k_hbm,
    cache_v_hbm,
    stream_ref,
    guard_ref,
    w_in,
    w_out,
    w_guard,
    keys,
    values,
    rows_in,
    rows_all,
    weight_all,
    hidden,
    active,
    part,
    got_core,
    sum_core,
    got_chip,
    sum_chip,
    got_z,
    stream_all,
    load_sem,
    z_send,
    z_recv,
    x_send,
    x_recv,
    y_send,
    y_recv,
    d_send,
    d_recv,
    c_send,
    c_recv,
    r1_send,
    r1_recv,
    r2_send,
    r2_recv,
    r3_send,
    r3_recv,
    s_send,
    s_recv,
):
    rows_n, width = tokens_ref.shape
    half = width // 2
    unit = gate_hbm.shape[2]
    me_e = lax.axis_index("ep")
    g = lax.axis_index("gd")
    core = me_e % CORES
    chip = me_e // CORES
    x, y = chip % 2, chip // 2
    x_chip = y * 2 + (1 - x)
    y_chip = (1 - y) * 2 + x
    d_chip = (1 - y) * 2 + (1 - x)
    sibling = (chip * CORES + (1 - core), g)
    x_dev = (x_chip * CORES + core, g)
    y_dev = (y_chip * CORES + core, g)
    d_dev = (d_chip * CORES + core, g)

    def z_of(step):
        return (g + step) % groups

    loads = []

    def load(src, dst):
        copy = pltpu.make_async_copy(src, dst, load_sem.at[len(loads)])
        copy.start()
        loads.append(copy)

    barrier = pltpu.get_barrier_semaphore()
    peers = [sibling, x_dev, y_dev, d_dev] + [(me_e, z_of(k)) for k in range(1, groups)]
    for peer in peers:
        pl.semaphore_signal(barrier, inc=1, device_id=peer, device_id_type=MESH)

    load(gate_hbm.at[0], w_in.at[:, 0:unit])
    load(up_hbm.at[0], w_in.at[:, unit : 2 * unit])
    load(down_hbm.at[0], w_out)
    q_n, k_n = query_hbm.shape[1], key_hbm.shape[1]
    load(query_hbm, w_guard.at[:, 0:q_n])
    load(key_hbm, w_guard.at[:, q_n : q_n + k_n])
    load(value_hbm, w_guard.at[:, q_n + k_n : q_n + 2 * k_n])
    load(cache_k_hbm, keys)
    load(cache_v_hbm, values)

    wide = tokens_ref[...].astype(jnp.float32)
    normed = wide * lax.rsqrt(jnp.mean(wide * wide, axis=-1, keepdims=True) + EPSILON)
    lanes = lax.broadcasted_iota(jnp.int32, (rows_n, 128), 1)
    table = jnp.zeros((rows_n, 128), jnp.float32)
    for k in range(ids_ref.shape[1]):
        table = table + jnp.where(lanes == ids_ref[:, k : k + 1], combine_ref[:, k : k + 1], 0.0)
    table_top = table.astype(jnp.bfloat16).astype(jnp.float32)
    packed = jnp.concatenate([normed[:, :half], normed[:, half:]], axis=0)
    rows_in[core, chip, g, :, 0:half] = packed.astype(jnp.bfloat16)
    rows_in[core, chip, g, :, half : half + 128] = jnp.concatenate(
        [table_top, table - table_top], axis=0
    ).astype(jnp.bfloat16)

    pl.semaphore_wait(barrier, len(peers))

    sends = []

    def send(src, dst, send_sem, recv_sem, device):
        copy = pltpu.make_async_remote_copy(
            src_ref=src,
            dst_ref=dst,
            send_sem=send_sem,
            recv_sem=recv_sem,
            device_id=device,
            device_id_type=MESH,
        )
        copy.start()
        sends.append(copy)
        return copy

    def row_send(chip_of, step, send_sem, recv_sem, device):
        block = rows_in.at[core, chip_of, (g + groups - step) % groups]
        return send(block, block, send_sem, recv_sem, device)

    z_copies, x_copies, y_copies, d_copies, c_copies = {}, {}, {}, {}, {}

    def share(kind, chip_of, step):
        c_copies[kind, step] = row_send(
            chip_of, step, c_send.at[kind, step], c_recv.at[kind, step], sibling
        )

    def spread(step):
        x_copies[step] = row_send(chip, step, x_send.at[step], x_recv.at[step], x_dev)
        y_copies[step] = row_send(chip, step, y_send.at[step], y_recv.at[step], y_dev)
        share(0, chip, step)

    def forward(step):
        x_copies[step].wait_recv()
        if step % 2 == 1:
            d_copies[step] = row_send(x_chip, step, d_send.at[step], d_recv.at[step], y_dev)
        share(1, x_chip, step)
        y_copies[step].wait_recv()
        if step % 2 == 0:
            d_copies[step] = row_send(y_chip, step, d_send.at[step], d_recv.at[step], x_dev)
        share(2, y_chip, step)

    for k in range(1, groups):
        z_copies[k] = row_send(chip, 0, z_send.at[k], z_recv.at[k], (me_e, z_of(k)))
    spread(0)
    for k in range(1, groups):
        z_copies[k].wait_recv()
        spread(k)
        forward(k - 1)
    forward(groups - 1)
    for k in range(groups):
        d_copies[k].wait_recv()
        share(3, d_chip, k)
    for k in range(groups):
        for kind in range(4):
            c_copies[kind, k].wait_recv()

    group_rows = groups * rows_n

    def unpack(block, carry):
        c, h = block // CHIPS, block % CHIPS
        start = pl.multiple_of(block * group_rows, group_rows)
        for side in range(2):
            got = rows_in[c, h, :, :, 0:half].astype(jnp.float32)
            got = got[:, side * rows_n : (side + 1) * rows_n].reshape(group_rows, half)
            rows_all[pl.ds(start, group_rows), side * half : (side + 1) * half] = got.astype(
                jnp.bfloat16
            )
        extra = rows_in[c, h, :, :, half : half + 128].astype(jnp.float32)
        weight_all[pl.ds(start, group_rows), :] = (extra[:, :rows_n] + extra[:, rows_n:]).reshape(
            group_rows, 128
        )
        return carry

    lax.fori_loop(0, CORES * CHIPS, unpack, 0)

    loads[0].wait()
    loads[1].wait()
    tile = 256

    def first(n, carry):
        cols = pl.ds(pl.multiple_of(n * tile, tile), tile)
        hidden[:, cols] = jnp.dot(
            rows_all[...], w_in[:, cols], preferred_element_type=jnp.float32
        )
        return carry

    lax.fori_loop(0, 2 * unit // tile, first, 0)
    table_all = weight_all[...]
    picked = lax.broadcasted_iota(jnp.int32, table_all.shape, 1) == me_e
    row_weight = jnp.sum(jnp.where(picked, table_all, 0.0), axis=-1, keepdims=True)
    gate_val = hidden[:, 0:unit]
    active[...] = (
        gate_val / (1.0 + jnp.exp(-gate_val)) * hidden[:, unit : 2 * unit] * row_weight
    ).astype(jnp.bfloat16)
    loads[2].wait()

    span = width // CHUNKS
    piece = span // 2
    r1, r2, r3, s_copies = {}, {}, {}, {}

    def expert_chunk(t):
        blocks_n = CORES * CHIPS * groups
        for side in range(2):
            lower = t * span + side * piece
            out = jnp.dot(
                active[...], w_out[:, lower : lower + piece], preferred_element_type=jnp.float32
            ).reshape(CORES, CHIPS, groups, rows_n, piece)
            if side == 0:
                top = out
        part[t] = jnp.concatenate([top, out], axis=3).astype(jnp.bfloat16)
        r1[t] = send(
            part.at[t, 1 - core], got_core.at[t], r1_send.at[t], r1_recv.at[t], sibling
        )

    def chip_chunk(t):
        r1[t].wait_recv()
        total = part[t, core].astype(jnp.float32) + got_core[t].astype(jnp.float32)
        sum_core[t] = total.astype(jnp.bfloat16)
        for kind, (chip_to, device) in enumerate(
            ((d_chip, d_dev), (x_chip, x_dev), (y_chip, y_dev))
        ):
            r2[t, kind] = send(
                sum_core.at[t, chip_to],
                got_chip.at[t, kind],
                r2_send.at[t, kind],
                r2_recv.at[t, kind],
                device,
            )

    def z_chunk(t):
        total = sum_core[t, chip].astype(jnp.float32)
        for kind in range(3):
            r2[t, kind].wait_recv()
            total = total + got_chip[t, kind].astype(jnp.float32)
        sum_chip[t] = total.astype(jnp.bfloat16)
        for k in range(1, groups):
            r3[t, k] = send(
                sum_chip.at[t, z_of(k)],
                got_z.at[t, k],
                r3_send.at[t, k],
                r3_recv.at[t, k],
                (me_e, z_of(k)),
            )

    def stream_chunk(t):
        total = sum_chip[t, g].astype(jnp.float32)
        for k in range(1, groups):
            r3[t, k].wait_recv()
            total = total + got_z[t, k].astype(jnp.float32)
        mixture = jnp.concatenate([total[:rows_n], total[rows_n:]], axis=1)
        cols = slice(t * span, (t + 1) * span)
        stream = tokens_ref[:, cols].astype(jnp.float32) + mixture
        stream_ref[:, cols] = stream.astype(jnp.bfloat16)
        stream_all[t, g] = jnp.concatenate(
            [stream[:, :piece], stream[:, piece:]], axis=0
        ).astype(jnp.bfloat16)
        for k in range(1, groups):
            block = stream_all.at[t, g]
            s_copies[t, k] = send(
                block, block, s_send.at[t, k], s_recv.at[t, k], (me_e, z_of(k))
            )

    state = {}

    def guard_chunk(t):
        for k in range(1, groups):
            s_copies[t, k].wait_recv()
        got = stream_all[t].astype(jnp.float32)
        if t == 0:
            for i in range(3, 8):
                loads[i].wait()
        for side in range(2):
            rows = got[:, side * rows_n : (side + 1) * rows_n].reshape(group_rows, piece)
            lower = t * span + side * piece
            product = jnp.dot(
                rows.astype(jnp.bfloat16),
                w_guard[lower : lower + piece, :],
                preferred_element_type=jnp.float32,
            )
            square = jnp.sum(rows * rows, axis=-1, keepdims=True)
            if t == 0 and side == 0:
                state["qkv"], state["square"] = product, square
            else:
                state["qkv"] = state["qkv"] + product
                state["square"] = state["square"] + square

    stages = (expert_chunk, chip_chunk, z_chunk, stream_chunk, guard_chunk)
    for step in range(CHUNKS + len(stages) - 1):
        for late, stage in enumerate(stages):
            if 0 <= step - late < CHUNKS:
                stage(step - late)

    qkv = state["qkv"] * lax.rsqrt(state["square"] / width + EPSILON)
    head = keys.shape[1]
    heads = q_n // head
    window = keys.shape[0] // group_rows
    scale = 1.0 / math.sqrt(head)
    query = jnp.concatenate([qkv[:, h * head : (h + 1) * head] for h in range(heads)], axis=0)
    key_new = qkv[:, q_n : q_n + k_n].astype(jnp.bfloat16).astype(jnp.float32)
    value_new = qkv[:, q_n + k_n :].astype(jnp.bfloat16).astype(jnp.float32)
    key_new = jnp.concatenate([key_new] * heads, axis=0)
    value_new = jnp.concatenate([value_new] * heads, axis=0)
    allowed_n = jnp.concatenate([lengths_ref[...]] * heads, axis=0)
    all_rows = heads * group_rows
    own_score = jnp.sum(query * key_new, axis=-1, keepdims=True) * scale
    scores = None
    rest = query
    for _ in range(3):
        top = rest.astype(jnp.bfloat16)
        rest = rest - top.astype(jnp.float32)
        term = lax.dot_general(
            top, keys[...], (((1,), (1,)), ((), ())), preferred_element_type=jnp.float32
        )
        scores = term if scores is None else scores + term
    scores = scores * scale
    column = lax.broadcasted_iota(jnp.int32, scores.shape, 1)
    row = lax.broadcasted_iota(jnp.int32, (all_rows, 1), 0) % group_rows
    upper = (row + 1) * window
    allowed = (column >= upper - allowed_n) & (column < upper)
    masked = jnp.where(allowed, scores, -jnp.inf)
    highest = jnp.maximum(jnp.max(masked, axis=-1, keepdims=True), own_score)
    weights = jnp.exp(masked - highest)
    own_weight = jnp.exp(own_score - highest)
    denominator = jnp.sum(weights, axis=-1, keepdims=True) + own_weight
    attended = own_weight * value_new
    rest = weights
    for _ in range(2):
        top = rest.astype(jnp.bfloat16)
        rest = rest - top.astype(jnp.float32)
        attended = attended + jnp.dot(top, values[...], preferred_element_type=jnp.float32)
    attended = attended / denominator
    guard_ref[...] = jnp.concatenate(
        [attended[h * group_rows : (h + 1) * group_rows] for h in range(heads)], axis=1
    ).astype(jnp.bfloat16)
    for copy in sends:
        copy.wait_send()


def fused_device(
    tokens,
    expert_ids,
    combine,
    w_gate,
    w_up,
    w_down,
    w_query,
    w_key,
    w_value,
    cache_keys,
    cache_values,
    lengths,
):
    rows_n, width = tokens.shape
    groups = lax.axis_size("gd")
    unit = w_gate.shape[2]
    group_rows, heads_kv, window, head = cache_keys.shape
    total_rows = CORES * CHIPS * groups * rows_n
    piece = width // CHUNKS // 2
    pack = 2 * rows_n
    guard_n = w_query.shape[1] + w_key.shape[1] + w_value.shape[1]
    bf16, f32 = jnp.bfloat16, jnp.float32
    dma = pltpu.SemaphoreType.DMA
    in_vmem = pl.BlockSpec(memory_space=pltpu.VMEM)
    in_any = pl.BlockSpec(memory_space=pl.ANY)
    return pl.pallas_call(
        functools.partial(fused_kernel, groups),
        out_shape=(
            jax.ShapeDtypeStruct((rows_n, width), bf16),
            jax.ShapeDtypeStruct((group_rows, w_query.shape[1]), bf16),
        ),
        in_specs=[in_vmem] * 4 + [in_any] * 8,
        out_specs=(in_vmem, in_vmem),
        scratch_shapes=[
            pltpu.VMEM((width, 2 * unit), bf16),
            pltpu.VMEM((unit, width), bf16),
            pltpu.VMEM((width, guard_n), bf16),
            pltpu.VMEM((group_rows * window, head), bf16),
            pltpu.VMEM((group_rows * window, head), bf16),
            pltpu.VMEM((CORES, CHIPS, groups, pack, width // 2 + 128), bf16),
            pltpu.VMEM((total_rows, width), bf16),
            pltpu.VMEM((total_rows, 128), f32),
            pltpu.VMEM((total_rows, 2 * unit), f32),
            pltpu.VMEM((total_rows, unit), bf16),
            pltpu.VMEM((CHUNKS, CORES, CHIPS, groups, pack, piece), bf16),
            pltpu.VMEM((CHUNKS, CHIPS, groups, pack, piece), bf16),
            pltpu.VMEM((CHUNKS, CHIPS, groups, pack, piece), bf16),
            pltpu.VMEM((CHUNKS, 3, groups, pack, piece), bf16),
            pltpu.VMEM((CHUNKS, groups, pack, piece), bf16),
            pltpu.VMEM((CHUNKS, groups, pack, piece), bf16),
            pltpu.VMEM((CHUNKS, groups, pack, piece), bf16),
            dma((8,)),
            dma((groups,)),
            dma((groups,)),
            dma((groups,)),
            dma((groups,)),
            dma((groups,)),
            dma((groups,)),
            dma((groups,)),
            dma((groups,)),
            dma((4, groups)),
            dma((4, groups)),
            dma((CHUNKS,)),
            dma((CHUNKS,)),
            dma((CHUNKS, 3)),
            dma((CHUNKS, 3)),
            dma((CHUNKS, groups)),
            dma((CHUNKS, groups)),
            dma((CHUNKS, groups)),
            dma((CHUNKS, groups)),
        ],
        compiler_params=pltpu.CompilerParams(
            collective_id=0, has_side_effects=True, vmem_limit_bytes=52 * 1024 * 1024
        ),
    )(
        tokens,
        expert_ids,
        combine,
        lengths.reshape(group_rows, 1),
        w_gate,
        w_up,
        w_down,
        w_query,
        w_key,
        w_value,
        cache_keys.reshape(group_rows * heads_kv * window, head),
        cache_values.reshape(group_rows * heads_kv * window, head),
    )


def solution(mesh):
    fused = mesh.shape["ep"] == 8 and mesh.shape["gd"] == 4
    return jax.shard_map(
        fused_device if fused else per_device,
        mesh=mesh,
        in_specs=(
            P(("ep", "gd"), None),
            P(("ep", "gd"), None),
            P(("ep", "gd"), None),
            P("ep", None, "gd"),
            P("ep", None, "gd"),
            P("ep", "gd", None),
            P(None, "gd"),
            P(None, "gd"),
            P(None, "gd"),
            P("ep", "gd", None, None),
            P("ep", "gd", None, None),
            P("ep"),
        ),
        out_specs=(P(("ep", "gd"), None), P("ep", "gd")),
        check_vma=False,
    )
```

```python
import functools
import math

import jax
import jax.numpy as jnp
from jax import lax
from jax.experimental import pallas as pl
from jax.experimental.pallas import tpu as pltpu
from jax.sharding import PartitionSpec as P

EPSILON = 1e-06


def norm_rows(values):
    widened = values.astype(jnp.float32)
    return (
        widened * lax.rsqrt(jnp.mean(widened * widened, axis=-1, keepdims=True) + EPSILON)
    ).astype(jnp.bfloat16)


def slot_numbers(chosen, experts):
    blocks_n, rows_n, picks_n = chosen.shape
    flat_ids = chosen.reshape(blocks_n, rows_n * picks_n)
    onehot = (flat_ids[:, :, None] == jnp.arange(experts, dtype=jnp.int32)[None, None, :]).astype(
        jnp.int32
    )
    before = jnp.cumsum(onehot, axis=1) - onehot
    return jnp.sum(before * onehot, axis=-1).reshape(blocks_n, rows_n, picks_n)


def build_slots(row_blocks, targets, slots_n):
    wanted = jnp.any(
        targets[:, None, :, :] == jnp.arange(slots_n, dtype=jnp.int32)[None, :, None, None], axis=-1
    )
    selector = wanted.astype(jnp.bfloat16)
    return jnp.einsum(
        "bsr,brd->bsd", selector, row_blocks, preferred_element_type=jnp.float32
    ).astype(jnp.bfloat16)


def per_device(
    tokens,
    expert_ids,
    combine,
    w_gate,
    w_up,
    w_down,
    w_query,
    w_key,
    w_value,
    cache_keys,
    cache_values,
    lengths,
):
    rows_n, width = tokens.shape
    picks_n = expert_ids.shape[1]
    experts = lax.axis_size("ep")
    members = lax.axis_size("gd")
    capacity = max(2, 3 * rows_n * picks_n // (2 * experts))
    slots_n = experts * capacity
    normed = norm_rows(tokens)
    own_slot = slot_numbers(expert_ids[None], experts)[0]
    own_dest = expert_ids * capacity + own_slot
    group_normed, group_ids = (
        lax.all_gather(normed, "gd", axis=0, tiled=True),
        lax.all_gather(expert_ids, "gd", axis=0, tiled=True),
    )
    group_ids = group_ids.reshape(members, rows_n, picks_n)
    group_dest = group_ids * capacity + slot_numbers(group_ids, experts)
    outgoing = build_slots(group_normed.reshape(members, rows_n, width), group_dest, slots_n)
    outgoing = outgoing.reshape(members, experts, capacity, width)
    arrived = lax.all_to_all(outgoing, "ep", split_axis=1, concat_axis=1, tiled=True)
    slot_rows = arrived.reshape(-1, width)
    gate_val = jnp.dot(slot_rows, w_gate[0], preferred_element_type=jnp.float32)
    up_val = jnp.dot(slot_rows, w_up[0], preferred_element_type=jnp.float32)
    active = (jax.nn.silu(gate_val) * up_val).astype(jnp.bfloat16)
    partial_out = jnp.dot(active, w_down[0], preferred_element_type=jnp.float32).astype(
        jnp.bfloat16
    )
    summed = lax.psum_scatter(
        lax.optimization_barrier(partial_out).astype(jnp.float32).astype(jnp.bfloat16),
        "gd",
        scatter_dimension=0,
        tiled=True,
    ).astype(jnp.float32)
    returned = lax.all_to_all(
        summed.reshape(experts, capacity, width), "ep", split_axis=0, concat_axis=0, tiled=True
    )
    matches = own_dest[:, :, None] == jnp.arange(slots_n, dtype=jnp.int32)[None, None, :]
    weight_rows = jnp.sum(jnp.where(matches, combine[:, :, None], 0.0), axis=1)
    mixture = jnp.dot(
        weight_rows,
        returned.reshape(slots_n, width),
        precision=lax.Precision.HIGHEST,
        preferred_element_type=jnp.float32,
    )
    stream = (tokens.astype(jnp.float32) + mixture).astype(jnp.bfloat16)
    group_stream = lax.all_gather(stream, "gd", axis=0, tiled=True)
    guard_norm = norm_rows(group_stream)
    queries = jnp.dot(guard_norm, w_query, preferred_element_type=jnp.float32)
    key_new = jnp.dot(guard_norm, w_key, preferred_element_type=jnp.float32).astype(jnp.bfloat16)
    value_new = jnp.dot(guard_norm, w_value, preferred_element_type=jnp.float32).astype(
        jnp.bfloat16
    )
    group_total, heads_kv, window_len, head_size = cache_keys.shape
    heads_per = w_query.shape[1] // (heads_kv * head_size)
    queries = queries.reshape(group_total, heads_kv, heads_per, head_size)
    key_new = key_new.reshape(group_total, heads_kv, head_size)
    value_new = value_new.reshape(group_total, heads_kv, head_size)
    scale_factor = 1.0 / math.sqrt(head_size)
    scores = (
        jnp.einsum(
            "rhgd,rhjd->rhgj",
            queries,
            cache_keys.astype(jnp.float32),
            precision=lax.Precision.HIGHEST,
        )
        * scale_factor
    )
    own_score = (
        jnp.einsum(
            "rhgd,rhd->rhg", queries, key_new.astype(jnp.float32), precision=lax.Precision.HIGHEST
        )
        * scale_factor
    )
    positions = jnp.arange(window_len, dtype=jnp.int32)
    allowed = positions[None, None, None, :] >= (window_len - lengths)[:, None, None, None]
    masked = jnp.where(allowed, scores, -jnp.inf)
    highest = jnp.maximum(jnp.max(masked, axis=-1), own_score)
    weights = jnp.exp(masked - highest[..., None])
    own_weight = jnp.exp(own_score - highest)
    denominator = jnp.sum(weights, axis=-1) + own_weight
    probabilities = weights / denominator[..., None]
    own_prob = own_weight / denominator
    attended = jnp.einsum(
        "rhgj,rhjd->rhgd",
        probabilities,
        cache_values.astype(jnp.float32),
        precision=lax.Precision.HIGHEST,
    )
    attended = attended + own_prob[..., None] * value_new.astype(jnp.float32)[:, :, None, :]
    guard = attended.astype(jnp.bfloat16).reshape(group_total, heads_kv * heads_per * head_size)
    return (stream, guard)


CORES = 2
CHIPS = 4
CHUNKS = 8
MESH = pl.DeviceIdType.MESH


def as_column(line):
    size = line.shape[1]
    across = lax.broadcasted_iota(jnp.int32, (size, size), 1)
    down = lax.broadcasted_iota(jnp.int32, (size, size), 0)
    return jnp.sum(jnp.where(across == down, line, 0.0), axis=1, keepdims=True)


def fused_kernel(
    groups,
    tokens_hbm,
    ids_hbm,
    combine_hbm,
    lengths_hbm,
    gate_hbm,
    up_hbm,
    down_hbm,
    query_hbm,
    key_hbm,
    value_hbm,
    cache_k_hbm,
    cache_v_hbm,
    stream_ref,
    guard_ref,
    tokens_ref,
    ids_ref,
    combine_ref,
    lengths_ref,
    w_in,
    w_out,
    w_guard,
    keys,
    values,
    rows_in,
    rows_all,
    weight_all,
    hidden,
    active,
    part,
    got_core,
    sum_core,
    got_chip,
    sum_mid,
    sum_chip,
    got_z,
    stream_all,
    load_sem,
    z_send,
    z_recv,
    x_send,
    x_recv,
    y_send,
    y_recv,
    d_send,
    d_recv,
    c_send,
    c_recv,
    r1_send,
    r1_recv,
    r2_send,
    r2_recv,
    r3_send,
    r3_recv,
    s_send,
    s_recv,
):
    rows_n, width = tokens_hbm.shape
    half = width // 2
    unit = gate_hbm.shape[2]
    me_e = lax.axis_index("ep")
    g = lax.axis_index("gd")
    core = me_e % CORES
    chip = me_e // CORES
    x, y = chip % 2, chip // 2
    x_chip = y * 2 + (1 - x)
    y_chip = (1 - y) * 2 + x
    d_chip = (1 - y) * 2 + (1 - x)
    sibling = (chip * CORES + (1 - core), g)
    x_dev = (x_chip * CORES + core, g)
    y_dev = (y_chip * CORES + core, g)

    def z_of(step):
        return (g + step) % groups

    loads = []

    def load(src, dst):
        copy = pltpu.make_async_copy(src, dst, load_sem.at[len(loads)])
        copy.start()
        loads.append(copy)

    barrier = pltpu.get_barrier_semaphore()
    peers = [sibling, x_dev, y_dev] + [(me_e, z_of(k)) for k in range(1, groups)]
    for peer in peers:
        pl.semaphore_signal(barrier, inc=1, device_id=peer, device_id_type=MESH)

    load(tokens_hbm, tokens_ref)
    load(ids_hbm, ids_ref)
    load(combine_hbm, combine_ref)
    load(lengths_hbm, lengths_ref)
    load(gate_hbm.at[0], w_in.at[:, 0:unit])
    load(up_hbm.at[0], w_in.at[:, unit : 2 * unit])
    load(down_hbm.at[0], w_out)
    q_n, k_n = query_hbm.shape[1], key_hbm.shape[1]
    load(query_hbm, w_guard.at[:, 0:q_n])
    load(key_hbm, w_guard.at[:, q_n : q_n + k_n])
    load(value_hbm, w_guard.at[:, q_n + k_n : q_n + 2 * k_n])
    load(cache_k_hbm, keys)
    load(cache_v_hbm, values)

    for i in range(3):
        loads[i].wait()
    wide = tokens_ref[...].astype(jnp.float32)
    normed = wide * lax.rsqrt(jnp.mean(wide * wide, axis=-1, keepdims=True) + EPSILON)
    lanes = lax.broadcasted_iota(jnp.int32, (rows_n, 128), 1)
    table = jnp.zeros((rows_n, 128), jnp.float32)
    for k in range(ids_ref.shape[0]):
        named = as_column(ids_ref[k : k + 1, :].astype(jnp.float32)).astype(jnp.int32)
        share_of = as_column(combine_ref[k : k + 1, :])
        table = table + jnp.where(lanes == named, share_of, 0.0)
    table_top = table.astype(jnp.bfloat16).astype(jnp.float32)
    packed = jnp.concatenate([normed[:, :half], normed[:, half:]], axis=0)
    rows_in[core, chip, g, :, 0:half] = packed.astype(jnp.bfloat16)
    rows_in[core, chip, g, :, half : half + 128] = jnp.concatenate(
        [table_top, table - table_top], axis=0
    ).astype(jnp.bfloat16)

    pl.semaphore_wait(barrier, len(peers))

    sends = []

    def send(src, dst, send_sem, recv_sem, device):
        copy = pltpu.make_async_remote_copy(
            src_ref=src,
            dst_ref=dst,
            send_sem=send_sem,
            recv_sem=recv_sem,
            device_id=device,
            device_id_type=MESH,
        )
        copy.start()
        sends.append(copy)
        return copy

    def row_send(chip_of, step, send_sem, recv_sem, device):
        block = rows_in.at[core, chip_of, (g + groups - step) % groups]
        return send(block, block, send_sem, recv_sem, device)

    z_copies, x_copies, y_copies, d_copies, c_copies = {}, {}, {}, {}, {}

    def share(kind, chip_of, step):
        c_copies[kind, step] = row_send(
            chip_of, step, c_send.at[kind, step], c_recv.at[kind, step], sibling
        )

    def spread(step):
        x_copies[step] = row_send(chip, step, x_send.at[step], x_recv.at[step], x_dev)
        y_copies[step] = row_send(chip, step, y_send.at[step], y_recv.at[step], y_dev)
        share(0, chip, step)

    def forward(step):
        x_copies[step].wait_recv()
        if step % 2 == 1:
            d_copies[step] = row_send(x_chip, step, d_send.at[step], d_recv.at[step], y_dev)
        share(1, x_chip, step)
        y_copies[step].wait_recv()
        if step % 2 == 0:
            d_copies[step] = row_send(y_chip, step, d_send.at[step], d_recv.at[step], x_dev)
        share(2, y_chip, step)

    for k in range(1, groups):
        z_copies[k] = row_send(chip, 0, z_send.at[k], z_recv.at[k], (me_e, z_of(k)))
    spread(0)
    for k in range(1, groups):
        z_copies[k].wait_recv()
        spread(k)
        forward(k - 1)
    forward(groups - 1)
    for k in range(groups):
        d_copies[k].wait_recv()
        share(3, d_chip, k)
    for k in range(groups):
        for kind in range(4):
            c_copies[kind, k].wait_recv()

    group_rows = groups * rows_n

    def unpack(block, carry):
        c, h = block // CHIPS, block % CHIPS
        start = pl.multiple_of(block * group_rows, group_rows)
        for side in range(2):
            got = rows_in[c, h, :, :, 0:half].astype(jnp.float32)
            got = got[:, side * rows_n : (side + 1) * rows_n].reshape(group_rows, half)
            rows_all[pl.ds(start, group_rows), side * half : (side + 1) * half] = got.astype(
                jnp.bfloat16
            )
        extra = rows_in[c, h, :, :, half : half + 128].astype(jnp.float32)
        weight_all[pl.ds(start, group_rows), :] = (extra[:, :rows_n] + extra[:, rows_n:]).reshape(
            group_rows, 128
        )
        return carry

    lax.fori_loop(0, CORES * CHIPS, unpack, 0)

    loads[4].wait()
    loads[5].wait()
    tile = 256

    def first(n, carry):
        cols = pl.ds(pl.multiple_of(n * tile, tile), tile)
        hidden[:, cols] = jnp.dot(
            rows_all[...], w_in[:, cols], preferred_element_type=jnp.float32
        )
        return carry

    lax.fori_loop(0, 2 * unit // tile, first, 0)
    table_all = weight_all[...]
    picked = lax.broadcasted_iota(jnp.int32, table_all.shape, 1) == me_e
    row_weight = jnp.sum(jnp.where(picked, table_all, 0.0), axis=-1, keepdims=True)
    gate_val = hidden[:, 0:unit]
    active[...] = (
        gate_val / (1.0 + jnp.exp(-gate_val)) * hidden[:, unit : 2 * unit] * row_weight
    ).astype(jnp.bfloat16)
    loads[6].wait()

    span = width // CHUNKS
    piece = span // 2
    r1, r2, r3, s_copies = {}, {}, {}, {}

    def expert_chunk(t):
        blocks_n = CORES * CHIPS * groups
        for side in range(2):
            lower = t * span + side * piece
            out = jnp.dot(
                active[...], w_out[:, lower : lower + piece], preferred_element_type=jnp.float32
            ).reshape(CORES, CHIPS, groups, rows_n, piece)
            if side == 0:
                top = out
        part[t] = jnp.concatenate([top, out], axis=3).astype(jnp.bfloat16)
        r1[t] = send(
            part.at[t, 1 - core], got_core.at[t], r1_send.at[t], r1_recv.at[t], sibling
        )

    def chip_chunk(t):
        r1[t].wait_recv()
        total = part[t, core].astype(jnp.float32) + got_core[t].astype(jnp.float32)
        sum_core[t] = total.astype(jnp.bfloat16)
        first_chip, first_dev = (x_chip, x_dev) if t % 2 == 0 else (y_chip, y_dev)
        for kind, chip_to in ((1, d_chip), (0, first_chip)):
            r2[t, kind] = send(
                sum_core.at[t, chip_to],
                got_chip.at[t, kind],
                r2_send.at[t, kind],
                r2_recv.at[t, kind],
                first_dev,
            )

    def mid_chunk(t):
        second_chip, second_dev = (y_chip, y_dev) if t % 2 == 0 else (x_chip, x_dev)
        r2[t, 1].wait_recv()
        total = sum_core[t, second_chip].astype(jnp.float32) + got_chip[t, 1].astype(jnp.float32)
        sum_mid[t] = total.astype(jnp.bfloat16)
        r2[t, 2] = send(
            sum_mid.at[t], got_chip.at[t, 2], r2_send.at[t, 2], r2_recv.at[t, 2], second_dev
        )

    def z_chunk(t):
        total = sum_core[t, chip].astype(jnp.float32)
        for kind in (0, 2):
            r2[t, kind].wait_recv()
            total = total + got_chip[t, kind].astype(jnp.float32)
        sum_chip[t] = total.astype(jnp.bfloat16)
        for k in range(1, groups):
            r3[t, k] = send(
                sum_chip.at[t, z_of(k)],
                got_z.at[t, k],
                r3_send.at[t, k],
                r3_recv.at[t, k],
                (me_e, z_of(k)),
            )

    def stream_chunk(t):
        total = sum_chip[t, g].astype(jnp.float32)
        for k in range(1, groups):
            r3[t, k].wait_recv()
            total = total + got_z[t, k].astype(jnp.float32)
        mixture = jnp.concatenate([total[:rows_n], total[rows_n:]], axis=1)
        cols = slice(t * span, (t + 1) * span)
        stream = tokens_ref[:, cols].astype(jnp.float32) + mixture
        stream_ref[:, cols] = stream.astype(jnp.bfloat16)
        stream_all[t, g] = jnp.concatenate(
            [stream[:, :piece], stream[:, piece:]], axis=0
        ).astype(jnp.bfloat16)
        for k in range(1, groups):
            block = stream_all.at[t, g]
            s_copies[t, k] = send(
                block, block, s_send.at[t, k], s_recv.at[t, k], (me_e, z_of(k))
            )

    state = {}

    def guard_chunk(t):
        for k in range(1, groups):
            s_copies[t, k].wait_recv()
        got = stream_all[t].astype(jnp.float32)
        if t == 0:
            for i in (3, 7, 8, 9, 10, 11):
                loads[i].wait()
        for side in range(2):
            rows = got[:, side * rows_n : (side + 1) * rows_n].reshape(group_rows, piece)
            lower = t * span + side * piece
            product = jnp.dot(
                rows.astype(jnp.bfloat16),
                w_guard[lower : lower + piece, :],
                preferred_element_type=jnp.float32,
            )
            square = jnp.sum(rows * rows, axis=-1, keepdims=True)
            if t == 0 and side == 0:
                state["qkv"], state["square"] = product, square
            else:
                state["qkv"] = state["qkv"] + product
                state["square"] = state["square"] + square

    stages = (expert_chunk, chip_chunk, mid_chunk, z_chunk, stream_chunk, guard_chunk)
    for step in range(CHUNKS + len(stages) - 1):
        for late, stage in enumerate(stages):
            if 0 <= step - late < CHUNKS:
                stage(step - late)

    qkv = state["qkv"] * lax.rsqrt(state["square"] / width + EPSILON)
    head = keys.shape[1]
    heads = q_n // head
    window = keys.shape[0] // group_rows
    scale = 1.0 / math.sqrt(head)
    key_new = qkv[:, q_n : q_n + k_n].astype(jnp.bfloat16).astype(jnp.float32)
    value_new = qkv[:, q_n + k_n :].astype(jnp.bfloat16).astype(jnp.float32)
    lengths_n = as_column(lengths_ref[...].astype(jnp.float32)).astype(jnp.int32)
    span_keys = rows_n * window
    outs = []
    for a in range(groups):
        here = slice(a * rows_n, (a + 1) * rows_n)
        query = jnp.concatenate([qkv[here, h * head : (h + 1) * head] for h in range(heads)], axis=0)
        key_own = jnp.concatenate([key_new[here]] * heads, axis=0)
        value_own = jnp.concatenate([value_new[here]] * heads, axis=0)
        allowed_n = jnp.concatenate([lengths_n[here]] * heads, axis=0)
        own_score = jnp.sum(query * key_own, axis=-1, keepdims=True) * scale
        pieces, rest = [], query
        for _ in range(3):
            top = rest.astype(jnp.bfloat16).astype(jnp.float32)
            pieces.append(top)
            rest = rest - top
        product = lax.dot_general(
            jnp.concatenate(pieces, axis=0).astype(jnp.bfloat16),
            keys[a * span_keys : (a + 1) * span_keys, :],
            (((1,), (1,)), ((), ())),
            preferred_element_type=jnp.float32,
        )
        all_rows = heads * rows_n
        scores = (
            product[:all_rows] + product[all_rows : 2 * all_rows] + product[2 * all_rows :]
        ) * scale
        column = lax.broadcasted_iota(jnp.int32, scores.shape, 1)
        row = lax.broadcasted_iota(jnp.int32, (all_rows, 1), 0) % rows_n
        upper = (row + 1) * window
        allowed = (column >= upper - allowed_n) & (column < upper)
        masked = jnp.where(allowed, scores, -jnp.inf)
        highest = jnp.maximum(jnp.max(masked, axis=-1, keepdims=True), own_score)
        weights = jnp.exp(masked - highest)
        own_weight = jnp.exp(own_score - highest)
        denominator = jnp.sum(weights, axis=-1, keepdims=True) + own_weight
        top = weights.astype(jnp.bfloat16).astype(jnp.float32)
        product = jnp.dot(
            jnp.concatenate([top, weights - top], axis=0).astype(jnp.bfloat16),
            values[a * span_keys : (a + 1) * span_keys, :],
            preferred_element_type=jnp.float32,
        )
        attended = product[:all_rows] + product[all_rows:] + own_weight * value_own
        attended = attended / denominator
        outs.append(
            jnp.concatenate(
                [attended[h * rows_n : (h + 1) * rows_n] for h in range(heads)], axis=1
            )
        )
    guard_ref[...] = jnp.concatenate(outs, axis=0).astype(jnp.bfloat16)
    for copy in sends:
        copy.wait_send()


def fused_device(
    tokens,
    expert_ids,
    combine,
    w_gate,
    w_up,
    w_down,
    w_query,
    w_key,
    w_value,
    cache_keys,
    cache_values,
    lengths,
):
    rows_n, width = tokens.shape
    groups = lax.axis_size("gd")
    unit = w_gate.shape[2]
    group_rows, heads_kv, window, head = cache_keys.shape
    total_rows = CORES * CHIPS * groups * rows_n
    piece = width // CHUNKS // 2
    pack = 2 * rows_n
    guard_n = w_query.shape[1] + w_key.shape[1] + w_value.shape[1]
    bf16, f32 = jnp.bfloat16, jnp.float32
    dma = pltpu.SemaphoreType.DMA
    in_vmem = pl.BlockSpec(memory_space=pltpu.VMEM)
    in_any = pl.BlockSpec(memory_space=pl.ANY)
    return pl.pallas_call(
        functools.partial(fused_kernel, groups),
        out_shape=(
            jax.ShapeDtypeStruct((rows_n, width), bf16),
            jax.ShapeDtypeStruct((group_rows, w_query.shape[1]), bf16),
        ),
        in_specs=[in_any] * 12,
        out_specs=(in_vmem, in_vmem),
        scratch_shapes=[
            pltpu.VMEM((rows_n, width), bf16),
            pltpu.VMEM((expert_ids.shape[1], rows_n), jnp.int32),
            pltpu.VMEM((combine.shape[1], rows_n), f32),
            pltpu.VMEM((1, group_rows), jnp.int32),
            pltpu.VMEM((width, 2 * unit), bf16),
            pltpu.VMEM((unit, width), bf16),
            pltpu.VMEM((width, guard_n), bf16),
            pltpu.VMEM((group_rows * window, head), bf16),
            pltpu.VMEM((group_rows * window, head), bf16),
            pltpu.VMEM((CORES, CHIPS, groups, pack, width // 2 + 128), bf16),
            pltpu.VMEM((total_rows, width), bf16),
            pltpu.VMEM((total_rows, 128), f32),
            pltpu.VMEM((total_rows, 2 * unit), f32),
            pltpu.VMEM((total_rows, unit), bf16),
            pltpu.VMEM((CHUNKS, CORES, CHIPS, groups, pack, piece), bf16),
            pltpu.VMEM((CHUNKS, CHIPS, groups, pack, piece), bf16),
            pltpu.VMEM((CHUNKS, CHIPS, groups, pack, piece), bf16),
            pltpu.VMEM((CHUNKS, 3, groups, pack, piece), bf16),
            pltpu.VMEM((CHUNKS, groups, pack, piece), bf16),
            pltpu.VMEM((CHUNKS, groups, pack, piece), bf16),
            pltpu.VMEM((CHUNKS, groups, pack, piece), bf16),
            pltpu.VMEM((CHUNKS, groups, pack, piece), bf16),
            dma((12,)),
            dma((groups,)),
            dma((groups,)),
            dma((groups,)),
            dma((groups,)),
            dma((groups,)),
            dma((groups,)),
            dma((groups,)),
            dma((groups,)),
            dma((4, groups)),
            dma((4, groups)),
            dma((CHUNKS,)),
            dma((CHUNKS,)),
            dma((CHUNKS, 3)),
            dma((CHUNKS, 3)),
            dma((CHUNKS, groups)),
            dma((CHUNKS, groups)),
            dma((CHUNKS, groups)),
            dma((CHUNKS, groups)),
        ],
        compiler_params=pltpu.CompilerParams(
            collective_id=0, has_side_effects=True, vmem_limit_bytes=63 * 1024 * 1024
        ),
    )(
        tokens,
        expert_ids.T,
        combine.T,
        lengths.reshape(1, group_rows),
        w_gate,
        w_up,
        w_down,
        w_query,
        w_key,
        w_value,
        cache_keys.reshape(group_rows * heads_kv * window, head),
        cache_values.reshape(group_rows * heads_kv * window, head),
    )


def solution(mesh):
    fused = mesh.shape["ep"] == 8 and mesh.shape["gd"] == 4
    return jax.shard_map(
        fused_device if fused else per_device,
        mesh=mesh,
        in_specs=(
            P(("ep", "gd"), None),
            P(("ep", "gd"), None),
            P(("ep", "gd"), None),
            P("ep", None, "gd"),
            P("ep", None, "gd"),
            P("ep", "gd", None),
            P(None, "gd"),
            P(None, "gd"),
            P(None, "gd"),
            P("ep", "gd", None, None),
            P("ep", "gd", None, None),
            P("ep"),
        ),
        out_specs=(P(("ep", "gd"), None), P("ep", "gd")),
        check_vma=False,
    )
```

```python
import functools
import math

import jax
import jax.numpy as jnp
from jax import lax
from jax.experimental import pallas as pl
from jax.experimental.pallas import tpu as pltpu
from jax.sharding import PartitionSpec as P

EPSILON = 1e-06


def norm_rows(values):
    widened = values.astype(jnp.float32)
    return (
        widened * lax.rsqrt(jnp.mean(widened * widened, axis=-1, keepdims=True) + EPSILON)
    ).astype(jnp.bfloat16)


def slot_numbers(chosen, experts):
    blocks_n, rows_n, picks_n = chosen.shape
    flat_ids = chosen.reshape(blocks_n, rows_n * picks_n)
    onehot = (flat_ids[:, :, None] == jnp.arange(experts, dtype=jnp.int32)[None, None, :]).astype(
        jnp.int32
    )
    before = jnp.cumsum(onehot, axis=1) - onehot
    return jnp.sum(before * onehot, axis=-1).reshape(blocks_n, rows_n, picks_n)


def build_slots(row_blocks, targets, slots_n):
    wanted = jnp.any(
        targets[:, None, :, :] == jnp.arange(slots_n, dtype=jnp.int32)[None, :, None, None], axis=-1
    )
    selector = wanted.astype(jnp.bfloat16)
    return jnp.einsum(
        "bsr,brd->bsd", selector, row_blocks, preferred_element_type=jnp.float32
    ).astype(jnp.bfloat16)


def per_device(
    tokens,
    expert_ids,
    combine,
    w_gate,
    w_up,
    w_down,
    w_query,
    w_key,
    w_value,
    cache_keys,
    cache_values,
    lengths,
):
    rows_n, width = tokens.shape
    picks_n = expert_ids.shape[1]
    experts = lax.axis_size("ep")
    members = lax.axis_size("gd")
    capacity = max(2, 3 * rows_n * picks_n // (2 * experts))
    slots_n = experts * capacity
    normed = norm_rows(tokens)
    own_slot = slot_numbers(expert_ids[None], experts)[0]
    own_dest = expert_ids * capacity + own_slot
    group_normed, group_ids = (
        lax.all_gather(normed, "gd", axis=0, tiled=True),
        lax.all_gather(expert_ids, "gd", axis=0, tiled=True),
    )
    group_ids = group_ids.reshape(members, rows_n, picks_n)
    group_dest = group_ids * capacity + slot_numbers(group_ids, experts)
    outgoing = build_slots(group_normed.reshape(members, rows_n, width), group_dest, slots_n)
    outgoing = outgoing.reshape(members, experts, capacity, width)
    arrived = lax.all_to_all(outgoing, "ep", split_axis=1, concat_axis=1, tiled=True)
    slot_rows = arrived.reshape(-1, width)
    gate_val = jnp.dot(slot_rows, w_gate[0], preferred_element_type=jnp.float32)
    up_val = jnp.dot(slot_rows, w_up[0], preferred_element_type=jnp.float32)
    active = (jax.nn.silu(gate_val) * up_val).astype(jnp.bfloat16)
    partial_out = jnp.dot(active, w_down[0], preferred_element_type=jnp.float32).astype(
        jnp.bfloat16
    )
    summed = lax.psum_scatter(
        lax.optimization_barrier(partial_out).astype(jnp.float32).astype(jnp.bfloat16),
        "gd",
        scatter_dimension=0,
        tiled=True,
    ).astype(jnp.float32)
    returned = lax.all_to_all(
        summed.reshape(experts, capacity, width), "ep", split_axis=0, concat_axis=0, tiled=True
    )
    matches = own_dest[:, :, None] == jnp.arange(slots_n, dtype=jnp.int32)[None, None, :]
    weight_rows = jnp.sum(jnp.where(matches, combine[:, :, None], 0.0), axis=1)
    mixture = jnp.dot(
        weight_rows,
        returned.reshape(slots_n, width),
        precision=lax.Precision.HIGHEST,
        preferred_element_type=jnp.float32,
    )
    stream = (tokens.astype(jnp.float32) + mixture).astype(jnp.bfloat16)
    group_stream = lax.all_gather(stream, "gd", axis=0, tiled=True)
    guard_norm = norm_rows(group_stream)
    queries = jnp.dot(guard_norm, w_query, preferred_element_type=jnp.float32)
    key_new = jnp.dot(guard_norm, w_key, preferred_element_type=jnp.float32).astype(jnp.bfloat16)
    value_new = jnp.dot(guard_norm, w_value, preferred_element_type=jnp.float32).astype(
        jnp.bfloat16
    )
    group_total, heads_kv, window_len, head_size = cache_keys.shape
    heads_per = w_query.shape[1] // (heads_kv * head_size)
    queries = queries.reshape(group_total, heads_kv, heads_per, head_size)
    key_new = key_new.reshape(group_total, heads_kv, head_size)
    value_new = value_new.reshape(group_total, heads_kv, head_size)
    scale_factor = 1.0 / math.sqrt(head_size)
    scores = (
        jnp.einsum(
            "rhgd,rhjd->rhgj",
            queries,
            cache_keys.astype(jnp.float32),
            precision=lax.Precision.HIGHEST,
        )
        * scale_factor
    )
    own_score = (
        jnp.einsum(
            "rhgd,rhd->rhg", queries, key_new.astype(jnp.float32), precision=lax.Precision.HIGHEST
        )
        * scale_factor
    )
    positions = jnp.arange(window_len, dtype=jnp.int32)
    allowed = positions[None, None, None, :] >= (window_len - lengths)[:, None, None, None]
    masked = jnp.where(allowed, scores, -jnp.inf)
    highest = jnp.maximum(jnp.max(masked, axis=-1), own_score)
    weights = jnp.exp(masked - highest[..., None])
    own_weight = jnp.exp(own_score - highest)
    denominator = jnp.sum(weights, axis=-1) + own_weight
    probabilities = weights / denominator[..., None]
    own_prob = own_weight / denominator
    attended = jnp.einsum(
        "rhgj,rhjd->rhgd",
        probabilities,
        cache_values.astype(jnp.float32),
        precision=lax.Precision.HIGHEST,
    )
    attended = attended + own_prob[..., None] * value_new.astype(jnp.float32)[:, :, None, :]
    guard = attended.astype(jnp.bfloat16).reshape(group_total, heads_kv * heads_per * head_size)
    return (stream, guard)


CORES = 2
CHIPS = 4
CHUNKS = 4
MESH = pl.DeviceIdType.MESH


def as_column(line):
    size = line.shape[1]
    across = lax.broadcasted_iota(jnp.int32, (size, size), 1)
    down = lax.broadcasted_iota(jnp.int32, (size, size), 0)
    return jnp.sum(jnp.where(across == down, line, 0.0), axis=1, keepdims=True)


def fused_kernel(
    groups,
    tokens_hbm,
    ids_hbm,
    combine_hbm,
    lengths_hbm,
    gate_hbm,
    up_hbm,
    down_hbm,
    query_hbm,
    key_hbm,
    value_hbm,
    cache_k_hbm,
    cache_v_hbm,
    stream_ref,
    guard_ref,
    tokens_ref,
    ids_ref,
    combine_ref,
    lengths_ref,
    w_in,
    w_out,
    w_guard,
    keys,
    values,
    rows_in,
    rows_all,
    weight_all,
    hidden,
    active,
    part,
    got_core,
    sum_core,
    got_chip,
    sum_mid,
    sum_chip,
    got_z,
    stream_all,
    load_sem,
    z_send,
    z_recv,
    x_send,
    x_recv,
    y_send,
    y_recv,
    d_send,
    d_recv,
    c_send,
    c_recv,
    r1_send,
    r1_recv,
    r2_send,
    r2_recv,
    r3_send,
    r3_recv,
    s_send,
    s_recv,
):
    rows_n, width = tokens_hbm.shape
    half = width // 2
    unit = gate_hbm.shape[2]
    me_e = lax.axis_index("ep")
    g = lax.axis_index("gd")
    core = me_e % CORES
    chip = me_e // CORES
    x, y = chip % 2, chip // 2
    x_chip = y * 2 + (1 - x)
    y_chip = (1 - y) * 2 + x
    d_chip = (1 - y) * 2 + (1 - x)
    sibling = (chip * CORES + (1 - core), g)
    x_dev = (x_chip * CORES + core, g)
    y_dev = (y_chip * CORES + core, g)

    def z_of(step):
        return (g + step) % groups

    loads = []

    def load(src, dst):
        copy = pltpu.make_async_copy(src, dst, load_sem.at[len(loads)])
        copy.start()
        loads.append(copy)

    barrier = pltpu.get_barrier_semaphore()
    peers = [sibling, x_dev, y_dev] + [(me_e, z_of(k)) for k in range(1, groups)]
    for peer in peers:
        pl.semaphore_signal(barrier, inc=1, device_id=peer, device_id_type=MESH)

    load(tokens_hbm, tokens_ref)
    load(ids_hbm, ids_ref)
    load(combine_hbm, combine_ref)
    load(lengths_hbm, lengths_ref)
    load(gate_hbm.at[0], w_in.at[:, 0:unit])
    load(up_hbm.at[0], w_in.at[:, unit : 2 * unit])
    load(down_hbm.at[0], w_out)
    q_n, k_n = query_hbm.shape[1], key_hbm.shape[1]
    load(query_hbm, w_guard.at[:, 0:q_n])
    load(key_hbm, w_guard.at[:, q_n : q_n + k_n])
    load(value_hbm, w_guard.at[:, q_n + k_n : q_n + 2 * k_n])
    load(cache_k_hbm, keys)
    load(cache_v_hbm, values)

    for i in range(3):
        loads[i].wait()
    wide = tokens_ref[...].astype(jnp.float32)
    normed = wide * lax.rsqrt(jnp.mean(wide * wide, axis=-1, keepdims=True) + EPSILON)
    lanes = lax.broadcasted_iota(jnp.int32, (rows_n, 128), 1)
    table = jnp.zeros((rows_n, 128), jnp.float32)
    for k in range(ids_ref.shape[0]):
        named = as_column(ids_ref[k : k + 1, :].astype(jnp.float32)).astype(jnp.int32)
        share_of = as_column(combine_ref[k : k + 1, :])
        table = table + jnp.where(lanes == named, share_of, 0.0)
    table_top = table.astype(jnp.bfloat16).astype(jnp.float32)
    packed = jnp.concatenate([normed[:, :half], normed[:, half:]], axis=0)
    rows_in[core, chip, g, :, 0:half] = packed.astype(jnp.bfloat16)
    rows_in[core, chip, g, :, half : half + 128] = jnp.concatenate(
        [table_top, table - table_top], axis=0
    ).astype(jnp.bfloat16)

    pl.semaphore_wait(barrier, len(peers))

    sends = []

    def send(src, dst, send_sem, recv_sem, device):
        copy = pltpu.make_async_remote_copy(
            src_ref=src,
            dst_ref=dst,
            send_sem=send_sem,
            recv_sem=recv_sem,
            device_id=device,
            device_id_type=MESH,
        )
        copy.start()
        sends.append(copy)
        return copy

    def row_send(chip_of, step, send_sem, recv_sem, device):
        block = rows_in.at[core, chip_of, (g + groups - step) % groups]
        return send(block, block, send_sem, recv_sem, device)

    z_copies, x_copies, y_copies, d_copies, c_copies = {}, {}, {}, {}, {}

    def share(kind, chip_of, step):
        c_copies[kind, step] = row_send(
            chip_of, step, c_send.at[kind, step], c_recv.at[kind, step], sibling
        )

    def spread(step):
        x_copies[step] = row_send(chip, step, x_send.at[step], x_recv.at[step], x_dev)
        y_copies[step] = row_send(chip, step, y_send.at[step], y_recv.at[step], y_dev)
        share(0, chip, step)

    def forward(step):
        x_copies[step].wait_recv()
        if step % 2 == 1:
            d_copies[step] = row_send(x_chip, step, d_send.at[step], d_recv.at[step], y_dev)
        share(1, x_chip, step)
        y_copies[step].wait_recv()
        if step % 2 == 0:
            d_copies[step] = row_send(y_chip, step, d_send.at[step], d_recv.at[step], x_dev)
        share(2, y_chip, step)

    for k in range(1, groups):
        z_copies[k] = row_send(chip, 0, z_send.at[k], z_recv.at[k], (me_e, z_of(k)))
    spread(0)
    for k in range(1, groups):
        z_copies[k].wait_recv()
        spread(k)
        forward(k - 1)
    forward(groups - 1)
    for k in range(groups):
        d_copies[k].wait_recv()
        share(3, d_chip, k)
    for k in range(groups):
        for kind in range(4):
            c_copies[kind, k].wait_recv()

    group_rows = groups * rows_n

    def unpack(block, carry):
        c, h = block // CHIPS, block % CHIPS
        start = pl.multiple_of(block * group_rows, group_rows)
        for side in range(2):
            got = rows_in[c, h, :, :, 0:half].astype(jnp.float32)
            got = got[:, side * rows_n : (side + 1) * rows_n].reshape(group_rows, half)
            rows_all[pl.ds(start, group_rows), side * half : (side + 1) * half] = got.astype(
                jnp.bfloat16
            )
        extra = rows_in[c, h, :, :, half : half + 128].astype(jnp.float32)
        weight_all[pl.ds(start, group_rows), :] = (extra[:, :rows_n] + extra[:, rows_n:]).reshape(
            group_rows, 128
        )
        return carry

    lax.fori_loop(0, CORES * CHIPS, unpack, 0)

    loads[4].wait()
    loads[5].wait()
    tile = 256

    def first(n, carry):
        cols = pl.ds(pl.multiple_of(n * tile, tile), tile)
        hidden[:, cols] = jnp.dot(
            rows_all[...], w_in[:, cols], preferred_element_type=jnp.float32
        )
        return carry

    lax.fori_loop(0, 2 * unit // tile, first, 0)
    table_all = weight_all[...]
    picked = lax.broadcasted_iota(jnp.int32, table_all.shape, 1) == me_e
    row_weight = jnp.sum(jnp.where(picked, table_all, 0.0), axis=-1, keepdims=True)
    gate_val = hidden[:, 0:unit]
    active[...] = (
        gate_val / (1.0 + jnp.exp(-gate_val)) * hidden[:, unit : 2 * unit] * row_weight
    ).astype(jnp.bfloat16)
    loads[6].wait()

    span = width // CHUNKS
    piece = span // 2
    r1, r2, r3, s_copies = {}, {}, {}, {}

    def expert_chunk(t):
        blocks_n = CORES * CHIPS * groups
        for side in range(2):
            lower = t * span + side * piece
            out = jnp.dot(
                active[...], w_out[:, lower : lower + piece], preferred_element_type=jnp.float32
            ).reshape(CORES, CHIPS, groups, rows_n, piece)
            if side == 0:
                top = out
        part[t] = jnp.concatenate([top, out], axis=3).astype(jnp.bfloat16)
        r1[t] = send(
            part.at[t, 1 - core], got_core.at[t], r1_send.at[t], r1_recv.at[t], sibling
        )

    def chip_chunk(t):
        r1[t].wait_recv()
        total = part[t, core].astype(jnp.float32) + got_core[t].astype(jnp.float32)
        sum_core[t] = total.astype(jnp.bfloat16)
        first_chip, first_dev = (x_chip, x_dev) if t % 2 == 0 else (y_chip, y_dev)
        for kind, chip_to in ((1, d_chip), (0, first_chip)):
            r2[t, kind] = send(
                sum_core.at[t, chip_to],
                got_chip.at[t, kind],
                r2_send.at[t, kind],
                r2_recv.at[t, kind],
                first_dev,
            )

    def mid_chunk(t):
        second_chip, second_dev = (y_chip, y_dev) if t % 2 == 0 else (x_chip, x_dev)
        r2[t, 1].wait_recv()
        total = sum_core[t, second_chip].astype(jnp.float32) + got_chip[t, 1].astype(jnp.float32)
        sum_mid[t] = total.astype(jnp.bfloat16)
        r2[t, 2] = send(
            sum_mid.at[t], got_chip.at[t, 2], r2_send.at[t, 2], r2_recv.at[t, 2], second_dev
        )

    def z_chunk(t):
        total = sum_core[t, chip].astype(jnp.float32)
        for kind in (0, 2):
            r2[t, kind].wait_recv()
            total = total + got_chip[t, kind].astype(jnp.float32)
        sum_chip[t] = total.astype(jnp.bfloat16)
        for k in range(1, groups):
            r3[t, k] = send(
                sum_chip.at[t, z_of(k)],
                got_z.at[t, k],
                r3_send.at[t, k],
                r3_recv.at[t, k],
                (me_e, z_of(k)),
            )

    def stream_chunk(t):
        total = sum_chip[t, g].astype(jnp.float32)
        for k in range(1, groups):
            r3[t, k].wait_recv()
            total = total + got_z[t, k].astype(jnp.float32)
        mixture = jnp.concatenate([total[:rows_n], total[rows_n:]], axis=1)
        cols = slice(t * span, (t + 1) * span)
        stream = tokens_ref[:, cols].astype(jnp.float32) + mixture
        stream_ref[:, cols] = stream.astype(jnp.bfloat16)
        stream_all[t, g] = jnp.concatenate(
            [stream[:, :piece], stream[:, piece:]], axis=0
        ).astype(jnp.bfloat16)
        for k in range(1, groups):
            block = stream_all.at[t, g]
            s_copies[t, k] = send(
                block, block, s_send.at[t, k], s_recv.at[t, k], (me_e, z_of(k))
            )

    state = {}

    def guard_chunk(t):
        for k in range(1, groups):
            s_copies[t, k].wait_recv()
        got = stream_all[t].astype(jnp.float32)
        if t == 0:
            for i in (3, 7, 8, 9, 10, 11):
                loads[i].wait()
        for side in range(2):
            rows = got[:, side * rows_n : (side + 1) * rows_n].reshape(group_rows, piece)
            lower = t * span + side * piece
            product = jnp.dot(
                rows.astype(jnp.bfloat16),
                w_guard[lower : lower + piece, :],
                preferred_element_type=jnp.float32,
            )
            square = jnp.sum(rows * rows, axis=-1, keepdims=True)
            if t == 0 and side == 0:
                state["qkv"], state["square"] = product, square
            else:
                state["qkv"] = state["qkv"] + product
                state["square"] = state["square"] + square

    stages = (expert_chunk, chip_chunk, mid_chunk, z_chunk, stream_chunk, guard_chunk)
    for step in range(CHUNKS + len(stages) - 1):
        for late, stage in enumerate(stages):
            if 0 <= step - late < CHUNKS:
                stage(step - late)

    qkv = state["qkv"] * lax.rsqrt(state["square"] / width + EPSILON)
    head = keys.shape[1]
    heads = q_n // head
    window = keys.shape[0] // group_rows
    scale = 1.0 / math.sqrt(head)
    key_new = qkv[:, q_n : q_n + k_n].astype(jnp.bfloat16).astype(jnp.float32)
    value_new = qkv[:, q_n + k_n :].astype(jnp.bfloat16).astype(jnp.float32)
    lengths_n = as_column(lengths_ref[...].astype(jnp.float32)).astype(jnp.int32)
    span_keys = rows_n * window
    outs = []
    for a in range(groups):
        here = slice(a * rows_n, (a + 1) * rows_n)
        query = jnp.concatenate([qkv[here, h * head : (h + 1) * head] for h in range(heads)], axis=0)
        key_own = jnp.concatenate([key_new[here]] * heads, axis=0)
        value_own = jnp.concatenate([value_new[here]] * heads, axis=0)
        allowed_n = jnp.concatenate([lengths_n[here]] * heads, axis=0)
        own_score = jnp.sum(query * key_own, axis=-1, keepdims=True) * scale
        pieces, rest = [], query
        for _ in range(3):
            top = rest.astype(jnp.bfloat16).astype(jnp.float32)
            pieces.append(top)
            rest = rest - top
        product = lax.dot_general(
            jnp.concatenate(pieces, axis=0).astype(jnp.bfloat16),
            keys[a * span_keys : (a + 1) * span_keys, :],
            (((1,), (1,)), ((), ())),
            preferred_element_type=jnp.float32,
        )
        all_rows = heads * rows_n
        scores = (
            product[:all_rows] + product[all_rows : 2 * all_rows] + product[2 * all_rows :]
        ) * scale
        column = lax.broadcasted_iota(jnp.int32, scores.shape, 1)
        row = lax.broadcasted_iota(jnp.int32, (all_rows, 1), 0) % rows_n
        upper = (row + 1) * window
        allowed = (column >= upper - allowed_n) & (column < upper)
        masked = jnp.where(allowed, scores, -jnp.inf)
        highest = jnp.maximum(jnp.max(masked, axis=-1, keepdims=True), own_score)
        weights = jnp.exp(masked - highest)
        own_weight = jnp.exp(own_score - highest)
        denominator = jnp.sum(weights, axis=-1, keepdims=True) + own_weight
        top = weights.astype(jnp.bfloat16).astype(jnp.float32)
        product = jnp.dot(
            jnp.concatenate([top, weights - top], axis=0).astype(jnp.bfloat16),
            values[a * span_keys : (a + 1) * span_keys, :],
            preferred_element_type=jnp.float32,
        )
        attended = product[:all_rows] + product[all_rows:] + own_weight * value_own
        attended = attended / denominator
        outs.append(
            jnp.concatenate(
                [attended[h * rows_n : (h + 1) * rows_n] for h in range(heads)], axis=1
            )
        )
    guard_ref[...] = jnp.concatenate(outs, axis=0).astype(jnp.bfloat16)
    for copy in sends:
        copy.wait_send()


def fused_device(
    tokens,
    expert_ids,
    combine,
    w_gate,
    w_up,
    w_down,
    w_query,
    w_key,
    w_value,
    cache_keys,
    cache_values,
    lengths,
):
    rows_n, width = tokens.shape
    groups = lax.axis_size("gd")
    unit = w_gate.shape[2]
    group_rows, heads_kv, window, head = cache_keys.shape
    total_rows = CORES * CHIPS * groups * rows_n
    piece = width // CHUNKS // 2
    pack = 2 * rows_n
    guard_n = w_query.shape[1] + w_key.shape[1] + w_value.shape[1]
    bf16, f32 = jnp.bfloat16, jnp.float32
    dma = pltpu.SemaphoreType.DMA
    in_vmem = pl.BlockSpec(memory_space=pltpu.VMEM)
    in_hbm = pl.BlockSpec(memory_space=pltpu.HBM)
    return pl.pallas_call(
        functools.partial(fused_kernel, groups),
        out_shape=(
            jax.ShapeDtypeStruct((rows_n, width), bf16),
            jax.ShapeDtypeStruct((group_rows, w_query.shape[1]), bf16),
        ),
        in_specs=[in_hbm] * 12,
        out_specs=(in_vmem, in_vmem),
        scratch_shapes=[
            pltpu.VMEM((rows_n, width), bf16),
            pltpu.VMEM((expert_ids.shape[1], rows_n), jnp.int32),
            pltpu.VMEM((combine.shape[1], rows_n), f32),
            pltpu.VMEM((1, group_rows), jnp.int32),
            pltpu.VMEM((width, 2 * unit), bf16),
            pltpu.VMEM((unit, width), bf16),
            pltpu.VMEM((width, guard_n), bf16),
            pltpu.VMEM((group_rows * window, head), bf16),
            pltpu.VMEM((group_rows * window, head), bf16),
            pltpu.VMEM((CORES, CHIPS, groups, pack, width // 2 + 128), bf16),
            pltpu.VMEM((total_rows, width), bf16),
            pltpu.VMEM((total_rows, 128), f32),
            pltpu.VMEM((total_rows, 2 * unit), f32),
            pltpu.VMEM((total_rows, unit), bf16),
            pltpu.VMEM((CHUNKS, CORES, CHIPS, groups, pack, piece), bf16),
            pltpu.VMEM((CHUNKS, CHIPS, groups, pack, piece), bf16),
            pltpu.VMEM((CHUNKS, CHIPS, groups, pack, piece), bf16),
            pltpu.VMEM((CHUNKS, 3, groups, pack, piece), bf16),
            pltpu.VMEM((CHUNKS, groups, pack, piece), bf16),
            pltpu.VMEM((CHUNKS, groups, pack, piece), bf16),
            pltpu.VMEM((CHUNKS, groups, pack, piece), bf16),
            pltpu.VMEM((CHUNKS, groups, pack, piece), bf16),
            dma((12,)),
            dma((groups,)),
            dma((groups,)),
            dma((groups,)),
            dma((groups,)),
            dma((groups,)),
            dma((groups,)),
            dma((groups,)),
            dma((groups,)),
            dma((4, groups)),
            dma((4, groups)),
            dma((CHUNKS,)),
            dma((CHUNKS,)),
            dma((CHUNKS, 3)),
            dma((CHUNKS, 3)),
            dma((CHUNKS, groups)),
            dma((CHUNKS, groups)),
            dma((CHUNKS, groups)),
            dma((CHUNKS, groups)),
        ],
        compiler_params=pltpu.CompilerParams(
            collective_id=0, has_side_effects=True, vmem_limit_bytes=64000 * 1024
        ),
    )(
        tokens,
        expert_ids.T,
        combine.T,
        lengths.reshape(1, group_rows),
        w_gate,
        w_up,
        w_down,
        w_query,
        w_key,
        w_value,
        cache_keys.reshape(group_rows * heads_kv * window, head),
        cache_values.reshape(group_rows * heads_kv * window, head),
    )


def solution(mesh):
    fused = mesh.shape["ep"] == 8 and mesh.shape["gd"] == 4
    return jax.shard_map(
        fused_device if fused else per_device,
        mesh=mesh,
        in_specs=(
            P(("ep", "gd"), None),
            P(("ep", "gd"), None),
            P(("ep", "gd"), None),
            P("ep", None, "gd"),
            P("ep", None, "gd"),
            P("ep", "gd", None),
            P(None, "gd"),
            P(None, "gd"),
            P(None, "gd"),
            P("ep", "gd", None, None),
            P("ep", "gd", None, None),
            P("ep"),
        ),
        out_specs=(P(("ep", "gd"), None), P("ep", "gd")),
        check_vma=False,
    )
```

```python
import functools
import math

import jax
import jax.numpy as jnp
from jax import lax
from jax.experimental import pallas as pl
from jax.experimental.pallas import tpu as pltpu
from jax.sharding import PartitionSpec as P

EPSILON = 1e-06


def norm_rows(values):
    widened = values.astype(jnp.float32)
    return (
        widened * lax.rsqrt(jnp.mean(widened * widened, axis=-1, keepdims=True) + EPSILON)
    ).astype(jnp.bfloat16)


def slot_numbers(chosen, experts):
    blocks_n, rows_n, picks_n = chosen.shape
    flat_ids = chosen.reshape(blocks_n, rows_n * picks_n)
    onehot = (flat_ids[:, :, None] == jnp.arange(experts, dtype=jnp.int32)[None, None, :]).astype(
        jnp.int32
    )
    before = jnp.cumsum(onehot, axis=1) - onehot
    return jnp.sum(before * onehot, axis=-1).reshape(blocks_n, rows_n, picks_n)


def build_slots(row_blocks, targets, slots_n):
    wanted = jnp.any(
        targets[:, None, :, :] == jnp.arange(slots_n, dtype=jnp.int32)[None, :, None, None], axis=-1
    )
    selector = wanted.astype(jnp.bfloat16)
    return jnp.einsum(
        "bsr,brd->bsd", selector, row_blocks, preferred_element_type=jnp.float32
    ).astype(jnp.bfloat16)


def per_device(
    tokens,
    expert_ids,
    combine,
    w_gate,
    w_up,
    w_down,
    w_query,
    w_key,
    w_value,
    cache_keys,
    cache_values,
    lengths,
):
    rows_n, width = tokens.shape
    picks_n = expert_ids.shape[1]
    experts = lax.axis_size("ep")
    members = lax.axis_size("gd")
    capacity = max(2, 3 * rows_n * picks_n // (2 * experts))
    slots_n = experts * capacity
    normed = norm_rows(tokens)
    own_slot = slot_numbers(expert_ids[None], experts)[0]
    own_dest = expert_ids * capacity + own_slot
    group_normed, group_ids = (
        lax.all_gather(normed, "gd", axis=0, tiled=True),
        lax.all_gather(expert_ids, "gd", axis=0, tiled=True),
    )
    group_ids = group_ids.reshape(members, rows_n, picks_n)
    group_dest = group_ids * capacity + slot_numbers(group_ids, experts)
    outgoing = build_slots(group_normed.reshape(members, rows_n, width), group_dest, slots_n)
    outgoing = outgoing.reshape(members, experts, capacity, width)
    arrived = lax.all_to_all(outgoing, "ep", split_axis=1, concat_axis=1, tiled=True)
    slot_rows = arrived.reshape(-1, width)
    gate_val = jnp.dot(slot_rows, w_gate[0], preferred_element_type=jnp.float32)
    up_val = jnp.dot(slot_rows, w_up[0], preferred_element_type=jnp.float32)
    active = (jax.nn.silu(gate_val) * up_val).astype(jnp.bfloat16)
    partial_out = jnp.dot(active, w_down[0], preferred_element_type=jnp.float32).astype(
        jnp.bfloat16
    )
    summed = lax.psum_scatter(
        lax.optimization_barrier(partial_out).astype(jnp.float32).astype(jnp.bfloat16),
        "gd",
        scatter_dimension=0,
        tiled=True,
    ).astype(jnp.float32)
    returned = lax.all_to_all(
        summed.reshape(experts, capacity, width), "ep", split_axis=0, concat_axis=0, tiled=True
    )
    matches = own_dest[:, :, None] == jnp.arange(slots_n, dtype=jnp.int32)[None, None, :]
    weight_rows = jnp.sum(jnp.where(matches, combine[:, :, None], 0.0), axis=1)
    mixture = jnp.dot(
        weight_rows,
        returned.reshape(slots_n, width),
        precision=lax.Precision.HIGHEST,
        preferred_element_type=jnp.float32,
    )
    stream = (tokens.astype(jnp.float32) + mixture).astype(jnp.bfloat16)
    group_stream = lax.all_gather(stream, "gd", axis=0, tiled=True)
    guard_norm = norm_rows(group_stream)
    queries = jnp.dot(guard_norm, w_query, preferred_element_type=jnp.float32)
    key_new = jnp.dot(guard_norm, w_key, preferred_element_type=jnp.float32).astype(jnp.bfloat16)
    value_new = jnp.dot(guard_norm, w_value, preferred_element_type=jnp.float32).astype(
        jnp.bfloat16
    )
    group_total, heads_kv, window_len, head_size = cache_keys.shape
    heads_per = w_query.shape[1] // (heads_kv * head_size)
    queries = queries.reshape(group_total, heads_kv, heads_per, head_size)
    key_new = key_new.reshape(group_total, heads_kv, head_size)
    value_new = value_new.reshape(group_total, heads_kv, head_size)
    scale_factor = 1.0 / math.sqrt(head_size)
    scores = (
        jnp.einsum(
            "rhgd,rhjd->rhgj",
            queries,
            cache_keys.astype(jnp.float32),
            precision=lax.Precision.HIGHEST,
        )
        * scale_factor
    )
    own_score = (
        jnp.einsum(
            "rhgd,rhd->rhg", queries, key_new.astype(jnp.float32), precision=lax.Precision.HIGHEST
        )
        * scale_factor
    )
    positions = jnp.arange(window_len, dtype=jnp.int32)
    allowed = positions[None, None, None, :] >= (window_len - lengths)[:, None, None, None]
    masked = jnp.where(allowed, scores, -jnp.inf)
    highest = jnp.maximum(jnp.max(masked, axis=-1), own_score)
    weights = jnp.exp(masked - highest[..., None])
    own_weight = jnp.exp(own_score - highest)
    denominator = jnp.sum(weights, axis=-1) + own_weight
    probabilities = weights / denominator[..., None]
    own_prob = own_weight / denominator
    attended = jnp.einsum(
        "rhgj,rhjd->rhgd",
        probabilities,
        cache_values.astype(jnp.float32),
        precision=lax.Precision.HIGHEST,
    )
    attended = attended + own_prob[..., None] * value_new.astype(jnp.float32)[:, :, None, :]
    guard = attended.astype(jnp.bfloat16).reshape(group_total, heads_kv * heads_per * head_size)
    return (stream, guard)


CORES = 2
CHIPS = 4
CHUNKS = 4
MESH = pl.DeviceIdType.MESH


def as_column(line):
    size = line.shape[1]
    across = lax.broadcasted_iota(jnp.int32, (size, size), 1)
    down = lax.broadcasted_iota(jnp.int32, (size, size), 0)
    return jnp.sum(jnp.where(across == down, line, 0.0), axis=1, keepdims=True)


def fused_kernel(
    groups,
    tokens_hbm,
    ids_hbm,
    combine_hbm,
    lengths_hbm,
    gate_hbm,
    up_hbm,
    down_hbm,
    query_hbm,
    key_hbm,
    value_hbm,
    cache_k_hbm,
    cache_v_hbm,
    stream_ref,
    guard_ref,
    tokens_ref,
    ids_ref,
    combine_ref,
    lengths_ref,
    w_in,
    w_out,
    w_guard,
    keys,
    values,
    rows_in,
    rows_all,
    weight_all,
    hidden,
    active,
    part,
    got_core,
    sum_core,
    got_chip,
    sum_mid,
    sum_chip,
    got_z,
    stream_all,
    load_sem,
    z_send,
    z_recv,
    x_send,
    x_recv,
    y_send,
    y_recv,
    d_send,
    d_recv,
    c_send,
    c_recv,
    r1_send,
    r1_recv,
    r2_send,
    r2_recv,
    r3_send,
    r3_recv,
    s_send,
    s_recv,
):
    rows_n, width = tokens_hbm.shape
    half = width // 2
    unit = gate_hbm.shape[2]
    me_e = lax.axis_index("ep")
    g = lax.axis_index("gd")
    core = me_e % CORES
    chip = me_e // CORES
    x, y = chip % 2, chip // 2
    x_chip = y * 2 + (1 - x)
    y_chip = (1 - y) * 2 + x
    d_chip = (1 - y) * 2 + (1 - x)
    sibling = (chip * CORES + (1 - core), g)
    x_dev = (x_chip * CORES + core, g)
    y_dev = (y_chip * CORES + core, g)

    def z_of(step):
        return (g + step) % groups

    loads = []

    def load(src, dst):
        copy = pltpu.make_async_copy(src, dst, load_sem.at[len(loads)])
        copy.start()
        loads.append(copy)

    barrier = pltpu.get_barrier_semaphore()
    peers = [sibling, x_dev, y_dev] + [(me_e, z_of(k)) for k in range(1, groups)]
    for peer in peers:
        pl.semaphore_signal(barrier, inc=1, device_id=peer, device_id_type=MESH)

    load(tokens_hbm, tokens_ref)
    load(ids_hbm, ids_ref)
    load(combine_hbm, combine_ref)
    load(lengths_hbm, lengths_ref)
    load(gate_hbm.at[0], w_in.at[:, 0:unit])
    load(up_hbm.at[0], w_in.at[:, unit : 2 * unit])
    load(down_hbm.at[0], w_out)
    q_n, k_n = query_hbm.shape[1], key_hbm.shape[1]
    load(query_hbm, w_guard.at[:, 0:q_n])
    load(key_hbm, w_guard.at[:, q_n : q_n + k_n])
    load(value_hbm, w_guard.at[:, q_n + k_n : q_n + 2 * k_n])
    load(cache_k_hbm, keys)
    load(cache_v_hbm, values)

    for i in range(3):
        loads[i].wait()
    wide = tokens_ref[...].astype(jnp.float32)
    normed = wide * lax.rsqrt(jnp.mean(wide * wide, axis=-1, keepdims=True) + EPSILON)
    lanes = lax.broadcasted_iota(jnp.int32, (rows_n, 128), 1)
    table = jnp.zeros((rows_n, 128), jnp.float32)
    for k in range(ids_ref.shape[0]):
        named = as_column(ids_ref[k : k + 1, :].astype(jnp.float32)).astype(jnp.int32)
        share_of = as_column(combine_ref[k : k + 1, :])
        table = table + jnp.where(lanes == named, share_of, 0.0)
    table_top = table.astype(jnp.bfloat16).astype(jnp.float32)
    packed = jnp.concatenate([normed[:, :half], normed[:, half:]], axis=0)
    rows_in[core, chip, g, :, 0:half] = packed.astype(jnp.bfloat16)
    rows_in[core, chip, g, :, half : half + 128] = jnp.concatenate(
        [table_top, table - table_top], axis=0
    ).astype(jnp.bfloat16)

    pl.semaphore_wait(barrier, len(peers))

    sends = []

    def send(src, dst, send_sem, recv_sem, device):
        copy = pltpu.make_async_remote_copy(
            src_ref=src,
            dst_ref=dst,
            send_sem=send_sem,
            recv_sem=recv_sem,
            device_id=device,
            device_id_type=MESH,
        )
        copy.start()
        sends.append(copy)
        return copy

    def row_send(chip_of, step, send_sem, recv_sem, device):
        block = rows_in.at[core, chip_of, (g + groups - step) % groups]
        return send(block, block, send_sem, recv_sem, device)

    z_copies, x_copies, y_copies, d_copies, c_copies = {}, {}, {}, {}, {}

    def share(kind, chip_of, step):
        c_copies[kind, step] = row_send(
            chip_of, step, c_send.at[kind, step], c_recv.at[kind, step], sibling
        )

    def spread(step):
        x_copies[step] = row_send(chip, step, x_send.at[step], x_recv.at[step], x_dev)
        y_copies[step] = row_send(chip, step, y_send.at[step], y_recv.at[step], y_dev)
        share(0, chip, step)

    def forward(step):
        x_copies[step].wait_recv()
        if step % 2 == 1:
            d_copies[step] = row_send(x_chip, step, d_send.at[step], d_recv.at[step], y_dev)
        share(1, x_chip, step)
        y_copies[step].wait_recv()
        if step % 2 == 0:
            d_copies[step] = row_send(y_chip, step, d_send.at[step], d_recv.at[step], x_dev)
        share(2, y_chip, step)

    for k in range(1, groups):
        z_copies[k] = row_send(chip, 0, z_send.at[k], z_recv.at[k], (me_e, z_of(k)))
    spread(0)
    for k in range(1, groups):
        z_copies[k].wait_recv()
        spread(k)
        forward(k - 1)
    forward(groups - 1)
    for k in range(groups):
        d_copies[k].wait_recv()
        share(3, d_chip, k)
    for k in range(groups):
        for kind in range(4):
            c_copies[kind, k].wait_recv()

    group_rows = groups * rows_n

    def unpack(block, carry):
        c, h = block // CHIPS, block % CHIPS
        start = pl.multiple_of(block * group_rows, group_rows)
        for side in range(2):
            got = rows_in[c, h, :, :, 0:half].astype(jnp.float32)
            got = got[:, side * rows_n : (side + 1) * rows_n].reshape(group_rows, half)
            rows_all[pl.ds(start, group_rows), side * half : (side + 1) * half] = got.astype(
                jnp.bfloat16
            )
        extra = rows_in[c, h, :, :, half : half + 128].astype(jnp.float32)
        weight_all[pl.ds(start, group_rows), :] = (extra[:, :rows_n] + extra[:, rows_n:]).reshape(
            group_rows, 128
        )
        return carry

    lax.fori_loop(0, CORES * CHIPS, unpack, 0)

    loads[4].wait()
    loads[5].wait()
    tile = 256

    def first(n, carry):
        cols = pl.ds(pl.multiple_of(n * tile, tile), tile)
        hidden[:, cols] = jnp.dot(
            rows_all[...], w_in[:, cols], preferred_element_type=jnp.float32
        )
        return carry

    lax.fori_loop(0, 2 * unit // tile, first, 0)
    table_all = weight_all[...]
    picked = lax.broadcasted_iota(jnp.int32, table_all.shape, 1) == me_e
    row_weight = jnp.sum(jnp.where(picked, table_all, 0.0), axis=-1, keepdims=True)
    gate_val = hidden[:, 0:unit]
    active[...] = (
        gate_val / (1.0 + jnp.exp(-gate_val)) * hidden[:, unit : 2 * unit] * row_weight
    ).astype(jnp.bfloat16)
    loads[6].wait()

    span = width // CHUNKS
    piece = span // 2
    paired = groups // 2
    r1, r2, r3, s_copies = {}, {}, {}, {}

    def expert_chunk(t):
        blocks_n = CORES * CHIPS * groups
        for side in range(2):
            lower = t * span + side * piece
            out = jnp.dot(
                active[...], w_out[:, lower : lower + piece], preferred_element_type=jnp.float32
            ).reshape(CORES, CHIPS, groups, rows_n, piece)
            if side == 0:
                top = out
        part[t] = jnp.concatenate([top, out], axis=3).astype(jnp.bfloat16)
        r1[t] = send(
            part.at[t, 1 - core], got_core.at[t], r1_send.at[t], r1_recv.at[t], sibling
        )

    def chip_chunk(t):
        r1[t].wait_recv()
        total = part[t, core].astype(jnp.float32) + got_core[t].astype(jnp.float32)
        sum_core[t] = total.astype(jnp.bfloat16)
        for kind, chips_to in ((1, (d_chip, d_chip)), (0, (x_chip, y_chip))):
            for side in range(2):
                some = pl.ds(side * paired, paired)
                r2[t, kind, side] = send(
                    sum_core.at[t, chips_to[side], some],
                    got_chip.at[t, kind, some],
                    r2_send.at[t, kind, side],
                    r2_recv.at[t, kind, side],
                    (x_dev, y_dev)[side],
                )

    def mid_chunk(t):
        for side in range(2):
            some = pl.ds(side * paired, paired)
            r2[t, 1, side].wait_recv()
            total = sum_core[t, (y_chip, x_chip)[side], some].astype(jnp.float32)
            total = total + got_chip[t, 1, some].astype(jnp.float32)
            sum_mid[t, some] = total.astype(jnp.bfloat16)
            r2[t, 2, side] = send(
                sum_mid.at[t, some],
                got_chip.at[t, 2, some],
                r2_send.at[t, 2, side],
                r2_recv.at[t, 2, side],
                (y_dev, x_dev)[side],
            )

    def z_chunk(t):
        total = sum_core[t, chip].astype(jnp.float32)
        for kind in (0, 2):
            for side in range(2):
                r2[t, kind, side].wait_recv()
            total = total + got_chip[t, kind].astype(jnp.float32)
        sum_chip[t] = total.astype(jnp.bfloat16)
        for k in range(1, groups):
            r3[t, k] = send(
                sum_chip.at[t, z_of(k)],
                got_z.at[t, k],
                r3_send.at[t, k],
                r3_recv.at[t, k],
                (me_e, z_of(k)),
            )

    def stream_chunk(t):
        total = sum_chip[t, g].astype(jnp.float32)
        for k in range(1, groups):
            r3[t, k].wait_recv()
            total = total + got_z[t, k].astype(jnp.float32)
        mixture = jnp.concatenate([total[:rows_n], total[rows_n:]], axis=1)
        cols = slice(t * span, (t + 1) * span)
        stream = tokens_ref[:, cols].astype(jnp.float32) + mixture
        stream_ref[:, cols] = stream.astype(jnp.bfloat16)
        stream_all[t, g] = jnp.concatenate(
            [stream[:, :piece], stream[:, piece:]], axis=0
        ).astype(jnp.bfloat16)
        for k in range(1, groups):
            block = stream_all.at[t, g]
            s_copies[t, k] = send(
                block, block, s_send.at[t, k], s_recv.at[t, k], (me_e, z_of(k))
            )

    state = {}

    def guard_chunk(t):
        for k in range(1, groups):
            s_copies[t, k].wait_recv()
        got = stream_all[t].astype(jnp.float32)
        if t == 0:
            for i in (3, 7, 8, 9, 10, 11):
                loads[i].wait()
        for side in range(2):
            rows = got[:, side * rows_n : (side + 1) * rows_n].reshape(group_rows, piece)
            lower = t * span + side * piece
            product = jnp.dot(
                rows.astype(jnp.bfloat16),
                w_guard[lower : lower + piece, :],
                preferred_element_type=jnp.float32,
            )
            square = jnp.sum(rows * rows, axis=-1, keepdims=True)
            if t == 0 and side == 0:
                state["qkv"], state["square"] = product, square
            else:
                state["qkv"] = state["qkv"] + product
                state["square"] = state["square"] + square

    stages = (expert_chunk, chip_chunk, mid_chunk, z_chunk, stream_chunk, guard_chunk)
    for step in range(CHUNKS + len(stages) - 1):
        for late, stage in enumerate(stages):
            if 0 <= step - late < CHUNKS:
                stage(step - late)

    qkv = state["qkv"] * lax.rsqrt(state["square"] / width + EPSILON)
    head = keys.shape[1]
    heads = q_n // head
    window = keys.shape[0] // group_rows
    scale = 1.0 / math.sqrt(head)
    key_new = qkv[:, q_n : q_n + k_n].astype(jnp.bfloat16).astype(jnp.float32)
    value_new = qkv[:, q_n + k_n :].astype(jnp.bfloat16).astype(jnp.float32)
    lengths_n = as_column(lengths_ref[...].astype(jnp.float32)).astype(jnp.int32)
    span_keys = rows_n * window
    outs = []
    for a in range(groups):
        here = slice(a * rows_n, (a + 1) * rows_n)
        query = jnp.concatenate([qkv[here, h * head : (h + 1) * head] for h in range(heads)], axis=0)
        key_own = jnp.concatenate([key_new[here]] * heads, axis=0)
        value_own = jnp.concatenate([value_new[here]] * heads, axis=0)
        allowed_n = jnp.concatenate([lengths_n[here]] * heads, axis=0)
        own_score = jnp.sum(query * key_own, axis=-1, keepdims=True) * scale
        pieces, rest = [], query
        for _ in range(3):
            top = rest.astype(jnp.bfloat16).astype(jnp.float32)
            pieces.append(top)
            rest = rest - top
        product = lax.dot_general(
            jnp.concatenate(pieces, axis=0).astype(jnp.bfloat16),
            keys[a * span_keys : (a + 1) * span_keys, :],
            (((1,), (1,)), ((), ())),
            preferred_element_type=jnp.float32,
        )
        all_rows = heads * rows_n
        scores = (
            product[:all_rows] + product[all_rows : 2 * all_rows] + product[2 * all_rows :]
        ) * scale
        column = lax.broadcasted_iota(jnp.int32, scores.shape, 1)
        row = lax.broadcasted_iota(jnp.int32, (all_rows, 1), 0) % rows_n
        upper = (row + 1) * window
        allowed = (column >= upper - allowed_n) & (column < upper)
        masked = jnp.where(allowed, scores, -jnp.inf)
        highest = jnp.maximum(jnp.max(masked, axis=-1, keepdims=True), own_score)
        weights = jnp.exp(masked - highest)
        own_weight = jnp.exp(own_score - highest)
        denominator = jnp.sum(weights, axis=-1, keepdims=True) + own_weight
        top = weights.astype(jnp.bfloat16).astype(jnp.float32)
        product = jnp.dot(
            jnp.concatenate([top, weights - top], axis=0).astype(jnp.bfloat16),
            values[a * span_keys : (a + 1) * span_keys, :],
            preferred_element_type=jnp.float32,
        )
        attended = product[:all_rows] + product[all_rows:] + own_weight * value_own
        attended = attended / denominator
        outs.append(
            jnp.concatenate(
                [attended[h * rows_n : (h + 1) * rows_n] for h in range(heads)], axis=1
            )
        )
    guard_ref[...] = jnp.concatenate(outs, axis=0).astype(jnp.bfloat16)
    for copy in sends:
        copy.wait_send()


def fused_device(
    tokens,
    expert_ids,
    combine,
    w_gate,
    w_up,
    w_down,
    w_query,
    w_key,
    w_value,
    cache_keys,
    cache_values,
    lengths,
):
    rows_n, width = tokens.shape
    groups = lax.axis_size("gd")
    unit = w_gate.shape[2]
    group_rows, heads_kv, window, head = cache_keys.shape
    total_rows = CORES * CHIPS * groups * rows_n
    piece = width // CHUNKS // 2
    pack = 2 * rows_n
    guard_n = w_query.shape[1] + w_key.shape[1] + w_value.shape[1]
    bf16, f32 = jnp.bfloat16, jnp.float32
    dma = pltpu.SemaphoreType.DMA
    in_vmem = pl.BlockSpec(memory_space=pltpu.VMEM)
    in_hbm = pl.BlockSpec(memory_space=pltpu.HBM)
    return pl.pallas_call(
        functools.partial(fused_kernel, groups),
        out_shape=(
            jax.ShapeDtypeStruct((rows_n, width), bf16),
            jax.ShapeDtypeStruct((group_rows, w_query.shape[1]), bf16),
        ),
        in_specs=[in_hbm] * 12,
        out_specs=(in_vmem, in_vmem),
        scratch_shapes=[
            pltpu.VMEM((rows_n, width), bf16),
            pltpu.VMEM((expert_ids.shape[1], rows_n), jnp.int32),
            pltpu.VMEM((combine.shape[1], rows_n), f32),
            pltpu.VMEM((1, group_rows), jnp.int32),
            pltpu.VMEM((width, 2 * unit), bf16),
            pltpu.VMEM((unit, width), bf16),
            pltpu.VMEM((width, guard_n), bf16),
            pltpu.VMEM((group_rows * window, head), bf16),
            pltpu.VMEM((group_rows * window, head), bf16),
            pltpu.VMEM((CORES, CHIPS, groups, pack, width // 2 + 128), bf16),
            pltpu.VMEM((total_rows, width), bf16),
            pltpu.VMEM((total_rows, 128), f32),
            pltpu.VMEM((total_rows, 2 * unit), f32),
            pltpu.VMEM((total_rows, unit), bf16),
            pltpu.VMEM((CHUNKS, CORES, CHIPS, groups, pack, piece), bf16),
            pltpu.VMEM((CHUNKS, CHIPS, groups, pack, piece), bf16),
            pltpu.VMEM((CHUNKS, CHIPS, groups, pack, piece), bf16),
            pltpu.VMEM((CHUNKS, 3, groups, pack, piece), bf16),
            pltpu.VMEM((CHUNKS, groups, pack, piece), bf16),
            pltpu.VMEM((CHUNKS, groups, pack, piece), bf16),
            pltpu.VMEM((CHUNKS, groups, pack, piece), bf16),
            pltpu.VMEM((CHUNKS, groups, pack, piece), bf16),
            dma((12,)),
            dma((groups,)),
            dma((groups,)),
            dma((groups,)),
            dma((groups,)),
            dma((groups,)),
            dma((groups,)),
            dma((groups,)),
            dma((groups,)),
            dma((4, groups)),
            dma((4, groups)),
            dma((CHUNKS,)),
            dma((CHUNKS,)),
            dma((CHUNKS, 3, 2)),
            dma((CHUNKS, 3, 2)),
            dma((CHUNKS, groups)),
            dma((CHUNKS, groups)),
            dma((CHUNKS, groups)),
            dma((CHUNKS, groups)),
        ],
        compiler_params=pltpu.CompilerParams(
            collective_id=0, has_side_effects=True, vmem_limit_bytes=64000 * 1024
        ),
    )(
        tokens,
        expert_ids.T,
        combine.T,
        lengths.reshape(1, group_rows),
        w_gate,
        w_up,
        w_down,
        w_query,
        w_key,
        w_value,
        cache_keys.reshape(group_rows * heads_kv * window, head),
        cache_values.reshape(group_rows * heads_kv * window, head),
    )


def solution(mesh):
    fused = mesh.shape["ep"] == 8 and mesh.shape["gd"] == 4
    return jax.shard_map(
        fused_device if fused else per_device,
        mesh=mesh,
        in_specs=(
            P(("ep", "gd"), None),
            P(("ep", "gd"), None),
            P(("ep", "gd"), None),
            P("ep", None, "gd"),
            P("ep", None, "gd"),
            P("ep", "gd", None),
            P(None, "gd"),
            P(None, "gd"),
            P(None, "gd"),
            P("ep", "gd", None, None),
            P("ep", "gd", None, None),
            P("ep"),
        ),
        out_specs=(P(("ep", "gd"), None), P("ep", "gd")),
        check_vma=False,
    )
```

```python
import functools
import math

import jax
import jax.numpy as jnp
from jax import lax
from jax.experimental import pallas as pl
from jax.experimental.pallas import tpu as pltpu
from jax.sharding import PartitionSpec as P

EPSILON = 1e-06


def norm_rows(values):
    widened = values.astype(jnp.float32)
    return (
        widened * lax.rsqrt(jnp.mean(widened * widened, axis=-1, keepdims=True) + EPSILON)
    ).astype(jnp.bfloat16)


def slot_numbers(chosen, experts):
    blocks_n, rows_n, picks_n = chosen.shape
    flat_ids = chosen.reshape(blocks_n, rows_n * picks_n)
    onehot = (flat_ids[:, :, None] == jnp.arange(experts, dtype=jnp.int32)[None, None, :]).astype(
        jnp.int32
    )
    before = jnp.cumsum(onehot, axis=1) - onehot
    return jnp.sum(before * onehot, axis=-1).reshape(blocks_n, rows_n, picks_n)


def build_slots(row_blocks, targets, slots_n):
    wanted = jnp.any(
        targets[:, None, :, :] == jnp.arange(slots_n, dtype=jnp.int32)[None, :, None, None], axis=-1
    )
    selector = wanted.astype(jnp.bfloat16)
    return jnp.einsum(
        "bsr,brd->bsd", selector, row_blocks, preferred_element_type=jnp.float32
    ).astype(jnp.bfloat16)


def per_device(
    tokens,
    expert_ids,
    combine,
    w_gate,
    w_up,
    w_down,
    w_query,
    w_key,
    w_value,
    cache_keys,
    cache_values,
    lengths,
):
    rows_n, width = tokens.shape
    picks_n = expert_ids.shape[1]
    experts = lax.axis_size("ep")
    members = lax.axis_size("gd")
    capacity = max(2, 3 * rows_n * picks_n // (2 * experts))
    slots_n = experts * capacity
    normed = norm_rows(tokens)
    own_slot = slot_numbers(expert_ids[None], experts)[0]
    own_dest = expert_ids * capacity + own_slot
    group_normed, group_ids = (
        lax.all_gather(normed, "gd", axis=0, tiled=True),
        lax.all_gather(expert_ids, "gd", axis=0, tiled=True),
    )
    group_ids = group_ids.reshape(members, rows_n, picks_n)
    group_dest = group_ids * capacity + slot_numbers(group_ids, experts)
    outgoing = build_slots(group_normed.reshape(members, rows_n, width), group_dest, slots_n)
    outgoing = outgoing.reshape(members, experts, capacity, width)
    arrived = lax.all_to_all(outgoing, "ep", split_axis=1, concat_axis=1, tiled=True)
    slot_rows = arrived.reshape(-1, width)
    gate_val = jnp.dot(slot_rows, w_gate[0], preferred_element_type=jnp.float32)
    up_val = jnp.dot(slot_rows, w_up[0], preferred_element_type=jnp.float32)
    active = (jax.nn.silu(gate_val) * up_val).astype(jnp.bfloat16)
    partial_out = jnp.dot(active, w_down[0], preferred_element_type=jnp.float32).astype(
        jnp.bfloat16
    )
    summed = lax.psum_scatter(
        lax.optimization_barrier(partial_out).astype(jnp.float32).astype(jnp.bfloat16),
        "gd",
        scatter_dimension=0,
        tiled=True,
    ).astype(jnp.float32)
    returned = lax.all_to_all(
        summed.reshape(experts, capacity, width), "ep", split_axis=0, concat_axis=0, tiled=True
    )
    matches = own_dest[:, :, None] == jnp.arange(slots_n, dtype=jnp.int32)[None, None, :]
    weight_rows = jnp.sum(jnp.where(matches, combine[:, :, None], 0.0), axis=1)
    mixture = jnp.dot(
        weight_rows,
        returned.reshape(slots_n, width),
        precision=lax.Precision.HIGHEST,
        preferred_element_type=jnp.float32,
    )
    stream = (tokens.astype(jnp.float32) + mixture).astype(jnp.bfloat16)
    group_stream = lax.all_gather(stream, "gd", axis=0, tiled=True)
    guard_norm = norm_rows(group_stream)
    queries = jnp.dot(guard_norm, w_query, preferred_element_type=jnp.float32)
    key_new = jnp.dot(guard_norm, w_key, preferred_element_type=jnp.float32).astype(jnp.bfloat16)
    value_new = jnp.dot(guard_norm, w_value, preferred_element_type=jnp.float32).astype(
        jnp.bfloat16
    )
    group_total, heads_kv, window_len, head_size = cache_keys.shape
    heads_per = w_query.shape[1] // (heads_kv * head_size)
    queries = queries.reshape(group_total, heads_kv, heads_per, head_size)
    key_new = key_new.reshape(group_total, heads_kv, head_size)
    value_new = value_new.reshape(group_total, heads_kv, head_size)
    scale_factor = 1.0 / math.sqrt(head_size)
    scores = (
        jnp.einsum(
            "rhgd,rhjd->rhgj",
            queries,
            cache_keys.astype(jnp.float32),
            precision=lax.Precision.HIGHEST,
        )
        * scale_factor
    )
    own_score = (
        jnp.einsum(
            "rhgd,rhd->rhg", queries, key_new.astype(jnp.float32), precision=lax.Precision.HIGHEST
        )
        * scale_factor
    )
    positions = jnp.arange(window_len, dtype=jnp.int32)
    allowed = positions[None, None, None, :] >= (window_len - lengths)[:, None, None, None]
    masked = jnp.where(allowed, scores, -jnp.inf)
    highest = jnp.maximum(jnp.max(masked, axis=-1), own_score)
    weights = jnp.exp(masked - highest[..., None])
    own_weight = jnp.exp(own_score - highest)
    denominator = jnp.sum(weights, axis=-1) + own_weight
    probabilities = weights / denominator[..., None]
    own_prob = own_weight / denominator
    attended = jnp.einsum(
        "rhgj,rhjd->rhgd",
        probabilities,
        cache_values.astype(jnp.float32),
        precision=lax.Precision.HIGHEST,
    )
    attended = attended + own_prob[..., None] * value_new.astype(jnp.float32)[:, :, None, :]
    guard = attended.astype(jnp.bfloat16).reshape(group_total, heads_kv * heads_per * head_size)
    return (stream, guard)


CORES = 2
CHIPS = 4
CHUNKS = 4
MESH = pl.DeviceIdType.MESH


def as_column(line):
    size = line.shape[1]
    across = lax.broadcasted_iota(jnp.int32, (size, size), 1)
    down = lax.broadcasted_iota(jnp.int32, (size, size), 0)
    return jnp.sum(jnp.where(across == down, line, 0.0), axis=1, keepdims=True)


def fused_kernel(
    groups,
    tokens_hbm,
    ids_hbm,
    combine_hbm,
    lengths_hbm,
    gate_hbm,
    up_hbm,
    down_hbm,
    query_hbm,
    key_hbm,
    value_hbm,
    cache_k_hbm,
    cache_v_hbm,
    stream_ref,
    guard_ref,
    tokens_ref,
    ids_ref,
    combine_ref,
    lengths_ref,
    w_in,
    w_out,
    w_guard,
    keys,
    values,
    rows_in,
    rows_all,
    weight_all,
    hidden,
    active,
    part,
    got_core,
    sum_core,
    got_chip,
    sum_mid,
    sum_chip,
    got_z,
    stream_all,
    load_sem,
    z_send,
    z_recv,
    x_send,
    x_recv,
    y_send,
    y_recv,
    d_send,
    d_recv,
    c_send,
    c_recv,
    r1_send,
    r1_recv,
    r2_send,
    r2_recv,
    r3_send,
    r3_recv,
    s_send,
    s_recv,
):
    rows_n, width = tokens_hbm.shape
    half = width // 2
    unit = gate_hbm.shape[2]
    me_e = lax.axis_index("ep")
    g = lax.axis_index("gd")
    core = me_e % CORES
    chip = me_e // CORES
    x, y = chip % 2, chip // 2
    x_chip = y * 2 + (1 - x)
    y_chip = (1 - y) * 2 + x
    d_chip = (1 - y) * 2 + (1 - x)
    sibling = (chip * CORES + (1 - core), g)
    x_dev = (x_chip * CORES + core, g)
    y_dev = (y_chip * CORES + core, g)

    def z_of(step):
        return (g + step) % groups

    loads = []

    def load(src, dst):
        copy = pltpu.make_async_copy(src, dst, load_sem.at[len(loads)])
        copy.start()
        loads.append(copy)

    barrier = pltpu.get_barrier_semaphore()
    peers = [sibling, x_dev, y_dev] + [(me_e, z_of(k)) for k in range(1, groups)]
    for peer in peers:
        pl.semaphore_signal(barrier, inc=1, device_id=peer, device_id_type=MESH)

    load(tokens_hbm, tokens_ref)
    load(ids_hbm, ids_ref)
    load(combine_hbm, combine_ref)
    load(lengths_hbm, lengths_ref)
    load(gate_hbm.at[0], w_in.at[:, 0:unit])
    load(up_hbm.at[0], w_in.at[:, unit : 2 * unit])
    load(down_hbm.at[0], w_out)
    q_n, k_n = query_hbm.shape[1], key_hbm.shape[1]
    load(query_hbm, w_guard.at[:, 0:q_n])
    load(key_hbm, w_guard.at[:, q_n : q_n + k_n])
    load(value_hbm, w_guard.at[:, q_n + k_n : q_n + 2 * k_n])
    load(cache_k_hbm, keys)
    load(cache_v_hbm, values)

    for i in range(3):
        loads[i].wait()
    wide = tokens_ref[...].astype(jnp.float32)
    normed = wide * lax.rsqrt(jnp.mean(wide * wide, axis=-1, keepdims=True) + EPSILON)
    lanes = lax.broadcasted_iota(jnp.int32, (rows_n, 128), 1)
    table = jnp.zeros((rows_n, 128), jnp.float32)
    for k in range(ids_ref.shape[0]):
        named = as_column(ids_ref[k : k + 1, :].astype(jnp.float32)).astype(jnp.int32)
        share_of = as_column(combine_ref[k : k + 1, :])
        table = table + jnp.where(lanes == named, share_of, 0.0)
    table_top = table.astype(jnp.bfloat16).astype(jnp.float32)
    packed = jnp.concatenate([normed[:, :half], normed[:, half:]], axis=0)
    rows_in[core, chip, g, :, 0:half] = packed.astype(jnp.bfloat16)
    rows_in[core, chip, g, :, half : half + 128] = jnp.concatenate(
        [table_top, table - table_top], axis=0
    ).astype(jnp.bfloat16)

    pl.semaphore_wait(barrier, len(peers))

    sends = []

    def send(src, dst, send_sem, recv_sem, device):
        copy = pltpu.make_async_remote_copy(
            src_ref=src,
            dst_ref=dst,
            send_sem=send_sem,
            recv_sem=recv_sem,
            device_id=device,
            device_id_type=MESH,
        )
        copy.start()
        sends.append(copy)
        return copy

    def row_send(chip_of, step, send_sem, recv_sem, device):
        block = rows_in.at[core, chip_of, (g + groups - step) % groups]
        return send(block, block, send_sem, recv_sem, device)

    z_copies, x_copies, y_copies, d_copies, c_copies = {}, {}, {}, {}, {}

    def share(kind, chip_of, step):
        c_copies[kind, step] = row_send(
            chip_of, step, c_send.at[kind, step], c_recv.at[kind, step], sibling
        )

    def spread(step):
        x_copies[step] = row_send(chip, step, x_send.at[step], x_recv.at[step], x_dev)
        y_copies[step] = row_send(chip, step, y_send.at[step], y_recv.at[step], y_dev)
        share(0, chip, step)

    def forward(step):
        x_copies[step].wait_recv()
        if step % 2 == 1:
            d_copies[step] = row_send(x_chip, step, d_send.at[step], d_recv.at[step], y_dev)
        share(1, x_chip, step)
        y_copies[step].wait_recv()
        if step % 2 == 0:
            d_copies[step] = row_send(y_chip, step, d_send.at[step], d_recv.at[step], x_dev)
        share(2, y_chip, step)

    for k in range(1, groups):
        z_copies[k] = row_send(chip, 0, z_send.at[k], z_recv.at[k], (me_e, z_of(k)))
    spread(0)
    for k in range(1, groups):
        z_copies[k].wait_recv()
        spread(k)
        forward(k - 1)
    forward(groups - 1)
    group_rows = groups * rows_n
    core_rows = CHIPS * group_rows
    tile = 256

    def unpack(c, h):
        start = pl.multiple_of((c * CHIPS + h) * group_rows, group_rows)
        for side in range(2):
            got = rows_in[c, h, :, :, 0:half].astype(jnp.float32)
            got = got[:, side * rows_n : (side + 1) * rows_n].reshape(group_rows, half)
            rows_all[pl.ds(start, group_rows), side * half : (side + 1) * half] = got.astype(
                jnp.bfloat16
            )
        extra = rows_in[c, h, :, :, half : half + 128].astype(jnp.float32)
        weight_all[pl.ds(start, group_rows), :] = (extra[:, :rows_n] + extra[:, rows_n:]).reshape(
            group_rows, 128
        )

    def first_layer(c):
        some = pl.ds(pl.multiple_of(c * core_rows, core_rows), core_rows)

        def first(n, carry):
            cols = pl.ds(pl.multiple_of(n * tile, tile), tile)
            hidden[some, cols] = jnp.dot(
                rows_all[some, :], w_in[:, cols], preferred_element_type=jnp.float32
            )
            return carry

        lax.fori_loop(0, 2 * unit // tile, first, 0)
        table_all = weight_all[some, :]
        picked = lax.broadcasted_iota(jnp.int32, table_all.shape, 1) == me_e
        row_weight = jnp.sum(jnp.where(picked, table_all, 0.0), axis=-1, keepdims=True)
        gate_val = hidden[some, 0:unit]
        active[some, :] = (
            gate_val / (1.0 + jnp.exp(-gate_val)) * hidden[some, unit : 2 * unit] * row_weight
        ).astype(jnp.bfloat16)

    unpack(core, chip)
    unpack(core, x_chip)
    unpack(core, y_chip)
    for k in range(groups):
        d_copies[k].wait_recv()
        share(3, d_chip, k)
    unpack(core, d_chip)
    loads[4].wait()
    loads[5].wait()
    first_layer(core)
    for kind, chip_of in enumerate((chip, x_chip, y_chip, d_chip)):
        for k in range(groups):
            c_copies[kind, k].wait_recv()
        unpack(1 - core, chip_of)
    first_layer(1 - core)
    loads[6].wait()

    span = width // CHUNKS
    piece = span // 2
    paired = groups // 2
    r1, r2, r3, s_copies = {}, {}, {}, {}

    def expert_half(t, c):
        some = pl.ds(pl.multiple_of(c * core_rows, core_rows), core_rows)
        outs = []
        for side in range(2):
            lower = t * span + side * piece
            outs.append(
                jnp.dot(
                    active[some, :],
                    w_out[:, lower : lower + piece],
                    preferred_element_type=jnp.float32,
                ).reshape(CHIPS, groups, rows_n, piece)
            )
        part[t, c] = jnp.concatenate(outs, axis=2).astype(jnp.bfloat16)

    def expert_chunk(t):
        expert_half(t, 1 - core)
        r1[t] = send(
            part.at[t, 1 - core], got_core.at[t], r1_send.at[t], r1_recv.at[t], sibling
        )
        expert_half(t, core)

    def chip_chunk(t):
        r1[t].wait_recv()
        total = part[t, core].astype(jnp.float32) + got_core[t].astype(jnp.float32)
        sum_core[t] = total.astype(jnp.bfloat16)
        for kind, chips_to in ((1, (d_chip, d_chip)), (0, (x_chip, y_chip))):
            for side in range(2):
                some = pl.ds(side * paired, paired)
                r2[t, kind, side] = send(
                    sum_core.at[t, chips_to[side], some],
                    got_chip.at[t, kind, some],
                    r2_send.at[t, kind, side],
                    r2_recv.at[t, kind, side],
                    (x_dev, y_dev)[side],
                )

    def mid_chunk(t):
        for side in range(2):
            some = pl.ds(side * paired, paired)
            r2[t, 1, side].wait_recv()
            total = sum_core[t, (y_chip, x_chip)[side], some].astype(jnp.float32)
            total = total + got_chip[t, 1, some].astype(jnp.float32)
            sum_mid[t, some] = total.astype(jnp.bfloat16)
            r2[t, 2, side] = send(
                sum_mid.at[t, some],
                got_chip.at[t, 2, some],
                r2_send.at[t, 2, side],
                r2_recv.at[t, 2, side],
                (y_dev, x_dev)[side],
            )

    def z_chunk(t):
        total = sum_core[t, chip].astype(jnp.float32)
        for kind in (0, 2):
            for side in range(2):
                r2[t, kind, side].wait_recv()
            total = total + got_chip[t, kind].astype(jnp.float32)
        sum_chip[t] = total.astype(jnp.bfloat16)
        for k in range(1, groups):
            r3[t, k] = send(
                sum_chip.at[t, z_of(k)],
                got_z.at[t, k],
                r3_send.at[t, k],
                r3_recv.at[t, k],
                (me_e, z_of(k)),
            )

    def stream_chunk(t):
        total = sum_chip[t, g].astype(jnp.float32)
        for k in range(1, groups):
            r3[t, k].wait_recv()
            total = total + got_z[t, k].astype(jnp.float32)
        mixture = jnp.concatenate([total[:rows_n], total[rows_n:]], axis=1)
        cols = slice(t * span, (t + 1) * span)
        stream = tokens_ref[:, cols].astype(jnp.float32) + mixture
        stream_ref[:, cols] = stream.astype(jnp.bfloat16)
        stream_all[t, g] = jnp.concatenate(
            [stream[:, :piece], stream[:, piece:]], axis=0
        ).astype(jnp.bfloat16)
        for k in range(1, groups):
            block = stream_all.at[t, g]
            s_copies[t, k] = send(
                block, block, s_send.at[t, k], s_recv.at[t, k], (me_e, z_of(k))
            )

    state = {}

    def guard_chunk(t):
        for k in range(1, groups):
            s_copies[t, k].wait_recv()
        got = stream_all[t].astype(jnp.float32)
        if t == 0:
            for i in (3, 7, 8, 9, 10, 11):
                loads[i].wait()
        for side in range(2):
            rows = got[:, side * rows_n : (side + 1) * rows_n].reshape(group_rows, piece)
            lower = t * span + side * piece
            product = jnp.dot(
                rows.astype(jnp.bfloat16),
                w_guard[lower : lower + piece, :],
                preferred_element_type=jnp.float32,
            )
            square = jnp.sum(rows * rows, axis=-1, keepdims=True)
            if t == 0 and side == 0:
                state["qkv"], state["square"] = product, square
            else:
                state["qkv"] = state["qkv"] + product
                state["square"] = state["square"] + square

    stages = (expert_chunk, chip_chunk, mid_chunk, z_chunk, stream_chunk, guard_chunk)
    for step in range(CHUNKS + len(stages) - 1):
        for late, stage in enumerate(stages):
            if 0 <= step - late < CHUNKS:
                stage(step - late)

    qkv = state["qkv"] * lax.rsqrt(state["square"] / width + EPSILON)
    head = keys.shape[1]
    heads = q_n // head
    window = keys.shape[0] // group_rows
    scale = 1.0 / math.sqrt(head)
    key_new = qkv[:, q_n : q_n + k_n].astype(jnp.bfloat16).astype(jnp.float32)
    value_new = qkv[:, q_n + k_n :].astype(jnp.bfloat16).astype(jnp.float32)
    lengths_n = as_column(lengths_ref[...].astype(jnp.float32)).astype(jnp.int32)
    span_keys = rows_n * window
    outs = []
    for a in range(groups):
        here = slice(a * rows_n, (a + 1) * rows_n)
        query = jnp.concatenate([qkv[here, h * head : (h + 1) * head] for h in range(heads)], axis=0)
        key_own = jnp.concatenate([key_new[here]] * heads, axis=0)
        value_own = jnp.concatenate([value_new[here]] * heads, axis=0)
        allowed_n = jnp.concatenate([lengths_n[here]] * heads, axis=0)
        own_score = jnp.sum(query * key_own, axis=-1, keepdims=True) * scale
        pieces, rest = [], query
        for _ in range(3):
            top = rest.astype(jnp.bfloat16).astype(jnp.float32)
            pieces.append(top)
            rest = rest - top
        product = lax.dot_general(
            jnp.concatenate(pieces, axis=0).astype(jnp.bfloat16),
            keys[a * span_keys : (a + 1) * span_keys, :],
            (((1,), (1,)), ((), ())),
            preferred_element_type=jnp.float32,
        )
        all_rows = heads * rows_n
        scores = (
            product[:all_rows] + product[all_rows : 2 * all_rows] + product[2 * all_rows :]
        ) * scale
        column = lax.broadcasted_iota(jnp.int32, scores.shape, 1)
        row = lax.broadcasted_iota(jnp.int32, (all_rows, 1), 0) % rows_n
        upper = (row + 1) * window
        allowed = (column >= upper - allowed_n) & (column < upper)
        masked = jnp.where(allowed, scores, -jnp.inf)
        highest = jnp.maximum(jnp.max(masked, axis=-1, keepdims=True), own_score)
        weights = jnp.exp(masked - highest)
        own_weight = jnp.exp(own_score - highest)
        denominator = jnp.sum(weights, axis=-1, keepdims=True) + own_weight
        top = weights.astype(jnp.bfloat16).astype(jnp.float32)
        product = jnp.dot(
            jnp.concatenate([top, weights - top], axis=0).astype(jnp.bfloat16),
            values[a * span_keys : (a + 1) * span_keys, :],
            preferred_element_type=jnp.float32,
        )
        attended = product[:all_rows] + product[all_rows:] + own_weight * value_own
        attended = attended / denominator
        outs.append(
            jnp.concatenate(
                [attended[h * rows_n : (h + 1) * rows_n] for h in range(heads)], axis=1
            )
        )
    guard_ref[...] = jnp.concatenate(outs, axis=0).astype(jnp.bfloat16)
    for copy in sends:
        copy.wait_send()


def fused_device(
    tokens,
    expert_ids,
    combine,
    w_gate,
    w_up,
    w_down,
    w_query,
    w_key,
    w_value,
    cache_keys,
    cache_values,
    lengths,
):
    rows_n, width = tokens.shape
    groups = lax.axis_size("gd")
    unit = w_gate.shape[2]
    group_rows, heads_kv, window, head = cache_keys.shape
    total_rows = CORES * CHIPS * groups * rows_n
    piece = width // CHUNKS // 2
    pack = 2 * rows_n
    guard_n = w_query.shape[1] + w_key.shape[1] + w_value.shape[1]
    bf16, f32 = jnp.bfloat16, jnp.float32
    dma = pltpu.SemaphoreType.DMA
    in_vmem = pl.BlockSpec(memory_space=pltpu.VMEM)
    in_hbm = pl.BlockSpec(memory_space=pltpu.HBM)
    return pl.pallas_call(
        functools.partial(fused_kernel, groups),
        out_shape=(
            jax.ShapeDtypeStruct((rows_n, width), bf16),
            jax.ShapeDtypeStruct((group_rows, w_query.shape[1]), bf16),
        ),
        in_specs=[in_hbm] * 12,
        out_specs=(in_vmem, in_vmem),
        scratch_shapes=[
            pltpu.VMEM((rows_n, width), bf16),
            pltpu.VMEM((expert_ids.shape[1], rows_n), jnp.int32),
            pltpu.VMEM((combine.shape[1], rows_n), f32),
            pltpu.VMEM((1, group_rows), jnp.int32),
            pltpu.VMEM((width, 2 * unit), bf16),
            pltpu.VMEM((unit, width), bf16),
            pltpu.VMEM((width, guard_n), bf16),
            pltpu.VMEM((group_rows * window, head), bf16),
            pltpu.VMEM((group_rows * window, head), bf16),
            pltpu.VMEM((CORES, CHIPS, groups, pack, width // 2 + 128), bf16),
            pltpu.VMEM((total_rows, width), bf16),
            pltpu.VMEM((total_rows, 128), f32),
            pltpu.VMEM((total_rows, 2 * unit), f32),
            pltpu.VMEM((total_rows, unit), bf16),
            pltpu.VMEM((CHUNKS, CORES, CHIPS, groups, pack, piece), bf16),
            pltpu.VMEM((CHUNKS, CHIPS, groups, pack, piece), bf16),
            pltpu.VMEM((CHUNKS, CHIPS, groups, pack, piece), bf16),
            pltpu.VMEM((CHUNKS, 3, groups, pack, piece), bf16),
            pltpu.VMEM((CHUNKS, groups, pack, piece), bf16),
            pltpu.VMEM((CHUNKS, groups, pack, piece), bf16),
            pltpu.VMEM((CHUNKS, groups, pack, piece), bf16),
            pltpu.VMEM((CHUNKS, groups, pack, piece), bf16),
            dma((12,)),
            dma((groups,)),
            dma((groups,)),
            dma((groups,)),
            dma((groups,)),
            dma((groups,)),
            dma((groups,)),
            dma((groups,)),
            dma((groups,)),
            dma((4, groups)),
            dma((4, groups)),
            dma((CHUNKS,)),
            dma((CHUNKS,)),
            dma((CHUNKS, 3, 2)),
            dma((CHUNKS, 3, 2)),
            dma((CHUNKS, groups)),
            dma((CHUNKS, groups)),
            dma((CHUNKS, groups)),
            dma((CHUNKS, groups)),
        ],
        compiler_params=pltpu.CompilerParams(
            collective_id=0, has_side_effects=True, vmem_limit_bytes=64000 * 1024
        ),
    )(
        tokens,
        expert_ids.T,
        combine.T,
        lengths.reshape(1, group_rows),
        w_gate,
        w_up,
        w_down,
        w_query,
        w_key,
        w_value,
        cache_keys.reshape(group_rows * heads_kv * window, head),
        cache_values.reshape(group_rows * heads_kv * window, head),
    )


def solution(mesh):
    fused = mesh.shape["ep"] == 8 and mesh.shape["gd"] == 4
    return jax.shard_map(
        fused_device if fused else per_device,
        mesh=mesh,
        in_specs=(
            P(("ep", "gd"), None),
            P(("ep", "gd"), None),
            P(("ep", "gd"), None),
            P("ep", None, "gd"),
            P("ep", None, "gd"),
            P("ep", "gd", None),
            P(None, "gd"),
            P(None, "gd"),
            P(None, "gd"),
            P("ep", "gd", None, None),
            P("ep", "gd", None, None),
            P("ep"),
        ),
        out_specs=(P(("ep", "gd"), None), P("ep", "gd")),
        check_vma=False,
    )
```

```python
import functools
import math

import jax
import jax.numpy as jnp
from jax import lax
from jax.experimental import pallas as pl
from jax.experimental.pallas import tpu as pltpu
from jax.sharding import PartitionSpec as P

EPSILON = 1e-06


def norm_rows(values):
    widened = values.astype(jnp.float32)
    return (
        widened * lax.rsqrt(jnp.mean(widened * widened, axis=-1, keepdims=True) + EPSILON)
    ).astype(jnp.bfloat16)


def slot_numbers(chosen, experts):
    blocks_n, rows_n, picks_n = chosen.shape
    flat_ids = chosen.reshape(blocks_n, rows_n * picks_n)
    onehot = (flat_ids[:, :, None] == jnp.arange(experts, dtype=jnp.int32)[None, None, :]).astype(
        jnp.int32
    )
    before = jnp.cumsum(onehot, axis=1) - onehot
    return jnp.sum(before * onehot, axis=-1).reshape(blocks_n, rows_n, picks_n)


def build_slots(row_blocks, targets, slots_n):
    wanted = jnp.any(
        targets[:, None, :, :] == jnp.arange(slots_n, dtype=jnp.int32)[None, :, None, None], axis=-1
    )
    selector = wanted.astype(jnp.bfloat16)
    return jnp.einsum(
        "bsr,brd->bsd", selector, row_blocks, preferred_element_type=jnp.float32
    ).astype(jnp.bfloat16)


def per_device(
    tokens,
    expert_ids,
    combine,
    w_gate,
    w_up,
    w_down,
    w_query,
    w_key,
    w_value,
    cache_keys,
    cache_values,
    lengths,
):
    rows_n, width = tokens.shape
    picks_n = expert_ids.shape[1]
    experts = lax.axis_size("ep")
    members = lax.axis_size("gd")
    capacity = max(2, 3 * rows_n * picks_n // (2 * experts))
    slots_n = experts * capacity
    normed = norm_rows(tokens)
    own_slot = slot_numbers(expert_ids[None], experts)[0]
    own_dest = expert_ids * capacity + own_slot
    group_normed, group_ids = (
        lax.all_gather(normed, "gd", axis=0, tiled=True),
        lax.all_gather(expert_ids, "gd", axis=0, tiled=True),
    )
    group_ids = group_ids.reshape(members, rows_n, picks_n)
    group_dest = group_ids * capacity + slot_numbers(group_ids, experts)
    outgoing = build_slots(group_normed.reshape(members, rows_n, width), group_dest, slots_n)
    outgoing = outgoing.reshape(members, experts, capacity, width)
    arrived = lax.all_to_all(outgoing, "ep", split_axis=1, concat_axis=1, tiled=True)
    slot_rows = arrived.reshape(-1, width)
    gate_val = jnp.dot(slot_rows, w_gate[0], preferred_element_type=jnp.float32)
    up_val = jnp.dot(slot_rows, w_up[0], preferred_element_type=jnp.float32)
    active = (jax.nn.silu(gate_val) * up_val).astype(jnp.bfloat16)
    partial_out = jnp.dot(active, w_down[0], preferred_element_type=jnp.float32).astype(
        jnp.bfloat16
    )
    summed = lax.psum_scatter(
        lax.optimization_barrier(partial_out).astype(jnp.float32).astype(jnp.bfloat16),
        "gd",
        scatter_dimension=0,
        tiled=True,
    ).astype(jnp.float32)
    returned = lax.all_to_all(
        summed.reshape(experts, capacity, width), "ep", split_axis=0, concat_axis=0, tiled=True
    )
    matches = own_dest[:, :, None] == jnp.arange(slots_n, dtype=jnp.int32)[None, None, :]
    weight_rows = jnp.sum(jnp.where(matches, combine[:, :, None], 0.0), axis=1)
    mixture = jnp.dot(
        weight_rows,
        returned.reshape(slots_n, width),
        precision=lax.Precision.HIGHEST,
        preferred_element_type=jnp.float32,
    )
    stream = (tokens.astype(jnp.float32) + mixture).astype(jnp.bfloat16)
    group_stream = lax.all_gather(stream, "gd", axis=0, tiled=True)
    guard_norm = norm_rows(group_stream)
    queries = jnp.dot(guard_norm, w_query, preferred_element_type=jnp.float32)
    key_new = jnp.dot(guard_norm, w_key, preferred_element_type=jnp.float32).astype(jnp.bfloat16)
    value_new = jnp.dot(guard_norm, w_value, preferred_element_type=jnp.float32).astype(
        jnp.bfloat16
    )
    group_total, heads_kv, window_len, head_size = cache_keys.shape
    heads_per = w_query.shape[1] // (heads_kv * head_size)
    queries = queries.reshape(group_total, heads_kv, heads_per, head_size)
    key_new = key_new.reshape(group_total, heads_kv, head_size)
    value_new = value_new.reshape(group_total, heads_kv, head_size)
    scale_factor = 1.0 / math.sqrt(head_size)
    scores = (
        jnp.einsum(
            "rhgd,rhjd->rhgj",
            queries,
            cache_keys.astype(jnp.float32),
            precision=lax.Precision.HIGHEST,
        )
        * scale_factor
    )
    own_score = (
        jnp.einsum(
            "rhgd,rhd->rhg", queries, key_new.astype(jnp.float32), precision=lax.Precision.HIGHEST
        )
        * scale_factor
    )
    positions = jnp.arange(window_len, dtype=jnp.int32)
    allowed = positions[None, None, None, :] >= (window_len - lengths)[:, None, None, None]
    masked = jnp.where(allowed, scores, -jnp.inf)
    highest = jnp.maximum(jnp.max(masked, axis=-1), own_score)
    weights = jnp.exp(masked - highest[..., None])
    own_weight = jnp.exp(own_score - highest)
    denominator = jnp.sum(weights, axis=-1) + own_weight
    probabilities = weights / denominator[..., None]
    own_prob = own_weight / denominator
    attended = jnp.einsum(
        "rhgj,rhjd->rhgd",
        probabilities,
        cache_values.astype(jnp.float32),
        precision=lax.Precision.HIGHEST,
    )
    attended = attended + own_prob[..., None] * value_new.astype(jnp.float32)[:, :, None, :]
    guard = attended.astype(jnp.bfloat16).reshape(group_total, heads_kv * heads_per * head_size)
    return (stream, guard)


CORES = 2
CHIPS = 4
CHUNKS = 2
MESH = pl.DeviceIdType.MESH


def as_column(line):
    size = line.shape[1]
    across = lax.broadcasted_iota(jnp.int32, (size, size), 1)
    down = lax.broadcasted_iota(jnp.int32, (size, size), 0)
    return jnp.sum(jnp.where(across == down, line, 0.0), axis=1, keepdims=True)


def fused_kernel(
    groups,
    tokens_hbm,
    ids_hbm,
    combine_hbm,
    lengths_hbm,
    gate_hbm,
    up_hbm,
    down_hbm,
    query_hbm,
    key_hbm,
    value_hbm,
    cache_k_hbm,
    cache_v_hbm,
    stream_ref,
    guard_ref,
    tokens_ref,
    ids_ref,
    combine_ref,
    lengths_ref,
    w_in,
    w_out,
    w_guard,
    keys,
    values,
    rows_in,
    rows_all,
    weight_all,
    hidden,
    active,
    part,
    got_core,
    sum_core,
    got_chip,
    sum_mid,
    sum_chip,
    got_z,
    stream_all,
    load_sem,
    z_send,
    z_recv,
    x_send,
    x_recv,
    y_send,
    y_recv,
    d_send,
    d_recv,
    c_send,
    c_recv,
    r1_send,
    r1_recv,
    r2_send,
    r2_recv,
    r3_send,
    r3_recv,
    s_send,
    s_recv,
):
    rows_n, width = tokens_hbm.shape
    half = width // 2
    unit = gate_hbm.shape[2]
    me_e = lax.axis_index("ep")
    g = lax.axis_index("gd")
    core = me_e % CORES
    chip = me_e // CORES
    x, y = chip % 2, chip // 2
    x_chip = y * 2 + (1 - x)
    y_chip = (1 - y) * 2 + x
    d_chip = (1 - y) * 2 + (1 - x)
    sibling = (chip * CORES + (1 - core), g)
    x_dev = (x_chip * CORES + core, g)
    y_dev = (y_chip * CORES + core, g)

    def z_of(step):
        return (g + step) % groups

    loads = []

    def load(src, dst):
        copy = pltpu.make_async_copy(src, dst, load_sem.at[len(loads)])
        copy.start()
        loads.append(copy)

    barrier = pltpu.get_barrier_semaphore()
    peers = [sibling, x_dev, y_dev] + [(me_e, z_of(k)) for k in range(1, groups)]
    for peer in peers:
        pl.semaphore_signal(barrier, inc=1, device_id=peer, device_id_type=MESH)

    load(tokens_hbm, tokens_ref)
    load(ids_hbm, ids_ref)
    load(combine_hbm, combine_ref)
    load(lengths_hbm, lengths_ref)
    load(gate_hbm.at[0], w_in.at[:, 0:unit])
    load(up_hbm.at[0], w_in.at[:, unit : 2 * unit])
    load(down_hbm.at[0], w_out)
    q_n, k_n = query_hbm.shape[1], key_hbm.shape[1]
    load(query_hbm, w_guard.at[:, 0:q_n])
    load(key_hbm, w_guard.at[:, q_n : q_n + k_n])
    load(value_hbm, w_guard.at[:, q_n + k_n : q_n + 2 * k_n])
    load(cache_k_hbm, keys)
    load(cache_v_hbm, values)

    for i in range(3):
        loads[i].wait()
    wide = tokens_ref[...].astype(jnp.float32)
    normed = wide * lax.rsqrt(jnp.mean(wide * wide, axis=-1, keepdims=True) + EPSILON)
    lanes = lax.broadcasted_iota(jnp.int32, (rows_n, 128), 1)
    table = jnp.zeros((rows_n, 128), jnp.float32)
    for k in range(ids_ref.shape[0]):
        named = as_column(ids_ref[k : k + 1, :].astype(jnp.float32)).astype(jnp.int32)
        share_of = as_column(combine_ref[k : k + 1, :])
        table = table + jnp.where(lanes == named, share_of, 0.0)
    table_top = table.astype(jnp.bfloat16).astype(jnp.float32)
    packed = jnp.concatenate([normed[:, :half], normed[:, half:]], axis=0)
    rows_in[core, chip, g, :, 0:half] = packed.astype(jnp.bfloat16)
    rows_in[core, chip, g, :, half : half + 128] = jnp.concatenate(
        [table_top, table - table_top], axis=0
    ).astype(jnp.bfloat16)

    pl.semaphore_wait(barrier, len(peers))

    sends = []

    def send(src, dst, send_sem, recv_sem, device):
        copy = pltpu.make_async_remote_copy(
            src_ref=src,
            dst_ref=dst,
            send_sem=send_sem,
            recv_sem=recv_sem,
            device_id=device,
            device_id_type=MESH,
        )
        copy.start()
        sends.append(copy)
        return copy

    def row_send(chip_of, step, send_sem, recv_sem, device):
        block = rows_in.at[core, chip_of, (g + groups - step) % groups]
        return send(block, block, send_sem, recv_sem, device)

    z_copies, x_copies, y_copies, d_copies, c_copies = {}, {}, {}, {}, {}

    def share(kind, chip_of, step):
        c_copies[kind, step] = row_send(
            chip_of, step, c_send.at[kind, step], c_recv.at[kind, step], sibling
        )

    def spread(step):
        x_copies[step] = row_send(chip, step, x_send.at[step], x_recv.at[step], x_dev)
        y_copies[step] = row_send(chip, step, y_send.at[step], y_recv.at[step], y_dev)
        share(0, chip, step)

    def forward(step):
        x_copies[step].wait_recv()
        if step % 2 == 1:
            d_copies[step] = row_send(x_chip, step, d_send.at[step], d_recv.at[step], y_dev)
        share(1, x_chip, step)
        y_copies[step].wait_recv()
        if step % 2 == 0:
            d_copies[step] = row_send(y_chip, step, d_send.at[step], d_recv.at[step], x_dev)
        share(2, y_chip, step)

    for k in range(1, groups):
        z_copies[k] = row_send(chip, 0, z_send.at[k], z_recv.at[k], (me_e, z_of(k)))
    spread(0)
    for k in range(1, groups):
        z_copies[k].wait_recv()
        spread(k)
        forward(k - 1)
    forward(groups - 1)
    group_rows = groups * rows_n
    core_rows = CHIPS * group_rows
    tile = 256

    def unpack(c, h):
        start = pl.multiple_of((c * CHIPS + h) * group_rows, group_rows)
        for side in range(2):
            got = rows_in[c, h, :, :, 0:half].astype(jnp.float32)
            got = got[:, side * rows_n : (side + 1) * rows_n].reshape(group_rows, half)
            rows_all[pl.ds(start, group_rows), side * half : (side + 1) * half] = got.astype(
                jnp.bfloat16
            )
        extra = rows_in[c, h, :, :, half : half + 128].astype(jnp.float32)
        weight_all[pl.ds(start, group_rows), :] = (extra[:, :rows_n] + extra[:, rows_n:]).reshape(
            group_rows, 128
        )

    def first_layer(c):
        some = pl.ds(pl.multiple_of(c * core_rows, core_rows), core_rows)

        def first(n, carry):
            cols = pl.ds(pl.multiple_of(n * tile, tile), tile)
            hidden[some, cols] = jnp.dot(
                rows_all[some, :], w_in[:, cols], preferred_element_type=jnp.float32
            )
            return carry

        lax.fori_loop(0, 2 * unit // tile, first, 0)
        table_all = weight_all[some, :]
        picked = lax.broadcasted_iota(jnp.int32, table_all.shape, 1) == me_e
        row_weight = jnp.sum(jnp.where(picked, table_all, 0.0), axis=-1, keepdims=True)
        gate_val = hidden[some, 0:unit]
        active[some, :] = (
            gate_val / (1.0 + jnp.exp(-gate_val)) * hidden[some, unit : 2 * unit] * row_weight
        ).astype(jnp.bfloat16)

    unpack(core, chip)
    unpack(core, x_chip)
    unpack(core, y_chip)
    for k in range(groups):
        d_copies[k].wait_recv()
        share(3, d_chip, k)
    unpack(core, d_chip)
    loads[4].wait()
    loads[5].wait()
    first_layer(core)
    for kind, chip_of in enumerate((chip, x_chip, y_chip, d_chip)):
        for k in range(groups):
            c_copies[kind, k].wait_recv()
        unpack(1 - core, chip_of)
    first_layer(1 - core)
    loads[6].wait()

    span = width // CHUNKS
    piece = span // 2
    paired = groups // 2
    r1, r2, r3, s_copies = {}, {}, {}, {}

    def expert_half(t, c):
        some = pl.ds(pl.multiple_of(c * core_rows, core_rows), core_rows)
        outs = []
        for side in range(2):
            lower = t * span + side * piece
            outs.append(
                jnp.dot(
                    active[some, :],
                    w_out[:, lower : lower + piece],
                    preferred_element_type=jnp.float32,
                ).reshape(CHIPS, groups, rows_n, piece)
            )
        part[t, c] = jnp.concatenate(outs, axis=2).astype(jnp.bfloat16)

    def expert_chunk(t):
        expert_half(t, 1 - core)
        r1[t] = send(
            part.at[t, 1 - core], got_core.at[t], r1_send.at[t], r1_recv.at[t], sibling
        )
        expert_half(t, core)

    def chip_chunk(t):
        r1[t].wait_recv()
        total = part[t, core].astype(jnp.float32) + got_core[t].astype(jnp.float32)
        sum_core[t] = total.astype(jnp.bfloat16)
        for kind, chips_to in ((1, (d_chip, d_chip)), (0, (x_chip, y_chip))):
            for side in range(2):
                some = pl.ds(side * paired, paired)
                r2[t, kind, side] = send(
                    sum_core.at[t, chips_to[side], some],
                    got_chip.at[t, kind, some],
                    r2_send.at[t, kind, side],
                    r2_recv.at[t, kind, side],
                    (x_dev, y_dev)[side],
                )

    def mid_chunk(t):
        for side in range(2):
            some = pl.ds(side * paired, paired)
            r2[t, 1, side].wait_recv()
            total = sum_core[t, (y_chip, x_chip)[side], some].astype(jnp.float32)
            total = total + got_chip[t, 1, some].astype(jnp.float32)
            sum_mid[t, some] = total.astype(jnp.bfloat16)
            r2[t, 2, side] = send(
                sum_mid.at[t, some],
                got_chip.at[t, 2, some],
                r2_send.at[t, 2, side],
                r2_recv.at[t, 2, side],
                (y_dev, x_dev)[side],
            )

    def z_chunk(t):
        total = sum_core[t, chip].astype(jnp.float32)
        for kind in (0, 2):
            for side in range(2):
                r2[t, kind, side].wait_recv()
            total = total + got_chip[t, kind].astype(jnp.float32)
        sum_chip[t] = total.astype(jnp.bfloat16)
        for k in range(1, groups):
            r3[t, k] = send(
                sum_chip.at[t, z_of(k)],
                got_z.at[t, k],
                r3_send.at[t, k],
                r3_recv.at[t, k],
                (me_e, z_of(k)),
            )

    def stream_chunk(t):
        total = sum_chip[t, g].astype(jnp.float32)
        for k in range(1, groups):
            r3[t, k].wait_recv()
            total = total + got_z[t, k].astype(jnp.float32)
        mixture = jnp.concatenate([total[:rows_n], total[rows_n:]], axis=1)
        cols = slice(t * span, (t + 1) * span)
        stream = tokens_ref[:, cols].astype(jnp.float32) + mixture
        stream_ref[:, cols] = stream.astype(jnp.bfloat16)
        stream_all[t, g] = jnp.concatenate(
            [stream[:, :piece], stream[:, piece:]], axis=0
        ).astype(jnp.bfloat16)
        for k in range(1, groups):
            block = stream_all.at[t, g]
            s_copies[t, k] = send(
                block, block, s_send.at[t, k], s_recv.at[t, k], (me_e, z_of(k))
            )

    state = {}

    def guard_chunk(t):
        for k in range(1, groups):
            s_copies[t, k].wait_recv()
        got = stream_all[t].astype(jnp.float32)
        if t == 0:
            for i in (3, 7, 8, 9, 10, 11):
                loads[i].wait()
        for side in range(2):
            rows = got[:, side * rows_n : (side + 1) * rows_n].reshape(group_rows, piece)
            lower = t * span + side * piece
            product = jnp.dot(
                rows.astype(jnp.bfloat16),
                w_guard[lower : lower + piece, :],
                preferred_element_type=jnp.float32,
            )
            square = jnp.sum(rows * rows, axis=-1, keepdims=True)
            if t == 0 and side == 0:
                state["qkv"], state["square"] = product, square
            else:
                state["qkv"] = state["qkv"] + product
                state["square"] = state["square"] + square

    stages = (expert_chunk, chip_chunk, mid_chunk, z_chunk, stream_chunk, guard_chunk)
    for step in range(CHUNKS + len(stages) - 1):
        for late, stage in enumerate(stages):
            if 0 <= step - late < CHUNKS:
                stage(step - late)

    qkv = state["qkv"] * lax.rsqrt(state["square"] / width + EPSILON)
    head = keys.shape[1]
    heads = q_n // head
    window = keys.shape[0] // group_rows
    scale = 1.0 / math.sqrt(head)
    key_new = qkv[:, q_n : q_n + k_n].astype(jnp.bfloat16).astype(jnp.float32)
    value_new = qkv[:, q_n + k_n :].astype(jnp.bfloat16).astype(jnp.float32)
    lengths_n = as_column(lengths_ref[...].astype(jnp.float32)).astype(jnp.int32)
    span_keys = rows_n * window
    outs = []
    for a in range(groups):
        here = slice(a * rows_n, (a + 1) * rows_n)
        query = jnp.concatenate([qkv[here, h * head : (h + 1) * head] for h in range(heads)], axis=0)
        key_own = jnp.concatenate([key_new[here]] * heads, axis=0)
        value_own = jnp.concatenate([value_new[here]] * heads, axis=0)
        allowed_n = jnp.concatenate([lengths_n[here]] * heads, axis=0)
        own_score = jnp.sum(query * key_own, axis=-1, keepdims=True) * scale
        pieces, rest = [], query
        for _ in range(3):
            top = rest.astype(jnp.bfloat16).astype(jnp.float32)
            pieces.append(top)
            rest = rest - top
        product = lax.dot_general(
            jnp.concatenate(pieces, axis=0).astype(jnp.bfloat16),
            keys[a * span_keys : (a + 1) * span_keys, :],
            (((1,), (1,)), ((), ())),
            preferred_element_type=jnp.float32,
        )
        all_rows = heads * rows_n
        scores = (
            product[:all_rows] + product[all_rows : 2 * all_rows] + product[2 * all_rows :]
        ) * scale
        column = lax.broadcasted_iota(jnp.int32, scores.shape, 1)
        row = lax.broadcasted_iota(jnp.int32, (all_rows, 1), 0) % rows_n
        upper = (row + 1) * window
        allowed = (column >= upper - allowed_n) & (column < upper)
        masked = jnp.where(allowed, scores, -jnp.inf)
        highest = jnp.maximum(jnp.max(masked, axis=-1, keepdims=True), own_score)
        weights = jnp.exp(masked - highest)
        own_weight = jnp.exp(own_score - highest)
        denominator = jnp.sum(weights, axis=-1, keepdims=True) + own_weight
        top = weights.astype(jnp.bfloat16).astype(jnp.float32)
        product = jnp.dot(
            jnp.concatenate([top, weights - top], axis=0).astype(jnp.bfloat16),
            values[a * span_keys : (a + 1) * span_keys, :],
            preferred_element_type=jnp.float32,
        )
        attended = product[:all_rows] + product[all_rows:] + own_weight * value_own
        attended = attended / denominator
        outs.append(
            jnp.concatenate(
                [attended[h * rows_n : (h + 1) * rows_n] for h in range(heads)], axis=1
            )
        )
    guard_ref[...] = jnp.concatenate(outs, axis=0).astype(jnp.bfloat16)
    for copy in sends:
        copy.wait_send()


def fused_device(
    tokens,
    expert_ids,
    combine,
    w_gate,
    w_up,
    w_down,
    w_query,
    w_key,
    w_value,
    cache_keys,
    cache_values,
    lengths,
):
    rows_n, width = tokens.shape
    groups = lax.axis_size("gd")
    unit = w_gate.shape[2]
    group_rows, heads_kv, window, head = cache_keys.shape
    total_rows = CORES * CHIPS * groups * rows_n
    piece = width // CHUNKS // 2
    pack = 2 * rows_n
    guard_n = w_query.shape[1] + w_key.shape[1] + w_value.shape[1]
    bf16, f32 = jnp.bfloat16, jnp.float32
    dma = pltpu.SemaphoreType.DMA
    in_vmem = pl.BlockSpec(memory_space=pltpu.VMEM)
    in_hbm = pl.BlockSpec(memory_space=pltpu.HBM)
    return pl.pallas_call(
        functools.partial(fused_kernel, groups),
        out_shape=(
            jax.ShapeDtypeStruct((rows_n, width), bf16),
            jax.ShapeDtypeStruct((group_rows, w_query.shape[1]), bf16),
        ),
        in_specs=[in_hbm] * 12,
        out_specs=(in_vmem, in_vmem),
        scratch_shapes=[
            pltpu.VMEM((rows_n, width), bf16),
            pltpu.VMEM((expert_ids.shape[1], rows_n), jnp.int32),
            pltpu.VMEM((combine.shape[1], rows_n), f32),
            pltpu.VMEM((1, group_rows), jnp.int32),
            pltpu.VMEM((width, 2 * unit), bf16),
            pltpu.VMEM((unit, width), bf16),
            pltpu.VMEM((width, guard_n), bf16),
            pltpu.VMEM((group_rows * window, head), bf16),
            pltpu.VMEM((group_rows * window, head), bf16),
            pltpu.VMEM((CORES, CHIPS, groups, pack, width // 2 + 128), bf16),
            pltpu.VMEM((total_rows, width), bf16),
            pltpu.VMEM((total_rows, 128), f32),
            pltpu.VMEM((total_rows, 2 * unit), f32),
            pltpu.VMEM((total_rows, unit), bf16),
            pltpu.VMEM((CHUNKS, CORES, CHIPS, groups, pack, piece), bf16),
            pltpu.VMEM((CHUNKS, CHIPS, groups, pack, piece), bf16),
            pltpu.VMEM((CHUNKS, CHIPS, groups, pack, piece), bf16),
            pltpu.VMEM((CHUNKS, 3, groups, pack, piece), bf16),
            pltpu.VMEM((CHUNKS, groups, pack, piece), bf16),
            pltpu.VMEM((CHUNKS, groups, pack, piece), bf16),
            pltpu.VMEM((CHUNKS, groups, pack, piece), bf16),
            pltpu.VMEM((CHUNKS, groups, pack, piece), bf16),
            dma((12,)),
            dma((groups,)),
            dma((groups,)),
            dma((groups,)),
            dma((groups,)),
            dma((groups,)),
            dma((groups,)),
            dma((groups,)),
            dma((groups,)),
            dma((4, groups)),
            dma((4, groups)),
            dma((CHUNKS,)),
            dma((CHUNKS,)),
            dma((CHUNKS, 3, 2)),
            dma((CHUNKS, 3, 2)),
            dma((CHUNKS, groups)),
            dma((CHUNKS, groups)),
            dma((CHUNKS, groups)),
            dma((CHUNKS, groups)),
        ],
        compiler_params=pltpu.CompilerParams(
            collective_id=0, has_side_effects=True, vmem_limit_bytes=64000 * 1024
        ),
    )(
        tokens,
        expert_ids.T,
        combine.T,
        lengths.reshape(1, group_rows),
        w_gate,
        w_up,
        w_down,
        w_query,
        w_key,
        w_value,
        cache_keys.reshape(group_rows * heads_kv * window, head),
        cache_values.reshape(group_rows * heads_kv * window, head),
    )


def solution(mesh):
    fused = mesh.shape["ep"] == 8 and mesh.shape["gd"] == 4
    return jax.shard_map(
        fused_device if fused else per_device,
        mesh=mesh,
        in_specs=(
            P(("ep", "gd"), None),
            P(("ep", "gd"), None),
            P(("ep", "gd"), None),
            P("ep", None, "gd"),
            P("ep", None, "gd"),
            P("ep", "gd", None),
            P(None, "gd"),
            P(None, "gd"),
            P(None, "gd"),
            P("ep", "gd", None, None),
            P("ep", "gd", None, None),
            P("ep"),
        ),
        out_specs=(P(("ep", "gd"), None), P("ep", "gd")),
        check_vma=False,
    )
```

```python
import functools
import math

import jax
import jax.numpy as jnp
from jax import lax
from jax.experimental import pallas as pl
from jax.experimental.pallas import tpu as pltpu
from jax.sharding import PartitionSpec as P

EPSILON = 1e-06


def norm_rows(values):
    widened = values.astype(jnp.float32)
    return (
        widened * lax.rsqrt(jnp.mean(widened * widened, axis=-1, keepdims=True) + EPSILON)
    ).astype(jnp.bfloat16)


def slot_numbers(chosen, experts):
    blocks_n, rows_n, picks_n = chosen.shape
    flat_ids = chosen.reshape(blocks_n, rows_n * picks_n)
    onehot = (flat_ids[:, :, None] == jnp.arange(experts, dtype=jnp.int32)[None, None, :]).astype(
        jnp.int32
    )
    before = jnp.cumsum(onehot, axis=1) - onehot
    return jnp.sum(before * onehot, axis=-1).reshape(blocks_n, rows_n, picks_n)


def build_slots(row_blocks, targets, slots_n):
    wanted = jnp.any(
        targets[:, None, :, :] == jnp.arange(slots_n, dtype=jnp.int32)[None, :, None, None], axis=-1
    )
    selector = wanted.astype(jnp.bfloat16)
    return jnp.einsum(
        "bsr,brd->bsd", selector, row_blocks, preferred_element_type=jnp.float32
    ).astype(jnp.bfloat16)


def per_device(
    tokens,
    expert_ids,
    combine,
    w_gate,
    w_up,
    w_down,
    w_query,
    w_key,
    w_value,
    cache_keys,
    cache_values,
    lengths,
):
    rows_n, width = tokens.shape
    picks_n = expert_ids.shape[1]
    experts = lax.axis_size("ep")
    members = lax.axis_size("gd")
    capacity = max(2, 3 * rows_n * picks_n // (2 * experts))
    slots_n = experts * capacity
    normed = norm_rows(tokens)
    own_slot = slot_numbers(expert_ids[None], experts)[0]
    own_dest = expert_ids * capacity + own_slot
    group_normed, group_ids = (
        lax.all_gather(normed, "gd", axis=0, tiled=True),
        lax.all_gather(expert_ids, "gd", axis=0, tiled=True),
    )
    group_ids = group_ids.reshape(members, rows_n, picks_n)
    group_dest = group_ids * capacity + slot_numbers(group_ids, experts)
    outgoing = build_slots(group_normed.reshape(members, rows_n, width), group_dest, slots_n)
    outgoing = outgoing.reshape(members, experts, capacity, width)
    arrived = lax.all_to_all(outgoing, "ep", split_axis=1, concat_axis=1, tiled=True)
    slot_rows = arrived.reshape(-1, width)
    gate_val = jnp.dot(slot_rows, w_gate[0], preferred_element_type=jnp.float32)
    up_val = jnp.dot(slot_rows, w_up[0], preferred_element_type=jnp.float32)
    active = (jax.nn.silu(gate_val) * up_val).astype(jnp.bfloat16)
    partial_out = jnp.dot(active, w_down[0], preferred_element_type=jnp.float32).astype(
        jnp.bfloat16
    )
    summed = lax.psum_scatter(
        lax.optimization_barrier(partial_out).astype(jnp.float32).astype(jnp.bfloat16),
        "gd",
        scatter_dimension=0,
        tiled=True,
    ).astype(jnp.float32)
    returned = lax.all_to_all(
        summed.reshape(experts, capacity, width), "ep", split_axis=0, concat_axis=0, tiled=True
    )
    matches = own_dest[:, :, None] == jnp.arange(slots_n, dtype=jnp.int32)[None, None, :]
    weight_rows = jnp.sum(jnp.where(matches, combine[:, :, None], 0.0), axis=1)
    mixture = jnp.dot(
        weight_rows,
        returned.reshape(slots_n, width),
        precision=lax.Precision.HIGHEST,
        preferred_element_type=jnp.float32,
    )
    stream = (tokens.astype(jnp.float32) + mixture).astype(jnp.bfloat16)
    group_stream = lax.all_gather(stream, "gd", axis=0, tiled=True)
    guard_norm = norm_rows(group_stream)
    queries = jnp.dot(guard_norm, w_query, preferred_element_type=jnp.float32)
    key_new = jnp.dot(guard_norm, w_key, preferred_element_type=jnp.float32).astype(jnp.bfloat16)
    value_new = jnp.dot(guard_norm, w_value, preferred_element_type=jnp.float32).astype(
        jnp.bfloat16
    )
    group_total, heads_kv, window_len, head_size = cache_keys.shape
    heads_per = w_query.shape[1] // (heads_kv * head_size)
    queries = queries.reshape(group_total, heads_kv, heads_per, head_size)
    key_new = key_new.reshape(group_total, heads_kv, head_size)
    value_new = value_new.reshape(group_total, heads_kv, head_size)
    scale_factor = 1.0 / math.sqrt(head_size)
    scores = (
        jnp.einsum(
            "rhgd,rhjd->rhgj",
            queries,
            cache_keys.astype(jnp.float32),
            precision=lax.Precision.HIGHEST,
        )
        * scale_factor
    )
    own_score = (
        jnp.einsum(
            "rhgd,rhd->rhg", queries, key_new.astype(jnp.float32), precision=lax.Precision.HIGHEST
        )
        * scale_factor
    )
    positions = jnp.arange(window_len, dtype=jnp.int32)
    allowed = positions[None, None, None, :] >= (window_len - lengths)[:, None, None, None]
    masked = jnp.where(allowed, scores, -jnp.inf)
    highest = jnp.maximum(jnp.max(masked, axis=-1), own_score)
    weights = jnp.exp(masked - highest[..., None])
    own_weight = jnp.exp(own_score - highest)
    denominator = jnp.sum(weights, axis=-1) + own_weight
    probabilities = weights / denominator[..., None]
    own_prob = own_weight / denominator
    attended = jnp.einsum(
        "rhgj,rhjd->rhgd",
        probabilities,
        cache_values.astype(jnp.float32),
        precision=lax.Precision.HIGHEST,
    )
    attended = attended + own_prob[..., None] * value_new.astype(jnp.float32)[:, :, None, :]
    guard = attended.astype(jnp.bfloat16).reshape(group_total, heads_kv * heads_per * head_size)
    return (stream, guard)


CORES = 2
CHIPS = 4
CHUNKS = 4
MESH = pl.DeviceIdType.MESH


def as_column(line):
    size = line.shape[1]
    across = lax.broadcasted_iota(jnp.int32, (size, size), 1)
    down = lax.broadcasted_iota(jnp.int32, (size, size), 0)
    return jnp.sum(jnp.where(across == down, line, 0.0), axis=1, keepdims=True)


def fused_kernel(
    groups,
    tokens_hbm,
    ids_hbm,
    combine_hbm,
    lengths_hbm,
    gate_hbm,
    up_hbm,
    down_hbm,
    query_hbm,
    key_hbm,
    value_hbm,
    cache_k_hbm,
    cache_v_hbm,
    stream_ref,
    guard_ref,
    tokens_ref,
    ids_ref,
    combine_ref,
    lengths_ref,
    w_in,
    w_out,
    w_guard,
    keys,
    values,
    rows_in,
    rows_all,
    weight_all,
    hidden,
    active,
    part,
    got_core,
    sum_core,
    got_chip,
    sum_mid,
    sum_chip,
    got_z,
    stream_all,
    load_sem,
    z_send,
    z_recv,
    x_send,
    x_recv,
    y_send,
    y_recv,
    d_send,
    d_recv,
    c_send,
    c_recv,
    r1_send,
    r1_recv,
    r2_send,
    r2_recv,
    r3_send,
    r3_recv,
    s_send,
    s_recv,
):
    rows_n, width = tokens_hbm.shape
    half = width // 2
    unit = gate_hbm.shape[2]
    me_e = lax.axis_index("ep")
    g = lax.axis_index("gd")
    core = me_e % CORES
    chip = me_e // CORES
    x, y = chip % 2, chip // 2
    x_chip = y * 2 + (1 - x)
    y_chip = (1 - y) * 2 + x
    d_chip = (1 - y) * 2 + (1 - x)
    sibling = (chip * CORES + (1 - core), g)
    x_dev = (x_chip * CORES + core, g)
    y_dev = (y_chip * CORES + core, g)
    d_dev = (d_chip * CORES + core, g)

    def z_of(step):
        return (g + step) % groups

    loads = []

    def load(src, dst):
        copy = pltpu.make_async_copy(src, dst, load_sem.at[len(loads)])
        copy.start()
        loads.append(copy)

    barrier = pltpu.get_barrier_semaphore()
    peers = [sibling, x_dev, y_dev, d_dev] + [(me_e, z_of(k)) for k in range(1, groups)]
    for peer in peers:
        pl.semaphore_signal(barrier, inc=1, device_id=peer, device_id_type=MESH)

    load(tokens_hbm, tokens_ref)
    load(ids_hbm, ids_ref)
    load(combine_hbm, combine_ref)
    load(lengths_hbm, lengths_ref)
    load(gate_hbm.at[0], w_in.at[:, 0:unit])
    load(up_hbm.at[0], w_in.at[:, unit : 2 * unit])
    load(down_hbm.at[0], w_out)
    q_n, k_n = query_hbm.shape[1], key_hbm.shape[1]
    load(query_hbm, w_guard.at[:, 0:q_n])
    load(key_hbm, w_guard.at[:, q_n : q_n + k_n])
    load(value_hbm, w_guard.at[:, q_n + k_n : q_n + 2 * k_n])
    load(cache_k_hbm, keys)
    load(cache_v_hbm, values)

    for i in range(3):
        loads[i].wait()
    wide = tokens_ref[...].astype(jnp.float32)
    normed = wide * lax.rsqrt(jnp.mean(wide * wide, axis=-1, keepdims=True) + EPSILON)
    lanes = lax.broadcasted_iota(jnp.int32, (rows_n, 128), 1)
    table = jnp.zeros((rows_n, 128), jnp.float32)
    for k in range(ids_ref.shape[0]):
        named = as_column(ids_ref[k : k + 1, :].astype(jnp.float32)).astype(jnp.int32)
        share_of = as_column(combine_ref[k : k + 1, :])
        table = table + jnp.where(lanes == named, share_of, 0.0)
    table_top = table.astype(jnp.bfloat16).astype(jnp.float32)
    packed = jnp.concatenate([normed[:, :half], normed[:, half:]], axis=0)
    rows_in[core, chip, g, :, 0:half] = packed.astype(jnp.bfloat16)
    rows_in[core, chip, g, :, half : half + 128] = jnp.concatenate(
        [table_top, table - table_top], axis=0
    ).astype(jnp.bfloat16)

    pl.semaphore_wait(barrier, len(peers))

    sends = []

    def send(src, dst, send_sem, recv_sem, device):
        copy = pltpu.make_async_remote_copy(
            src_ref=src,
            dst_ref=dst,
            send_sem=send_sem,
            recv_sem=recv_sem,
            device_id=device,
            device_id_type=MESH,
        )
        copy.start()
        sends.append(copy)
        return copy

    def row_send(chip_of, step, send_sem, recv_sem, device):
        block = rows_in.at[core, chip_of, (g + groups - step) % groups]
        return send(block, block, send_sem, recv_sem, device)

    z_copies, x_copies, y_copies, d_copies, c_copies = {}, {}, {}, {}, {}

    def share(kind, chip_of, step):
        c_copies[kind, step] = row_send(
            chip_of, step, c_send.at[kind, step], c_recv.at[kind, step], sibling
        )

    def spread(step):
        x_copies[step] = row_send(chip, step, x_send.at[step], x_recv.at[step], x_dev)
        y_copies[step] = row_send(chip, step, y_send.at[step], y_recv.at[step], y_dev)
        if step == groups - 1:
            d_copies[step] = row_send(chip, step, d_send.at[step], d_recv.at[step], d_dev)
        share(0, chip, step)

    def forward(step):
        x_copies[step].wait_recv()
        if step % 2 == 1 and step < groups - 1:
            d_copies[step] = row_send(x_chip, step, d_send.at[step], d_recv.at[step], y_dev)
        share(1, x_chip, step)
        y_copies[step].wait_recv()
        if step % 2 == 0 and step < groups - 1:
            d_copies[step] = row_send(y_chip, step, d_send.at[step], d_recv.at[step], x_dev)
        share(2, y_chip, step)

    for k in range(1, groups):
        z_copies[k] = row_send(chip, 0, z_send.at[k], z_recv.at[k], (me_e, z_of(k)))
    spread(0)
    for k in range(1, groups):
        z_copies[k].wait_recv()
        spread(k)
        forward(k - 1)
    forward(groups - 1)
    group_rows = groups * rows_n
    core_rows = CHIPS * group_rows
    tile = 256

    def unpack(c, h):
        start = pl.multiple_of((c * CHIPS + h) * group_rows, group_rows)
        for side in range(2):
            got = rows_in[c, h, :, :, 0:half].astype(jnp.float32)
            got = got[:, side * rows_n : (side + 1) * rows_n].reshape(group_rows, half)
            rows_all[pl.ds(start, group_rows), side * half : (side + 1) * half] = got.astype(
                jnp.bfloat16
            )
        extra = rows_in[c, h, :, :, half : half + 128].astype(jnp.float32)
        weight_all[pl.ds(start, group_rows), :] = (extra[:, :rows_n] + extra[:, rows_n:]).reshape(
            group_rows, 128
        )

    def first_layer(c):
        some = pl.ds(pl.multiple_of(c * core_rows, core_rows), core_rows)

        def first(n, carry):
            cols = pl.ds(pl.multiple_of(n * tile, tile), tile)
            hidden[some, cols] = jnp.dot(
                rows_all[some, :], w_in[:, cols], preferred_element_type=jnp.float32
            )
            return carry

        lax.fori_loop(0, 2 * unit // tile, first, 0)
        table_all = weight_all[some, :]
        picked = lax.broadcasted_iota(jnp.int32, table_all.shape, 1) == me_e
        row_weight = jnp.sum(jnp.where(picked, table_all, 0.0), axis=-1, keepdims=True)
        gate_val = hidden[some, 0:unit]
        active[some, :] = (
            gate_val / (1.0 + jnp.exp(-gate_val)) * hidden[some, unit : 2 * unit] * row_weight
        ).astype(jnp.bfloat16)

    unpack(core, chip)
    unpack(core, x_chip)
    unpack(core, y_chip)
    for k in range(groups):
        d_copies[k].wait_recv()
        share(3, d_chip, k)
    unpack(core, d_chip)
    loads[4].wait()
    loads[5].wait()
    first_layer(core)
    for kind, chip_of in enumerate((chip, x_chip, y_chip, d_chip)):
        for k in range(groups):
            c_copies[kind, k].wait_recv()
        unpack(1 - core, chip_of)
    first_layer(1 - core)
    loads[6].wait()

    span = width // CHUNKS
    piece = span // 2
    paired = groups // 2
    r1, r2, r3, s_copies = {}, {}, {}, {}

    def expert_half(t, c):
        some = pl.ds(pl.multiple_of(c * core_rows, core_rows), core_rows)
        outs = []
        for side in range(2):
            lower = t * span + side * piece
            outs.append(
                jnp.dot(
                    active[some, :],
                    w_out[:, lower : lower + piece],
                    preferred_element_type=jnp.float32,
                ).reshape(CHIPS, groups, rows_n, piece)
            )
        part[t, c] = jnp.concatenate(outs, axis=2).astype(jnp.bfloat16)

    def expert_chunk(t):
        expert_half(t, 1 - core)
        r1[t] = send(
            part.at[t, 1 - core], got_core.at[t], r1_send.at[t], r1_recv.at[t], sibling
        )
        expert_half(t, core)

    def chip_chunk(t):
        r1[t].wait_recv()
        total = part[t, core].astype(jnp.float32) + got_core[t].astype(jnp.float32)
        sum_core[t] = total.astype(jnp.bfloat16)
        for kind, chips_to in ((1, (d_chip, d_chip)), (0, (x_chip, y_chip))):
            for side in range(2):
                some = pl.ds(side * paired, paired)
                r2[t, kind, side] = send(
                    sum_core.at[t, chips_to[side], some],
                    got_chip.at[t, kind, some],
                    r2_send.at[t, kind, side],
                    r2_recv.at[t, kind, side],
                    (x_dev, y_dev)[side],
                )

    def mid_chunk(t):
        for side in range(2):
            some = pl.ds(side * paired, paired)
            r2[t, 1, side].wait_recv()
            total = sum_core[t, (y_chip, x_chip)[side], some].astype(jnp.float32)
            total = total + got_chip[t, 1, some].astype(jnp.float32)
            sum_mid[t, some] = total.astype(jnp.bfloat16)
            r2[t, 2, side] = send(
                sum_mid.at[t, some],
                got_chip.at[t, 2, some],
                r2_send.at[t, 2, side],
                r2_recv.at[t, 2, side],
                (y_dev, x_dev)[side],
            )

    def z_chunk(t):
        total = sum_core[t, chip].astype(jnp.float32)
        for kind in (0, 2):
            for side in range(2):
                r2[t, kind, side].wait_recv()
            total = total + got_chip[t, kind].astype(jnp.float32)
        sum_chip[t] = total.astype(jnp.bfloat16)
        for k in range(1, groups):
            r3[t, k] = send(
                sum_chip.at[t, z_of(k)],
                got_z.at[t, k],
                r3_send.at[t, k],
                r3_recv.at[t, k],
                (me_e, z_of(k)),
            )

    def stream_chunk(t):
        total = sum_chip[t, g].astype(jnp.float32)
        for k in range(1, groups):
            r3[t, k].wait_recv()
            total = total + got_z[t, k].astype(jnp.float32)
        mixture = jnp.concatenate([total[:rows_n], total[rows_n:]], axis=1)
        cols = slice(t * span, (t + 1) * span)
        stream = tokens_ref[:, cols].astype(jnp.float32) + mixture
        stream_ref[:, cols] = stream.astype(jnp.bfloat16)
        stream_all[t, g] = jnp.concatenate(
            [stream[:, :piece], stream[:, piece:]], axis=0
        ).astype(jnp.bfloat16)
        for k in range(1, groups):
            block = stream_all.at[t, g]
            s_copies[t, k] = send(
                block, block, s_send.at[t, k], s_recv.at[t, k], (me_e, z_of(k))
            )

    state = {}

    def guard_chunk(t):
        for k in range(1, groups):
            s_copies[t, k].wait_recv()
        got = stream_all[t].astype(jnp.float32)
        if t == 0:
            for i in (3, 7, 8, 9, 10, 11):
                loads[i].wait()
        for side in range(2):
            rows = got[:, side * rows_n : (side + 1) * rows_n].reshape(group_rows, piece)
            lower = t * span + side * piece
            product = jnp.dot(
                rows.astype(jnp.bfloat16),
                w_guard[lower : lower + piece, :],
                preferred_element_type=jnp.float32,
            )
            square = jnp.sum(rows * rows, axis=-1, keepdims=True)
            if t == 0 and side == 0:
                state["qkv"], state["square"] = product, square
            else:
                state["qkv"] = state["qkv"] + product
                state["square"] = state["square"] + square

    stages = (expert_chunk, chip_chunk, mid_chunk, z_chunk, stream_chunk, guard_chunk)
    for step in range(CHUNKS + len(stages) - 1):
        for late, stage in enumerate(stages):
            if 0 <= step - late < CHUNKS:
                stage(step - late)

    qkv = state["qkv"] * lax.rsqrt(state["square"] / width + EPSILON)
    head = keys.shape[1]
    heads = q_n // head
    window = keys.shape[0] // group_rows
    scale = 1.0 / math.sqrt(head)
    key_new = qkv[:, q_n : q_n + k_n].astype(jnp.bfloat16).astype(jnp.float32)
    value_new = qkv[:, q_n + k_n :].astype(jnp.bfloat16).astype(jnp.float32)
    lengths_n = as_column(lengths_ref[...].astype(jnp.float32)).astype(jnp.int32)
    span_keys = rows_n * window
    outs = []
    for a in range(groups):
        here = slice(a * rows_n, (a + 1) * rows_n)
        query = jnp.concatenate([qkv[here, h * head : (h + 1) * head] for h in range(heads)], axis=0)
        key_own = jnp.concatenate([key_new[here]] * heads, axis=0)
        value_own = jnp.concatenate([value_new[here]] * heads, axis=0)
        allowed_n = jnp.concatenate([lengths_n[here]] * heads, axis=0)
        own_score = jnp.sum(query * key_own, axis=-1, keepdims=True) * scale
        pieces, rest = [], query
        for _ in range(3):
            top = rest.astype(jnp.bfloat16).astype(jnp.float32)
            pieces.append(top)
            rest = rest - top
        product = lax.dot_general(
            jnp.concatenate(pieces, axis=0).astype(jnp.bfloat16),
            keys[a * span_keys : (a + 1) * span_keys, :],
            (((1,), (1,)), ((), ())),
            preferred_element_type=jnp.float32,
        )
        all_rows = heads * rows_n
        scores = (
            product[:all_rows] + product[all_rows : 2 * all_rows] + product[2 * all_rows :]
        ) * scale
        column = lax.broadcasted_iota(jnp.int32, scores.shape, 1)
        row = lax.broadcasted_iota(jnp.int32, (all_rows, 1), 0) % rows_n
        upper = (row + 1) * window
        allowed = (column >= upper - allowed_n) & (column < upper)
        masked = jnp.where(allowed, scores, -jnp.inf)
        highest = jnp.maximum(jnp.max(masked, axis=-1, keepdims=True), own_score)
        weights = jnp.exp(masked - highest)
        own_weight = jnp.exp(own_score - highest)
        denominator = jnp.sum(weights, axis=-1, keepdims=True) + own_weight
        top = weights.astype(jnp.bfloat16).astype(jnp.float32)
        product = jnp.dot(
            jnp.concatenate([top, weights - top], axis=0).astype(jnp.bfloat16),
            values[a * span_keys : (a + 1) * span_keys, :],
            preferred_element_type=jnp.float32,
        )
        attended = product[:all_rows] + product[all_rows:] + own_weight * value_own
        attended = attended / denominator
        outs.append(
            jnp.concatenate(
                [attended[h * rows_n : (h + 1) * rows_n] for h in range(heads)], axis=1
            )
        )
    guard_ref[...] = jnp.concatenate(outs, axis=0).astype(jnp.bfloat16)
    for copy in sends:
        copy.wait_send()


def fused_device(
    tokens,
    expert_ids,
    combine,
    w_gate,
    w_up,
    w_down,
    w_query,
    w_key,
    w_value,
    cache_keys,
    cache_values,
    lengths,
):
    rows_n, width = tokens.shape
    groups = lax.axis_size("gd")
    unit = w_gate.shape[2]
    group_rows, heads_kv, window, head = cache_keys.shape
    total_rows = CORES * CHIPS * groups * rows_n
    piece = width // CHUNKS // 2
    pack = 2 * rows_n
    guard_n = w_query.shape[1] + w_key.shape[1] + w_value.shape[1]
    bf16, f32 = jnp.bfloat16, jnp.float32
    dma = pltpu.SemaphoreType.DMA
    in_vmem = pl.BlockSpec(memory_space=pltpu.VMEM)
    in_hbm = pl.BlockSpec(memory_space=pltpu.HBM)
    return pl.pallas_call(
        functools.partial(fused_kernel, groups),
        out_shape=(
            jax.ShapeDtypeStruct((rows_n, width), bf16),
            jax.ShapeDtypeStruct((group_rows, w_query.shape[1]), bf16),
        ),
        in_specs=[in_hbm] * 12,
        out_specs=(in_vmem, in_vmem),
        scratch_shapes=[
            pltpu.VMEM((rows_n, width), bf16),
            pltpu.VMEM((expert_ids.shape[1], rows_n), jnp.int32),
            pltpu.VMEM((combine.shape[1], rows_n), f32),
            pltpu.VMEM((1, group_rows), jnp.int32),
            pltpu.VMEM((width, 2 * unit), bf16),
            pltpu.VMEM((unit, width), bf16),
            pltpu.VMEM((width, guard_n), bf16),
            pltpu.VMEM((group_rows * window, head), bf16),
            pltpu.VMEM((group_rows * window, head), bf16),
            pltpu.VMEM((CORES, CHIPS, groups, pack, width // 2 + 128), bf16),
            pltpu.VMEM((total_rows, width), bf16),
            pltpu.VMEM((total_rows, 128), f32),
            pltpu.VMEM((total_rows, 2 * unit), f32),
            pltpu.VMEM((total_rows, unit), bf16),
            pltpu.VMEM((CHUNKS, CORES, CHIPS, groups, pack, piece), bf16),
            pltpu.VMEM((CHUNKS, CHIPS, groups, pack, piece), bf16),
            pltpu.VMEM((CHUNKS, CHIPS, groups, pack, piece), bf16),
            pltpu.VMEM((CHUNKS, 3, groups, pack, piece), bf16),
            pltpu.VMEM((CHUNKS, groups, pack, piece), bf16),
            pltpu.VMEM((CHUNKS, groups, pack, piece), bf16),
            pltpu.VMEM((CHUNKS, groups, pack, piece), bf16),
            pltpu.VMEM((CHUNKS, groups, pack, piece), bf16),
            dma((12,)),
            dma((groups,)),
            dma((groups,)),
            dma((groups,)),
            dma((groups,)),
            dma((groups,)),
            dma((groups,)),
            dma((groups,)),
            dma((groups,)),
            dma((4, groups)),
            dma((4, groups)),
            dma((CHUNKS,)),
            dma((CHUNKS,)),
            dma((CHUNKS, 3, 2)),
            dma((CHUNKS, 3, 2)),
            dma((CHUNKS, groups)),
            dma((CHUNKS, groups)),
            dma((CHUNKS, groups)),
            dma((CHUNKS, groups)),
        ],
        compiler_params=pltpu.CompilerParams(
            collective_id=0, has_side_effects=True, vmem_limit_bytes=64000 * 1024
        ),
    )(
        tokens,
        expert_ids.T,
        combine.T,
        lengths.reshape(1, group_rows),
        w_gate,
        w_up,
        w_down,
        w_query,
        w_key,
        w_value,
        cache_keys.reshape(group_rows * heads_kv * window, head),
        cache_values.reshape(group_rows * heads_kv * window, head),
    )


def solution(mesh):
    fused = mesh.shape["ep"] == 8 and mesh.shape["gd"] == 4
    return jax.shard_map(
        fused_device if fused else per_device,
        mesh=mesh,
        in_specs=(
            P(("ep", "gd"), None),
            P(("ep", "gd"), None),
            P(("ep", "gd"), None),
            P("ep", None, "gd"),
            P("ep", None, "gd"),
            P("ep", "gd", None),
            P(None, "gd"),
            P(None, "gd"),
            P(None, "gd"),
            P("ep", "gd", None, None),
            P("ep", "gd", None, None),
            P("ep"),
        ),
        out_specs=(P(("ep", "gd"), None), P("ep", "gd")),
        check_vma=False,
    )
```

```python
import functools
import math

import jax
import jax.numpy as jnp
from jax import lax
from jax.experimental import pallas as pl
from jax.experimental.pallas import tpu as pltpu
from jax.sharding import PartitionSpec as P

EPSILON = 1e-06


def norm_rows(values):
    widened = values.astype(jnp.float32)
    return (
        widened * lax.rsqrt(jnp.mean(widened * widened, axis=-1, keepdims=True) + EPSILON)
    ).astype(jnp.bfloat16)


def slot_numbers(chosen, experts):
    blocks_n, rows_n, picks_n = chosen.shape
    flat_ids = chosen.reshape(blocks_n, rows_n * picks_n)
    onehot = (flat_ids[:, :, None] == jnp.arange(experts, dtype=jnp.int32)[None, None, :]).astype(
        jnp.int32
    )
    before = jnp.cumsum(onehot, axis=1) - onehot
    return jnp.sum(before * onehot, axis=-1).reshape(blocks_n, rows_n, picks_n)


def build_slots(row_blocks, targets, slots_n):
    wanted = jnp.any(
        targets[:, None, :, :] == jnp.arange(slots_n, dtype=jnp.int32)[None, :, None, None], axis=-1
    )
    selector = wanted.astype(jnp.bfloat16)
    return jnp.einsum(
        "bsr,brd->bsd", selector, row_blocks, preferred_element_type=jnp.float32
    ).astype(jnp.bfloat16)


def per_device(
    tokens,
    expert_ids,
    combine,
    w_gate,
    w_up,
    w_down,
    w_query,
    w_key,
    w_value,
    cache_keys,
    cache_values,
    lengths,
):
    rows_n, width = tokens.shape
    picks_n = expert_ids.shape[1]
    experts = lax.axis_size("ep")
    members = lax.axis_size("gd")
    capacity = max(2, 3 * rows_n * picks_n // (2 * experts))
    slots_n = experts * capacity
    normed = norm_rows(tokens)
    own_slot = slot_numbers(expert_ids[None], experts)[0]
    own_dest = expert_ids * capacity + own_slot
    group_normed, group_ids = (
        lax.all_gather(normed, "gd", axis=0, tiled=True),
        lax.all_gather(expert_ids, "gd", axis=0, tiled=True),
    )
    group_ids = group_ids.reshape(members, rows_n, picks_n)
    group_dest = group_ids * capacity + slot_numbers(group_ids, experts)
    outgoing = build_slots(group_normed.reshape(members, rows_n, width), group_dest, slots_n)
    outgoing = outgoing.reshape(members, experts, capacity, width)
    arrived = lax.all_to_all(outgoing, "ep", split_axis=1, concat_axis=1, tiled=True)
    slot_rows = arrived.reshape(-1, width)
    gate_val = jnp.dot(slot_rows, w_gate[0], preferred_element_type=jnp.float32)
    up_val = jnp.dot(slot_rows, w_up[0], preferred_element_type=jnp.float32)
    active = (jax.nn.silu(gate_val) * up_val).astype(jnp.bfloat16)
    partial_out = jnp.dot(active, w_down[0], preferred_element_type=jnp.float32).astype(
        jnp.bfloat16
    )
    summed = lax.psum_scatter(
        lax.optimization_barrier(partial_out).astype(jnp.float32).astype(jnp.bfloat16),
        "gd",
        scatter_dimension=0,
        tiled=True,
    ).astype(jnp.float32)
    returned = lax.all_to_all(
        summed.reshape(experts, capacity, width), "ep", split_axis=0, concat_axis=0, tiled=True
    )
    matches = own_dest[:, :, None] == jnp.arange(slots_n, dtype=jnp.int32)[None, None, :]
    weight_rows = jnp.sum(jnp.where(matches, combine[:, :, None], 0.0), axis=1)
    mixture = jnp.dot(
        weight_rows,
        returned.reshape(slots_n, width),
        precision=lax.Precision.HIGHEST,
        preferred_element_type=jnp.float32,
    )
    stream = (tokens.astype(jnp.float32) + mixture).astype(jnp.bfloat16)
    group_stream = lax.all_gather(stream, "gd", axis=0, tiled=True)
    guard_norm = norm_rows(group_stream)
    queries = jnp.dot(guard_norm, w_query, preferred_element_type=jnp.float32)
    key_new = jnp.dot(guard_norm, w_key, preferred_element_type=jnp.float32).astype(jnp.bfloat16)
    value_new = jnp.dot(guard_norm, w_value, preferred_element_type=jnp.float32).astype(
        jnp.bfloat16
    )
    group_total, heads_kv, window_len, head_size = cache_keys.shape
    heads_per = w_query.shape[1] // (heads_kv * head_size)
    queries = queries.reshape(group_total, heads_kv, heads_per, head_size)
    key_new = key_new.reshape(group_total, heads_kv, head_size)
    value_new = value_new.reshape(group_total, heads_kv, head_size)
    scale_factor = 1.0 / math.sqrt(head_size)
    scores = (
        jnp.einsum(
            "rhgd,rhjd->rhgj",
            queries,
            cache_keys.astype(jnp.float32),
            precision=lax.Precision.HIGHEST,
        )
        * scale_factor
    )
    own_score = (
        jnp.einsum(
            "rhgd,rhd->rhg", queries, key_new.astype(jnp.float32), precision=lax.Precision.HIGHEST
        )
        * scale_factor
    )
    positions = jnp.arange(window_len, dtype=jnp.int32)
    allowed = positions[None, None, None, :] >= (window_len - lengths)[:, None, None, None]
    masked = jnp.where(allowed, scores, -jnp.inf)
    highest = jnp.maximum(jnp.max(masked, axis=-1), own_score)
    weights = jnp.exp(masked - highest[..., None])
    own_weight = jnp.exp(own_score - highest)
    denominator = jnp.sum(weights, axis=-1) + own_weight
    probabilities = weights / denominator[..., None]
    own_prob = own_weight / denominator
    attended = jnp.einsum(
        "rhgj,rhjd->rhgd",
        probabilities,
        cache_values.astype(jnp.float32),
        precision=lax.Precision.HIGHEST,
    )
    attended = attended + own_prob[..., None] * value_new.astype(jnp.float32)[:, :, None, :]
    guard = attended.astype(jnp.bfloat16).reshape(group_total, heads_kv * heads_per * head_size)
    return (stream, guard)


CORES = 2
CHIPS = 4
CHUNKS = 4
MESH = pl.DeviceIdType.MESH


def as_column(line):
    size = line.shape[1]
    across = lax.broadcasted_iota(jnp.int32, (size, size), 1)
    down = lax.broadcasted_iota(jnp.int32, (size, size), 0)
    return jnp.sum(jnp.where(across == down, line, 0.0), axis=1, keepdims=True)


def fused_kernel(
    groups,
    tokens_hbm,
    ids_hbm,
    combine_hbm,
    lengths_hbm,
    gate_hbm,
    up_hbm,
    down_hbm,
    query_hbm,
    key_hbm,
    value_hbm,
    cache_k_hbm,
    cache_v_hbm,
    stream_ref,
    guard_ref,
    tokens_ref,
    ids_ref,
    combine_ref,
    lengths_ref,
    w_in,
    w_out,
    w_guard,
    keys,
    values,
    rows_in,
    rows_all,
    weight_all,
    hidden,
    active,
    part,
    got_core,
    sum_core,
    got_chip,
    sum_mid,
    sum_chip,
    got_z,
    stream_all,
    load_sem,
    z_send,
    z_recv,
    x_send,
    x_recv,
    y_send,
    y_recv,
    d_send,
    d_recv,
    c_send,
    c_recv,
    r1_send,
    r1_recv,
    r2_send,
    r2_recv,
    r3_send,
    r3_recv,
    s_send,
    s_recv,
):
    rows_n, width = tokens_hbm.shape
    half = width // 2
    unit = gate_hbm.shape[2]
    me_e = lax.axis_index("ep")
    g = lax.axis_index("gd")
    core = me_e % CORES
    chip = me_e // CORES
    x, y = chip % 2, chip // 2
    x_chip = y * 2 + (1 - x)
    y_chip = (1 - y) * 2 + x
    d_chip = (1 - y) * 2 + (1 - x)
    sibling = (chip * CORES + (1 - core), g)
    x_dev = (x_chip * CORES + core, g)
    y_dev = (y_chip * CORES + core, g)
    d_dev = (d_chip * CORES + core, g)

    def z_of(step):
        return (g + step) % groups

    loads = []

    def load(src, dst):
        copy = pltpu.make_async_copy(src, dst, load_sem.at[len(loads)])
        copy.start()
        loads.append(copy)

    barrier = pltpu.get_barrier_semaphore()
    peers = [sibling, x_dev, y_dev, d_dev] + [(me_e, z_of(k)) for k in range(1, groups)]
    for peer in peers:
        pl.semaphore_signal(barrier, inc=1, device_id=peer, device_id_type=MESH)

    load(tokens_hbm, tokens_ref)
    load(ids_hbm, ids_ref)
    load(combine_hbm, combine_ref)
    load(lengths_hbm, lengths_ref)
    load(gate_hbm.at[0], w_in.at[:, 0:unit])
    load(up_hbm.at[0], w_in.at[:, unit : 2 * unit])
    load(down_hbm.at[0], w_out)
    q_n, k_n = query_hbm.shape[1], key_hbm.shape[1]
    load(query_hbm, w_guard.at[:, 0:q_n])
    load(key_hbm, w_guard.at[:, q_n : q_n + k_n])
    load(value_hbm, w_guard.at[:, q_n + k_n : q_n + 2 * k_n])
    load(cache_k_hbm, keys)
    load(cache_v_hbm, values)

    for i in range(3):
        loads[i].wait()
    wide = tokens_ref[...].astype(jnp.float32)
    normed = wide * lax.rsqrt(jnp.mean(wide * wide, axis=-1, keepdims=True) + EPSILON)
    lanes = lax.broadcasted_iota(jnp.int32, (rows_n, 128), 1)
    table = jnp.zeros((rows_n, 128), jnp.float32)
    for k in range(ids_ref.shape[0]):
        named = as_column(ids_ref[k : k + 1, :].astype(jnp.float32)).astype(jnp.int32)
        share_of = as_column(combine_ref[k : k + 1, :])
        table = table + jnp.where(lanes == named, share_of, 0.0)
    table_top = table.astype(jnp.bfloat16).astype(jnp.float32)
    packed = jnp.concatenate([normed[:, :half], normed[:, half:]], axis=0)
    rows_in[core, chip, g, :, 0:half] = packed.astype(jnp.bfloat16)
    rows_in[core, chip, g, :, half : half + 128] = jnp.concatenate(
        [table_top, table - table_top], axis=0
    ).astype(jnp.bfloat16)

    pl.semaphore_wait(barrier, len(peers))

    sends = []

    def send(src, dst, send_sem, recv_sem, device):
        copy = pltpu.make_async_remote_copy(
            src_ref=src,
            dst_ref=dst,
            send_sem=send_sem,
            recv_sem=recv_sem,
            device_id=device,
            device_id_type=MESH,
        )
        copy.start()
        sends.append(copy)
        return copy

    def row_send(chip_of, step, send_sem, recv_sem, device):
        block = rows_in.at[core, chip_of, (g + groups - step) % groups]
        return send(block, block, send_sem, recv_sem, device)

    z_copies, x_copies, y_copies, d_copies, c_copies = {}, {}, {}, {}, {}

    def share(kind, chip_of, step):
        c_copies[kind, step] = row_send(
            chip_of, step, c_send.at[kind, step], c_recv.at[kind, step], sibling
        )

    def spread(step):
        x_copies[step] = row_send(chip, step, x_send.at[step], x_recv.at[step], x_dev)
        y_copies[step] = row_send(chip, step, y_send.at[step], y_recv.at[step], y_dev)
        if step >= groups - 2:
            d_copies[step] = row_send(chip, step, d_send.at[step], d_recv.at[step], d_dev)
        share(0, chip, step)

    def forward(step):
        x_copies[step].wait_recv()
        if step % 2 == 1 and step < groups - 2:
            d_copies[step] = row_send(x_chip, step, d_send.at[step], d_recv.at[step], y_dev)
        share(1, x_chip, step)
        y_copies[step].wait_recv()
        if step % 2 == 0 and step < groups - 2:
            d_copies[step] = row_send(y_chip, step, d_send.at[step], d_recv.at[step], x_dev)
        share(2, y_chip, step)

    for k in range(1, groups):
        z_copies[k] = row_send(chip, 0, z_send.at[k], z_recv.at[k], (me_e, z_of(k)))
    spread(0)
    for k in range(1, groups):
        z_copies[k].wait_recv()
        spread(k)
        forward(k - 1)
    forward(groups - 1)
    group_rows = groups * rows_n
    core_rows = CHIPS * group_rows
    tile = 256

    def unpack(c, h):
        start = pl.multiple_of((c * CHIPS + h) * group_rows, group_rows)
        for side in range(2):
            got = rows_in[c, h, :, :, 0:half].astype(jnp.float32)
            got = got[:, side * rows_n : (side + 1) * rows_n].reshape(group_rows, half)
            rows_all[pl.ds(start, group_rows), side * half : (side + 1) * half] = got.astype(
                jnp.bfloat16
            )
        extra = rows_in[c, h, :, :, half : half + 128].astype(jnp.float32)
        weight_all[pl.ds(start, group_rows), :] = (extra[:, :rows_n] + extra[:, rows_n:]).reshape(
            group_rows, 128
        )

    def first_layer(c):
        some = pl.ds(pl.multiple_of(c * core_rows, core_rows), core_rows)

        def first(n, carry):
            cols = pl.ds(pl.multiple_of(n * tile, tile), tile)
            hidden[some, cols] = jnp.dot(
                rows_all[some, :], w_in[:, cols], preferred_element_type=jnp.float32
            )
            return carry

        lax.fori_loop(0, 2 * unit // tile, first, 0)
        table_all = weight_all[some, :]
        picked = lax.broadcasted_iota(jnp.int32, table_all.shape, 1) == me_e
        row_weight = jnp.sum(jnp.where(picked, table_all, 0.0), axis=-1, keepdims=True)
        gate_val = hidden[some, 0:unit]
        active[some, :] = (
            gate_val / (1.0 + jnp.exp(-gate_val)) * hidden[some, unit : 2 * unit] * row_weight
        ).astype(jnp.bfloat16)

    unpack(core, chip)
    unpack(core, x_chip)
    unpack(core, y_chip)
    for k in range(groups):
        d_copies[k].wait_recv()
        share(3, d_chip, k)
    unpack(core, d_chip)
    loads[4].wait()
    loads[5].wait()
    first_layer(core)
    for kind, chip_of in enumerate((chip, x_chip, y_chip, d_chip)):
        for k in range(groups):
            c_copies[kind, k].wait_recv()
        unpack(1 - core, chip_of)
    first_layer(1 - core)
    loads[6].wait()

    span = width // CHUNKS
    piece = span // 2
    paired = groups // 2
    r1, r2, r3, s_copies = {}, {}, {}, {}

    def expert_half(t, c):
        some = pl.ds(pl.multiple_of(c * core_rows, core_rows), core_rows)
        outs = []
        for side in range(2):
            lower = t * span + side * piece
            outs.append(
                jnp.dot(
                    active[some, :],
                    w_out[:, lower : lower + piece],
                    preferred_element_type=jnp.float32,
                ).reshape(CHIPS, groups, rows_n, piece)
            )
        part[t, c] = jnp.concatenate(outs, axis=2).astype(jnp.bfloat16)

    def expert_chunk(t):
        expert_half(t, 1 - core)
        r1[t] = send(
            part.at[t, 1 - core], got_core.at[t], r1_send.at[t], r1_recv.at[t], sibling
        )
        expert_half(t, core)

    def chip_chunk(t):
        r1[t].wait_recv()
        total = part[t, core].astype(jnp.float32) + got_core[t].astype(jnp.float32)
        sum_core[t] = total.astype(jnp.bfloat16)
        for kind, chips_to in ((1, (d_chip, d_chip)), (0, (x_chip, y_chip))):
            for side in range(2):
                some = pl.ds(side * paired, paired)
                r2[t, kind, side] = send(
                    sum_core.at[t, chips_to[side], some],
                    got_chip.at[t, kind, some],
                    r2_send.at[t, kind, side],
                    r2_recv.at[t, kind, side],
                    (x_dev, y_dev)[side],
                )

    def mid_chunk(t):
        for side in range(2):
            some = pl.ds(side * paired, paired)
            r2[t, 1, side].wait_recv()
            total = sum_core[t, (y_chip, x_chip)[side], some].astype(jnp.float32)
            total = total + got_chip[t, 1, some].astype(jnp.float32)
            sum_mid[t, some] = total.astype(jnp.bfloat16)
            r2[t, 2, side] = send(
                sum_mid.at[t, some],
                got_chip.at[t, 2, some],
                r2_send.at[t, 2, side],
                r2_recv.at[t, 2, side],
                (y_dev, x_dev)[side],
            )

    def z_chunk(t):
        total = sum_core[t, chip].astype(jnp.float32)
        for kind in (0, 2):
            for side in range(2):
                r2[t, kind, side].wait_recv()
            total = total + got_chip[t, kind].astype(jnp.float32)
        sum_chip[t] = total.astype(jnp.bfloat16)
        for k in range(1, groups):
            r3[t, k] = send(
                sum_chip.at[t, z_of(k)],
                got_z.at[t, k],
                r3_send.at[t, k],
                r3_recv.at[t, k],
                (me_e, z_of(k)),
            )

    def stream_chunk(t):
        total = sum_chip[t, g].astype(jnp.float32)
        for k in range(1, groups):
            r3[t, k].wait_recv()
            total = total + got_z[t, k].astype(jnp.float32)
        mixture = jnp.concatenate([total[:rows_n], total[rows_n:]], axis=1)
        cols = slice(t * span, (t + 1) * span)
        stream = tokens_ref[:, cols].astype(jnp.float32) + mixture
        stream_ref[:, cols] = stream.astype(jnp.bfloat16)
        stream_all[t, g] = jnp.concatenate(
            [stream[:, :piece], stream[:, piece:]], axis=0
        ).astype(jnp.bfloat16)
        for k in range(1, groups):
            block = stream_all.at[t, g]
            s_copies[t, k] = send(
                block, block, s_send.at[t, k], s_recv.at[t, k], (me_e, z_of(k))
            )

    state = {}

    def guard_chunk(t):
        for k in range(1, groups):
            s_copies[t, k].wait_recv()
        got = stream_all[t].astype(jnp.float32)
        if t == 0:
            for i in (3, 7, 8, 9, 10, 11):
                loads[i].wait()
        for side in range(2):
            rows = got[:, side * rows_n : (side + 1) * rows_n].reshape(group_rows, piece)
            lower = t * span + side * piece
            product = jnp.dot(
                rows.astype(jnp.bfloat16),
                w_guard[lower : lower + piece, :],
                preferred_element_type=jnp.float32,
            )
            square = jnp.sum(rows * rows, axis=-1, keepdims=True)
            if t == 0 and side == 0:
                state["qkv"], state["square"] = product, square
            else:
                state["qkv"] = state["qkv"] + product
                state["square"] = state["square"] + square

    stages = (expert_chunk, chip_chunk, mid_chunk, z_chunk, stream_chunk, guard_chunk)
    for step in range(CHUNKS + len(stages) - 1):
        for late, stage in enumerate(stages):
            if 0 <= step - late < CHUNKS:
                stage(step - late)

    qkv = state["qkv"] * lax.rsqrt(state["square"] / width + EPSILON)
    head = keys.shape[1]
    heads = q_n // head
    window = keys.shape[0] // group_rows
    scale = 1.0 / math.sqrt(head)
    key_new = qkv[:, q_n : q_n + k_n].astype(jnp.bfloat16).astype(jnp.float32)
    value_new = qkv[:, q_n + k_n :].astype(jnp.bfloat16).astype(jnp.float32)
    lengths_n = as_column(lengths_ref[...].astype(jnp.float32)).astype(jnp.int32)
    span_keys = rows_n * window
    outs = []
    for a in range(groups):
        here = slice(a * rows_n, (a + 1) * rows_n)
        query = jnp.concatenate([qkv[here, h * head : (h + 1) * head] for h in range(heads)], axis=0)
        key_own = jnp.concatenate([key_new[here]] * heads, axis=0)
        value_own = jnp.concatenate([value_new[here]] * heads, axis=0)
        allowed_n = jnp.concatenate([lengths_n[here]] * heads, axis=0)
        own_score = jnp.sum(query * key_own, axis=-1, keepdims=True) * scale
        pieces, rest = [], query
        for _ in range(3):
            top = rest.astype(jnp.bfloat16).astype(jnp.float32)
            pieces.append(top)
            rest = rest - top
        product = lax.dot_general(
            jnp.concatenate(pieces, axis=0).astype(jnp.bfloat16),
            keys[a * span_keys : (a + 1) * span_keys, :],
            (((1,), (1,)), ((), ())),
            preferred_element_type=jnp.float32,
        )
        all_rows = heads * rows_n
        scores = (
            product[:all_rows] + product[all_rows : 2 * all_rows] + product[2 * all_rows :]
        ) * scale
        column = lax.broadcasted_iota(jnp.int32, scores.shape, 1)
        row = lax.broadcasted_iota(jnp.int32, (all_rows, 1), 0) % rows_n
        upper = (row + 1) * window
        allowed = (column >= upper - allowed_n) & (column < upper)
        masked = jnp.where(allowed, scores, -jnp.inf)
        highest = jnp.maximum(jnp.max(masked, axis=-1, keepdims=True), own_score)
        weights = jnp.exp(masked - highest)
        own_weight = jnp.exp(own_score - highest)
        denominator = jnp.sum(weights, axis=-1, keepdims=True) + own_weight
        top = weights.astype(jnp.bfloat16).astype(jnp.float32)
        product = jnp.dot(
            jnp.concatenate([top, weights - top], axis=0).astype(jnp.bfloat16),
            values[a * span_keys : (a + 1) * span_keys, :],
            preferred_element_type=jnp.float32,
        )
        attended = product[:all_rows] + product[all_rows:] + own_weight * value_own
        attended = attended / denominator
        outs.append(
            jnp.concatenate(
                [attended[h * rows_n : (h + 1) * rows_n] for h in range(heads)], axis=1
            )
        )
    guard_ref[...] = jnp.concatenate(outs, axis=0).astype(jnp.bfloat16)
    for copy in sends:
        copy.wait_send()


def fused_device(
    tokens,
    expert_ids,
    combine,
    w_gate,
    w_up,
    w_down,
    w_query,
    w_key,
    w_value,
    cache_keys,
    cache_values,
    lengths,
):
    rows_n, width = tokens.shape
    groups = lax.axis_size("gd")
    unit = w_gate.shape[2]
    group_rows, heads_kv, window, head = cache_keys.shape
    total_rows = CORES * CHIPS * groups * rows_n
    piece = width // CHUNKS // 2
    pack = 2 * rows_n
    guard_n = w_query.shape[1] + w_key.shape[1] + w_value.shape[1]
    bf16, f32 = jnp.bfloat16, jnp.float32
    dma = pltpu.SemaphoreType.DMA
    in_vmem = pl.BlockSpec(memory_space=pltpu.VMEM)
    in_hbm = pl.BlockSpec(memory_space=pltpu.HBM)
    return pl.pallas_call(
        functools.partial(fused_kernel, groups),
        out_shape=(
            jax.ShapeDtypeStruct((rows_n, width), bf16),
            jax.ShapeDtypeStruct((group_rows, w_query.shape[1]), bf16),
        ),
        in_specs=[in_hbm] * 12,
        out_specs=(in_vmem, in_vmem),
        scratch_shapes=[
            pltpu.VMEM((rows_n, width), bf16),
            pltpu.VMEM((expert_ids.shape[1], rows_n), jnp.int32),
            pltpu.VMEM((combine.shape[1], rows_n), f32),
            pltpu.VMEM((1, group_rows), jnp.int32),
            pltpu.VMEM((width, 2 * unit), bf16),
            pltpu.VMEM((unit, width), bf16),
            pltpu.VMEM((width, guard_n), bf16),
            pltpu.VMEM((group_rows * window, head), bf16),
            pltpu.VMEM((group_rows * window, head), bf16),
            pltpu.VMEM((CORES, CHIPS, groups, pack, width // 2 + 128), bf16),
            pltpu.VMEM((total_rows, width), bf16),
            pltpu.VMEM((total_rows, 128), f32),
            pltpu.VMEM((total_rows, 2 * unit), f32),
            pltpu.VMEM((total_rows, unit), bf16),
            pltpu.VMEM((CHUNKS, CORES, CHIPS, groups, pack, piece), bf16),
            pltpu.VMEM((CHUNKS, CHIPS, groups, pack, piece), bf16),
            pltpu.VMEM((CHUNKS, CHIPS, groups, pack, piece), bf16),
            pltpu.VMEM((CHUNKS, 3, groups, pack, piece), bf16),
            pltpu.VMEM((CHUNKS, groups, pack, piece), bf16),
            pltpu.VMEM((CHUNKS, groups, pack, piece), bf16),
            pltpu.VMEM((CHUNKS, groups, pack, piece), bf16),
            pltpu.VMEM((CHUNKS, groups, pack, piece), bf16),
            dma((12,)),
            dma((groups,)),
            dma((groups,)),
            dma((groups,)),
            dma((groups,)),
            dma((groups,)),
            dma((groups,)),
            dma((groups,)),
            dma((groups,)),
            dma((4, groups)),
            dma((4, groups)),
            dma((CHUNKS,)),
            dma((CHUNKS,)),
            dma((CHUNKS, 3, 2)),
            dma((CHUNKS, 3, 2)),
            dma((CHUNKS, groups)),
            dma((CHUNKS, groups)),
            dma((CHUNKS, groups)),
            dma((CHUNKS, groups)),
        ],
        compiler_params=pltpu.CompilerParams(
            collective_id=0, has_side_effects=True, vmem_limit_bytes=64000 * 1024
        ),
    )(
        tokens,
        expert_ids.T,
        combine.T,
        lengths.reshape(1, group_rows),
        w_gate,
        w_up,
        w_down,
        w_query,
        w_key,
        w_value,
        cache_keys.reshape(group_rows * heads_kv * window, head),
        cache_values.reshape(group_rows * heads_kv * window, head),
    )


def solution(mesh):
    fused = mesh.shape["ep"] == 8 and mesh.shape["gd"] == 4
    return jax.shard_map(
        fused_device if fused else per_device,
        mesh=mesh,
        in_specs=(
            P(("ep", "gd"), None),
            P(("ep", "gd"), None),
            P(("ep", "gd"), None),
            P("ep", None, "gd"),
            P("ep", None, "gd"),
            P("ep", "gd", None),
            P(None, "gd"),
            P(None, "gd"),
            P(None, "gd"),
            P("ep", "gd", None, None),
            P("ep", "gd", None, None),
            P("ep"),
        ),
        out_specs=(P(("ep", "gd"), None), P("ep", "gd")),
        check_vma=False,
    )
```
